256 devices in a mesh: outer: 16 (over y_hi, x, core), inner: 16 (over z, y_lo).
Axes of the slice: x: 4, y: 4 (y_hi: 2, y_lo: 2; y = y_hi * 2 + y_lo), z: 8, core: 2. Of those that a mesh axis runs over, the one named last changes fastest.
Arguments:
- queries: bfloat16 [32768, 1024], P(('outer', 'inner')), may hold values from -4.5 to 4.5
- key_vectors: bfloat16 [32768, 128], P(('outer', 'inner')), may hold values from -4.5 to 4.5
- value_vectors: bfloat16 [32768, 128], P(('outer', 'inner')), may hold values from -4 to 4
- grad_output: bfloat16 [32768, 1024], P(('outer', 'inner')), may hold values from -4 to 4
- positions: int32 [32768], P(('outer', 'inner')), may hold values from 0 to 32767, as said below
Outputs:
- attended: bfloat16 [32768, 1024], P(('outer', 'inner'))
- grad_queries: bfloat16 [32768, 1024], P(('outer', 'inner'))
- grad_keys: bfloat16 [32768, 128], P(('outer', 'inner'))
- grad_values: bfloat16 [32768, 128], P(('outer', 'inner'))
The draws below stay inside these ranges and needn't reach their ends.
Inputs may be any that keep to these rules, and one draw needn't show every extreme that they name: Each run of 2048 rows holds the positions of one segment, 2048 times the segment's number plus 0 to 2047, each once. The 128 rows of one device hold two blocks of 64 ascending consecutive positions: block b of its segment first, then block 31 - b, where b runs over a permutation of 0 to 15 drawn anew for each segment.
All inputs are finite; a program needn't handle non-finite values.
Results may differ from the reference program's by a relative error of at most 0.03.
Values may be sent and summed in bfloat16 or wider, within the bound.
No kernel may reach another device: no remote copies, remote signals or barrier semaphores. Data moves between devices by JAX's collectives and lax.ppermute only.
A program may use at most 64 MiB of HBM per device.

```python
import jax
import jax.numpy as jnp
from jax import lax

HEADS = 8
HEAD_DIM = 128
TOK_DEV = 128
GROUP = 16
SEGMENTS = 16
SPAN = 2048
LENGTH = 32768


def draw_key_vectors(key, part):
    key = jax.random.fold_in(key, 7)
    rough = jnp.clip(jax.random.normal(key, (LENGTH, HEAD_DIM), jnp.float32), -4.5, 4.5)
    return rough.astype(jnp.bfloat16)


def draw_queries(key, part):
    key = jax.random.fold_in(key, 9)
    rough = jnp.clip(jax.random.normal(key, (LENGTH, HEADS * HEAD_DIM), jnp.float32), -4.5, 4.5)
    return rough.astype(jnp.bfloat16)


def draw_positions(key, part):
    key = jax.random.fold_in(key, 11)
    block_len = TOK_DEV // 2
    seg_keys = jax.random.split(key, SEGMENTS)
    order = jax.vmap(lambda seg_key: jax.random.permutation(seg_key, GROUP))(seg_keys)
    local = jnp.arange(TOK_DEV)
    in_first = local < block_len
    offsets = local % block_len
    block_ids = jnp.where(in_first[None, None, :], order[:, :, None], 2 * GROUP - 1 - order[:, :, None])
    result = jnp.arange(SEGMENTS)[:, None, None] * SPAN + block_ids * block_len + offsets[None, None, :]
    return result.reshape(LENGTH).astype(jnp.int32)


def block_scale(key, extent, pieces, smallest, top_value):
    def one(axis_at, parts):
        heights = jax.random.uniform(jax.random.fold_in(jax.random.fold_in(key, 6), axis_at), (parts,), jnp.float32, smallest / len(pieces), top_value / len(pieces))
        return jnp.repeat(jnp.exp(heights), extent[axis_at] // parts).reshape((-1,) + (1,) * (len(extent) - axis_at - 1))

    gain = one(*pieces[0])
    for cut in pieces[1:]:
        gain = gain * one(*cut)
    return gain


def gaussian(stream_key, extent, deviation, bound, pieces=(), kind=jnp.bfloat16):
    entries = deviation * jax.random.normal(stream_key, extent, jnp.float32)
    if pieces:
        entries = entries * block_scale(stream_key, extent, pieces, -0.22, 0.18)
    return jnp.clip(entries, -bound, bound).astype(kind)


def setup_inputs(seed: int = 0) -> dict:
    arg_keys = jax.random.split(jax.random.key(seed), 6)
    queries = draw_queries(jax.random.fold_in(arg_keys[5], 71), 0)
    key_vectors = draw_key_vectors(jax.random.fold_in(arg_keys[5], 71), 0)
    value_vectors = gaussian(arg_keys[2], (LENGTH, HEAD_DIM), 1.0, 4.0, ((0, 256),))
    grad_output = gaussian(arg_keys[3], (LENGTH, HEADS * HEAD_DIM), 1.0, 4.0, ((0, 256),))
    positions = draw_positions(jax.random.fold_in(arg_keys[5], 71), 0)
    return {"queries": queries, "key_vectors": key_vectors, "value_vectors": value_vectors, "grad_output": grad_output, "positions": positions}


masked_score = -1.0e30


def head_terms(query_head, grad_head, both_keys, both_values, allowed, score_scale):
    scores = jnp.dot(query_head, both_keys.T, preferred_element_type=jnp.float32) * score_scale
    scores = jnp.where(allowed, scores, masked_score)
    row_max = jnp.max(scores, axis=-1, keepdims=True)
    exp_scores = jnp.exp(scores - row_max)
    probs = exp_scores / jnp.sum(exp_scores, axis=-1, keepdims=True)
    weights = probs.astype(jnp.bfloat16)
    attn_out = jnp.dot(weights, both_values, preferred_element_type=jnp.float32).astype(jnp.bfloat16)
    row_delta = jnp.sum(grad_head.astype(jnp.float32) * attn_out.astype(jnp.float32), axis=-1, keepdims=True)
    prob_grad = jnp.dot(grad_head, both_values.T, preferred_element_type=jnp.float32)
    score_grad = (probs * (prob_grad - row_delta)).astype(jnp.bfloat16)
    query_grad = (jnp.dot(score_grad, both_keys, preferred_element_type=jnp.float32) * score_scale).astype(jnp.bfloat16)
    key_grad = jnp.dot(score_grad.T, query_head, preferred_element_type=jnp.float32) * score_scale
    value_grad = jnp.dot(weights.T, grad_head, preferred_element_type=jnp.float32)
    return attn_out, query_grad, key_grad, value_grad


def reference(queries, key_vectors, value_vectors, grad_output, positions):
    score_scale = float(HEAD_DIM) ** -0.5
    query_seg = queries.reshape(SEGMENTS, SPAN, HEADS, HEAD_DIM).transpose(0, 2, 1, 3)
    grad_seg = grad_output.reshape(SEGMENTS, SPAN, HEADS, HEAD_DIM).transpose(0, 2, 1, 3)
    key_seg = key_vectors.reshape(SEGMENTS, SPAN, HEAD_DIM)
    value_seg = value_vectors.reshape(SEGMENTS, SPAN, HEAD_DIM)
    zero_block = jnp.zeros((1, SPAN, HEAD_DIM), key_vectors.dtype)
    prev_keys = jnp.concatenate([zero_block, key_seg[:-1]], axis=0)
    prev_values = jnp.concatenate([zero_block, value_seg[:-1]], axis=0)
    pos_seg = positions.reshape(SEGMENTS, SPAN)
    has_prev = jnp.arange(SEGMENTS) > 0

    def segment_terms(items):
        query_heads, grad_heads, own_keys, own_values, prev_key, prev_value, seg_pos, prev_flag = items
        both_keys = jnp.concatenate([prev_key, own_keys], axis=0)
        both_values = jnp.concatenate([prev_value, own_values], axis=0)
        allowed = jnp.concatenate([jnp.broadcast_to(prev_flag, (SPAN, SPAN)),
                                   seg_pos[None, :] <= seg_pos[:, None]], axis=1)

        def per_head(head_items):
            return head_terms(head_items[0], head_items[1], both_keys, both_values, allowed, score_scale)

        attn_out, query_grad, key_grad, value_grad = lax.map(per_head, (query_heads, grad_heads))
        return attn_out, query_grad, jnp.sum(key_grad, axis=0), jnp.sum(value_grad, axis=0)

    attn_out, query_grad, key_total, value_total = lax.map(
        segment_terms, (query_seg, grad_seg, key_seg, value_seg, prev_keys, prev_values, pos_seg, has_prev))
    zero_terms = jnp.zeros((1, SPAN, HEAD_DIM), jnp.float32)
    key_back = jnp.concatenate([key_total[1:, :SPAN], zero_terms], axis=0)
    value_back = jnp.concatenate([value_total[1:, :SPAN], zero_terms], axis=0)
    grad_keys = (key_total[:, SPAN:] + key_back).reshape(LENGTH, HEAD_DIM).astype(jnp.bfloat16)
    grad_values = (value_total[:, SPAN:] + value_back).reshape(LENGTH, HEAD_DIM).astype(jnp.bfloat16)
    attended = attn_out.transpose(0, 2, 1, 3).reshape(LENGTH, HEADS * HEAD_DIM)
    grad_queries = query_grad.transpose(0, 2, 1, 3).reshape(LENGTH, HEADS * HEAD_DIM)
    return attended, grad_queries, grad_keys, grad_values
```

```python
import jax
import jax.numpy as jnp
from jax import lax
from jax.sharding import PartitionSpec as P

masked_score = -1e30


def from_behind(block, axis, distance):
    devices = range(lax.axis_size(axis))
    route = [(i - distance, i) for i in devices if i - distance in devices]
    return lax.ppermute(block, axis, route)


def gather_direct(block, axis):
    count = lax.axis_size(axis)
    copies = jnp.broadcast_to(block[None], (count,) + block.shape)
    gathered = lax.all_to_all(copies, axis, 0, 0, tiled=True)
    return gathered.reshape((count * block.shape[0],) + block.shape[1:])


def sum_direct(terms, axis):
    count = lax.axis_size(axis)
    parts = terms.reshape((count, terms.shape[0] // count) + terms.shape[1:])
    parts = lax.all_to_all(parts, axis, 0, 0, tiled=True)
    return jnp.sum(parts.astype(jnp.float32), axis=0)


def block_scores(query_block, key_block, score_scale):
    return (
        jnp.einsum("thd,kd->thk", query_block, key_block, preferred_element_type=jnp.float32)
        * score_scale
    )


def body(queries, key_vectors, value_vectors, grad_output, positions):
    tok_rows, full_width = queries.shape
    head_dim = key_vectors.shape[1]
    head_count = full_width // head_dim
    score_scale = float(head_dim) ** (-0.5)
    key_value = jnp.concatenate([key_vectors, value_vectors], axis=1)
    group_kv, group_positions = (
        gather_direct(key_value, "inner"),
        gather_direct(positions, "inner"),
    )
    prev_kv = from_behind(group_kv, "outer", 1)
    own_keys = group_kv[:, :head_dim]
    own_values = group_kv[:, head_dim:]
    prev_keys = prev_kv[:, :head_dim]
    prev_values = prev_kv[:, head_dim:]
    has_prev = lax.axis_index("outer") > 0
    own_mask = group_positions[None, :] <= positions[:, None]
    head_block = head_count
    while head_block * tok_rows > 512 and head_block % 2 == 0:
        head_block = head_block // 2
    span_rows = group_kv.shape[0]
    own_terms = jnp.zeros((span_rows, 2 * head_dim), jnp.float32)
    prev_terms = jnp.zeros((span_rows, 2 * head_dim), jnp.float32)
    attn_parts = []
    query_parts = []
    for head_start in range(0, head_count, head_block):
        col_start = head_start * head_dim
        col_stop = (head_start + head_block) * head_dim
        query_block = queries[:, col_start:col_stop].reshape(tok_rows, head_block, head_dim)
        grad_block = grad_output[:, col_start:col_stop].reshape(tok_rows, head_block, head_dim)
        own_scores = jnp.where(
            own_mask[:, None, :], block_scores(query_block, own_keys, score_scale), masked_score
        )
        prev_scores = jnp.where(
            has_prev, block_scores(query_block, prev_keys, score_scale), masked_score
        )
        row_max = jnp.maximum(
            jnp.max(own_scores, axis=-1, keepdims=True),
            jnp.max(prev_scores, axis=-1, keepdims=True),
        )
        own_exp = jnp.exp(own_scores - row_max)
        prev_exp = jnp.exp(prev_scores - row_max)
        row_total = jnp.sum(own_exp, axis=-1, keepdims=True) + jnp.sum(
            prev_exp, axis=-1, keepdims=True
        )
        own_probs = own_exp / row_total
        prev_probs = prev_exp / row_total
        own_weights = own_probs.astype(jnp.bfloat16)
        prev_weights = prev_probs.astype(jnp.bfloat16)
        attn_sum = jnp.einsum(
            "thk,kd->thd", own_weights, own_values, preferred_element_type=jnp.float32
        )
        attn_sum = attn_sum + jnp.einsum(
            "thk,kd->thd", prev_weights, prev_values, preferred_element_type=jnp.float32
        )
        attn_out = attn_sum.astype(jnp.bfloat16)
        row_delta = jnp.sum(
            grad_block.astype(jnp.float32) * attn_out.astype(jnp.float32), axis=-1, keepdims=True
        )
        own_pgrad = jnp.einsum(
            "thd,kd->thk", grad_block, own_values, preferred_element_type=jnp.float32
        )
        prev_pgrad = jnp.einsum(
            "thd,kd->thk", grad_block, prev_values, preferred_element_type=jnp.float32
        )
        own_dscore = (own_probs * (own_pgrad - row_delta)).astype(jnp.bfloat16)
        prev_dscore = (prev_probs * (prev_pgrad - row_delta)).astype(jnp.bfloat16)
        query_grad = jnp.einsum(
            "thk,kd->thd", own_dscore, own_keys, preferred_element_type=jnp.float32
        )
        query_grad = query_grad + jnp.einsum(
            "thk,kd->thd", prev_dscore, prev_keys, preferred_element_type=jnp.float32
        )
        query_grad = (query_grad * score_scale).astype(jnp.bfloat16)
        own_terms = own_terms + jnp.concatenate(
            [
                jnp.einsum(
                    "thk,thd->kd", own_dscore, query_block, preferred_element_type=jnp.float32
                )
                * score_scale,
                jnp.einsum(
                    "thk,thd->kd", own_weights, grad_block, preferred_element_type=jnp.float32
                ),
            ],
            axis=1,
        )
        prev_terms = prev_terms + jnp.concatenate(
            [
                jnp.einsum(
                    "thk,thd->kd", prev_dscore, query_block, preferred_element_type=jnp.float32
                )
                * score_scale,
                jnp.einsum(
                    "thk,thd->kd", prev_weights, grad_block, preferred_element_type=jnp.float32
                ),
            ],
            axis=1,
        )
        attn_parts.append(attn_out.reshape(tok_rows, head_block * head_dim))
        query_parts.append(query_grad.reshape(tok_rows, head_block * head_dim))
    attended = jnp.concatenate(attn_parts, axis=1)
    grad_queries = jnp.concatenate(query_parts, axis=1)
    returned = from_behind(prev_terms.astype(jnp.bfloat16), "outer", -1).astype(prev_terms.dtype)
    key_grads = sum_direct((own_terms + returned).astype(jnp.bfloat16), "inner")
    grad_keys = key_grads[:, :head_dim].astype(jnp.bfloat16)
    grad_values = key_grads[:, head_dim:].astype(jnp.bfloat16)
    return (attended, grad_queries, grad_keys, grad_values)


def solution(mesh):
    return jax.shard_map(
        body,
        mesh=mesh,
        in_specs=(
            P(("outer", "inner"), None),
            P(("outer", "inner"), None),
            P(("outer", "inner"), None),
            P(("outer", "inner"), None),
            P(("outer", "inner")),
        ),
        out_specs=(
            P(("outer", "inner"), None),
            P(("outer", "inner"), None),
            P(("outer", "inner"), None),
            P(("outer", "inner"), None),
        ),
        check_vma=False,
    )
```

```python
import jax
import jax.numpy as jnp
from jax import lax
from jax.experimental import pallas as pl
from jax.experimental.pallas import tpu as pltpu
from jax.sharding import PartitionSpec as P

masked_score = -1e30
tile_keys = 256
log2_e = 1.4426950408889634
block_rows = 64
tag_rows = 16


def from_behind(block, axis, distance):
    devices = range(lax.axis_size(axis))
    route = [(i - distance, i) for i in devices if i - distance in devices]
    return lax.ppermute(block, axis, route)


def gather_direct(block, axis):
    count = lax.axis_size(axis)
    copies = jnp.broadcast_to(block[None], (count,) + block.shape)
    return lax.all_to_all(copies, axis, 0, 0, tiled=True)


def sum_direct(terms, axis):
    parts = lax.all_to_all(terms, axis, 0, 0, tiled=True)
    return jnp.sum(parts.astype(jnp.float32), axis=0)


def dot_nn(a, b):
    return lax.dot_general(a, b, (((1,), (0,)), ((), ())), preferred_element_type=jnp.float32)


def dot_nt(a, b):
    return lax.dot_general(a, b, (((1,), (1,)), ((), ())), preferred_element_type=jnp.float32)


def dot_tn(a, b):
    return lax.dot_general(a, b, (((0,), (0,)), ((), ())), preferred_element_type=jnp.float32)


def stack_heads(source, half, heads, head_dim):
    rows = slice(half * block_rows, (half + 1) * block_rows)
    return jnp.concatenate(
        [source[rows, h * head_dim : (h + 1) * head_dim] for h in range(heads)], axis=0
    )


def own_tile(step, low_tiles):
    half = jnp.where(step >= low_tiles, 1, 0)
    return half, pl.multiple_of((step - half * low_tiles) * tile_keys, tile_keys)


def low_tile_count(block_ref):
    per_tile = tile_keys // block_rows
    return (block_ref[0] + per_tile) // per_tile


def own_forward(
    block_ref, q_ref, k_ref, v_ref, qs_ref, ks_ref, vs_ref, slots_ref, p_ref, m_ref, l_ref, o_ref, s_ref
):
    group, span, head_dim = v_ref.shape
    heads = q_ref.shape[1] // head_dim
    steps, _, width = p_ref.shape
    blocks = 2 * group
    exponent_scale = log2_e * float(head_dim) ** (-0.5)
    for half in range(2):
        qs_ref[half] = stack_heads(q_ref, half, heads, head_dim)
    for g in range(group):
        slot = jnp.max(k_ref[g, span:, :].astype(jnp.float32)).astype(jnp.int32)
        slots_ref[g] = slot
        for half, place in ((0, slot), (1, blocks - 1 - slot)):
            target = pl.ds(pl.multiple_of(place * block_rows, block_rows), block_rows)
            rows = slice(half * block_rows, (half + 1) * block_rows)
            ks_ref[target, :] = k_ref[g, rows, :]
            vs_ref[target, :] = v_ref[g, rows, :]
    m_ref[...] = jnp.full(m_ref.shape, masked_score, jnp.float32)
    l_ref[...] = jnp.zeros(l_ref.shape, jnp.float32)
    o_ref[...] = jnp.zeros(o_ref.shape, jnp.float32)
    low_tiles = low_tile_count(block_ref)
    key_row = lax.broadcasted_iota(jnp.int32, (tile_keys, width), 0)
    query_row = lax.rem(lax.broadcasted_iota(jnp.int32, (1, width), 1), block_rows)
    for step in range(steps):
        half, start = own_tile(step, low_tiles)
        scores = dot_nt(ks_ref[pl.ds(start, tile_keys), :], qs_ref[half])
        block = jnp.where(half == 1, blocks - 1 - block_ref[0], block_ref[0])
        limit = block * block_rows + query_row - start
        scores = jnp.where(key_row <= limit, scores, masked_score)
        s_ref[step] = scores
        m_ref[half] = jnp.maximum(m_ref[half], jnp.max(scores, axis=0, keepdims=True))
    for step in range(steps):
        half, start = own_tile(step, low_tiles)
        raised = jnp.exp2((s_ref[step] - m_ref[half]) * exponent_scale)
        l_ref[half] += jnp.sum(raised, axis=0, keepdims=True)
        raised = raised.astype(jnp.bfloat16)
        p_ref[step] = raised
        o_ref[half] += dot_tn(vs_ref[pl.ds(start, tile_keys), :], raised)


def prev_both(
    has_ref, qs_ref, do_ref, k_ref, v_ref, m_own_ref, l_own_ref, o_own_ref,
    att_ref, terms_ref, dos_ref, shift_ref, dqt_ref, s_ref, p_ref,
):
    group, span, head_dim = v_ref.shape
    _, width, _ = qs_ref.shape
    heads = width // block_rows
    per_tile = tile_keys // span
    tiles = group // per_tile
    scale = float(head_dim) ** (-0.5)
    exponent_scale = log2_e * scale
    has_prev = has_ref[0] > 0

    def key_tile(ref, tile):
        return jnp.concatenate(
            [ref[tile * per_tile + j, :span, :] for j in range(per_tile)], axis=0
        )

    m_prev, shifts, scaled = [], [], []
    for half in range(2):
        peak = jnp.full((1, width), masked_score, jnp.float32)
        for tile in range(tiles):
            scores = dot_nt(key_tile(k_ref, tile), qs_ref[half])
            s_ref[half, tile] = scores
            peak = jnp.maximum(peak, jnp.max(scores, axis=0, keepdims=True))
        m_prev.append(jnp.where(has_prev, peak, masked_score))
    for half in range(2):
        peak = m_prev[half]
        total = jnp.zeros((1, width), jnp.float32)
        out = jnp.zeros((head_dim, width), jnp.float32)
        for tile in range(tiles):
            raised = jnp.exp2(
                jnp.where(has_prev, s_ref[half, tile] - peak, 0.0) * exponent_scale
            )
            total += jnp.sum(raised, axis=0, keepdims=True)
            raised = raised.astype(jnp.bfloat16)
            p_ref[half, tile] = raised
            out += dot_tn(key_tile(v_ref, tile), raised)
        top = jnp.maximum(peak, m_own_ref[half])
        own_factor = jnp.exp2((m_own_ref[half] - top) * exponent_scale)
        prev_factor = jnp.where(has_prev, jnp.exp2((peak - top) * exponent_scale), 0.0)
        full = own_factor * l_own_ref[half] + prev_factor * total
        inverse = 1.0 / full
        own_factor = own_factor * inverse
        prev_factor = prev_factor * inverse
        out = (own_factor * o_own_ref[half] + prev_factor * out).astype(jnp.bfloat16)
        out = out.astype(jnp.float32)
        grad = stack_heads(do_ref, half, heads, head_dim).astype(jnp.float32).T
        delta = jnp.sum(grad * out, axis=0, keepdims=True)
        dos_ref[half] = (grad * own_factor).astype(jnp.bfloat16)
        shift_ref[half] = delta * own_factor
        scaled.append((grad * prev_factor).astype(jnp.bfloat16))
        shifts.append(delta * prev_factor)
        out = out.T.astype(jnp.bfloat16)
        for h in range(heads):
            att_ref[half * block_rows : (half + 1) * block_rows, h * head_dim : (h + 1) * head_dim] = (
                out[h * block_rows : (h + 1) * block_rows]
            )
    dqt_ref[...] = jnp.zeros(dqt_ref.shape, jnp.float32)
    for tile in range(tiles):
        keys, values = key_tile(k_ref, tile), key_tile(v_ref, tile)
        key_grad = jnp.zeros((tile_keys, head_dim), jnp.float32)
        value_grad = jnp.zeros((tile_keys, head_dim), jnp.float32)
        for half in range(2):
            weights = p_ref[half, tile]
            value_grad += dot_nt(weights, scaled[half])
            change = dot_nn(values, scaled[half]) - shifts[half]
            change = (weights.astype(jnp.float32) * change).astype(jnp.bfloat16)
            key_grad += dot_nn(change, qs_ref[half])
            dqt_ref[half] += dot_tn(keys, change)
        key_grad = (key_grad * scale).astype(jnp.bfloat16)
        value_grad = value_grad.astype(jnp.bfloat16)
        for j in range(per_tile):
            rows = slice(j * span, (j + 1) * span)
            terms_ref[tile * per_tile + j, :, :head_dim] = key_grad[rows]
            terms_ref[tile * per_tile + j, :, head_dim:] = value_grad[rows]


def own_backward(
    block_ref, slots_ref, qs_ref, ks_ref, vs_ref, p_ref, dos_ref, shift_ref, dqt_ref,
    dq_ref, terms_ref, acc_ref, dqa_ref,
):
    steps, _, width = p_ref.shape
    group, span, _ = terms_ref.shape
    head_dim = ks_ref.shape[1]
    heads = width // block_rows
    blocks = 2 * group
    scale = float(head_dim) ** (-0.5)
    acc_ref[...] = jnp.zeros(acc_ref.shape, jnp.float32)
    dqa_ref[...] = dqt_ref[...]
    low_tiles = low_tile_count(block_ref)
    for step in range(steps):
        half, start = own_tile(step, low_tiles)
        window = pl.ds(start, tile_keys)
        weights = p_ref[step]
        grad = dos_ref[half]
        acc_ref[window, head_dim:] += dot_nt(weights, grad)
        change = dot_nn(vs_ref[window, :], grad) - shift_ref[half]
        change = (weights.astype(jnp.float32) * change).astype(jnp.bfloat16)
        acc_ref[window, :head_dim] += dot_nn(change, qs_ref[half]) * scale
        dqa_ref[half] += dot_tn(ks_ref[window, :], change)
    for g in range(group):
        slot = slots_ref[g]
        for half, place in ((0, slot), (1, blocks - 1 - slot)):
            source = pl.ds(pl.multiple_of(place * block_rows, block_rows), block_rows)
            terms_ref[g, half * block_rows : (half + 1) * block_rows, :] = acc_ref[
                source, :
            ].astype(jnp.bfloat16)
    for half in range(2):
        grad = (dqa_ref[half].T * scale).astype(jnp.bfloat16)
        for h in range(heads):
            dq_ref[half * block_rows : (half + 1) * block_rows, h * head_dim : (h + 1) * head_dim] = (
                grad[h * block_rows : (h + 1) * block_rows]
            )


def call(kernel, name, outs, in_smem, scratch, out_smem=(), flops=0):
    vmem = pl.BlockSpec(memory_space=pltpu.VMEM)
    smem = pl.BlockSpec(memory_space=pltpu.SMEM)

    def run(*operands):
        return pl.pallas_call(
            kernel,
            name=name,
            out_shape=[jax.ShapeDtypeStruct(shape, dtype) for shape, dtype in outs],
            in_specs=[smem if i in in_smem else vmem for i in range(len(operands))],
            out_specs=[smem if i in out_smem else vmem for i in range(len(outs))],
            scratch_shapes=[pltpu.VMEM(shape, dtype) for shape, dtype in scratch],
            compiler_params=pltpu.CompilerParams(vmem_limit_bytes=48 * 1024 * 1024),
            cost_estimate=pl.CostEstimate(flops=flops, bytes_accessed=4 << 20, transcendentals=0),
        )(*operands)

    return run


def body(queries, key_vectors, value_vectors, grad_output, positions):
    tok_rows, full_width = queries.shape
    head_dim = key_vectors.shape[1]
    heads = full_width // head_dim
    group = lax.axis_size("inner")
    span_rows = group * tok_rows
    width = heads * block_rows
    steps = span_rows // tile_keys + 1
    bf16, f32 = jnp.bfloat16, jnp.float32
    block = (positions[:1] % span_rows) // block_rows
    tag = jnp.broadcast_to(block.astype(bf16)[:, None], (tag_rows, head_dim))
    key_group = gather_direct(jnp.concatenate([key_vectors, tag], axis=0), "inner")
    value_group = gather_direct(value_vectors, "inner")
    prev_keys = from_behind(key_group, "outer", 1)
    prev_values = from_behind(value_group, "outer", 1)
    has_prev = (lax.axis_index("outer") > 0).astype(jnp.int32).reshape(1)

    unit = 2 * tile_keys * width * head_dim
    row_stat = ((2, 1, width), f32)
    by_query = ((2, head_dim, width), f32)
    qs, ks, vs, slots, p_own, m_own, l_own, o_own = call(
        own_forward,
        "own_forward",
        [
            ((2, width, head_dim), bf16),
            ((span_rows, head_dim), bf16),
            ((span_rows, head_dim), bf16),
            ((group,), jnp.int32),
            ((steps, tile_keys, width), bf16),
            row_stat,
            row_stat,
            by_query,
        ],
        (0,),
        [((steps, tile_keys, width), f32)],
        out_smem=(3,),
        flops=2 * steps * unit,
    )(block, queries, key_group, value_group)
    tiles = span_rows // tile_keys
    attended, prev_terms, dos, shift, dqt = call(
        prev_both,
        "prev_both",
        [
            ((tok_rows, full_width), bf16),
            ((group, tok_rows, 2 * head_dim), bf16),
            ((2, head_dim, width), bf16),
            row_stat,
            by_query,
        ],
        (0,),
        [((2, tiles, tile_keys, width), f32), ((2, tiles, tile_keys, width), bf16)],
        flops=6 * 2 * tiles * unit,
    )(has_prev, qs, grad_output, prev_keys, prev_values, m_own, l_own, o_own)
    returned = from_behind(prev_terms, "outer", -1)
    grad_queries, own_terms = call(
        own_backward,
        "own_backward",
        [((tok_rows, full_width), bf16), ((group, tok_rows, 2 * head_dim), bf16)],
        (0, 1),
        [((span_rows, 2 * head_dim), f32), by_query],
        flops=4 * steps * unit,
    )(block, slots, qs, ks, vs, p_own, dos, shift, dqt)
    terms = (own_terms.astype(f32) + returned.astype(f32)).astype(bf16)
    key_grads = sum_direct(terms, "inner")
    grad_keys = key_grads[:, :head_dim].astype(bf16)
    grad_values = key_grads[:, head_dim:].astype(bf16)
    return (attended, grad_queries, grad_keys, grad_values)


def solution(mesh):
    rows = P(("outer", "inner"), None)
    return jax.shard_map(
        body,
        mesh=mesh,
        in_specs=(rows, rows, rows, rows, P(("outer", "inner"))),
        out_specs=(rows, rows, rows, rows),
        check_vma=False,
    )
```

```python
import jax
import jax.numpy as jnp
from jax import lax
from jax.experimental import pallas as pl
from jax.experimental.pallas import tpu as pltpu
from jax.sharding import PartitionSpec as P

masked_score = -1e30
tile_keys = 256
log2_e = 1.4426950408889634
block_rows = 64
tag_rows = 16


def from_behind(block, axis, distance):
    devices = range(lax.axis_size(axis))
    route = [(i - distance, i) for i in devices if i - distance in devices]
    return lax.ppermute(block, axis, route)


def to_partner(block, axis):
    return lax.ppermute(block, axis, [(i, i ^ 1) for i in range(lax.axis_size(axis))])


def exchange(parts, axis):
    count = lax.axis_size(axis)
    groups = [list(range(first, count, 2)) for first in range(2)]
    return lax.all_to_all(parts, axis, 0, 0, axis_index_groups=groups, tiled=True)


def dot_nn(a, b):
    return lax.dot_general(a, b, (((1,), (0,)), ((), ())), preferred_element_type=jnp.float32)


def dot_nt(a, b):
    return lax.dot_general(a, b, (((1,), (1,)), ((), ())), preferred_element_type=jnp.float32)


def dot_tn(a, b):
    return lax.dot_general(a, b, (((0,), (0,)), ((), ())), preferred_element_type=jnp.float32)


def stack_heads(source, half, heads, head_dim):
    rows = slice(half * block_rows, (half + 1) * block_rows)
    return jnp.concatenate(
        [source[rows, h * head_dim : (h + 1) * head_dim] for h in range(heads)], axis=0
    )


def own_tile(step, allowed_ref):
    low = 0 if step < 5 else 2
    local = step % 5
    per_tile = tile_keys // block_rows
    low_tiles = (allowed_ref[low] + per_tile - 1) // per_tile
    high = jnp.where(local >= low_tiles, 1, 0)
    tile = local - high * low_tiles
    return low + high, tile


def own_forward(
    block_ref, q_ref, q_partner_ref, kv_ref,
    qs_ref, ks_ref, vs_ref, slots_ref, allowed_ref, p_ref, m_ref, l_ref, o_ref, s_ref,
):
    group, _, both = kv_ref.shape
    head_dim = both // 2
    span = 2 * block_rows
    heads = q_ref.shape[1] // head_dim
    steps, _, width = p_ref.shape
    blocks = 2 * group
    tiles = blocks * block_rows // tile_keys
    exponent_scale = log2_e * float(head_dim) ** (-0.5)
    for j, source in enumerate((q_ref, q_partner_ref)):
        for half in range(2):
            qs_ref[2 * j + half] = stack_heads(source, half, heads, head_dim)
    tags = [jnp.max(kv_ref[g, span:, :].astype(jnp.float32)).astype(jnp.int32) for g in range(group)]

    def count(test):
        return sum(jnp.where(test(tag), 1, 0) for tag in tags)

    for j in range(2):
        mine = block_ref[j]
        allowed_ref[2 * j] = count(lambda tag: tag <= mine)
        allowed_ref[2 * j + 1] = blocks - count(lambda tag: tag < mine)
    for g in range(group):
        slot = count(lambda tag: tag < tags[g])
        slots_ref[g] = slot
        for half, place in ((0, slot), (1, blocks - 1 - slot)):
            target = pl.ds(pl.multiple_of(place * block_rows, block_rows), block_rows)
            rows = slice(half * block_rows, (half + 1) * block_rows)
            ks_ref[target, :] = kv_ref[g, rows, :head_dim]
            vs_ref[target, :] = kv_ref[g, rows, head_dim:]
    m_ref[...] = jnp.full(m_ref.shape, masked_score, jnp.float32)
    l_ref[...] = jnp.zeros(l_ref.shape, jnp.float32)
    o_ref[...] = jnp.zeros(o_ref.shape, jnp.float32)
    key_row = lax.broadcasted_iota(jnp.int32, (tile_keys, width), 0)
    query_row = lax.rem(lax.broadcasted_iota(jnp.int32, (1, width), 1), block_rows)
    for step in range(steps):
        at, tile = own_tile(step, allowed_ref)
        start = pl.multiple_of(jnp.minimum(tile, tiles - 1) * tile_keys, tile_keys)
        scores = dot_nt(ks_ref[pl.ds(start, tile_keys), :], qs_ref[at])
        last = query_row if step < 5 else block_rows - 1
        limit = (allowed_ref[at] - 1) * block_rows + last - tile * tile_keys
        scores = jnp.where(key_row <= limit, scores, masked_score)
        s_ref[step] = scores
        m_ref[at] = jnp.maximum(m_ref[at], jnp.max(scores, axis=0, keepdims=True))
    for step in range(steps):
        at, tile = own_tile(step, allowed_ref)
        start = pl.multiple_of(jnp.minimum(tile, tiles - 1) * tile_keys, tile_keys)
        raised = jnp.exp2((s_ref[step] - m_ref[at]) * exponent_scale)
        l_ref[at] += jnp.sum(raised, axis=0, keepdims=True)
        raised = raised.astype(jnp.bfloat16)
        p_ref[step] = raised
        o_ref[at] += dot_tn(vs_ref[pl.ds(start, tile_keys), :], raised)


def key_tile(ref, tile, columns):
    per_tile = tile_keys // (2 * block_rows)
    return jnp.concatenate(
        [ref[tile * per_tile + j, : 2 * block_rows, columns] for j in range(per_tile)], axis=0
    )


def prev_forward(
    has_ref, qs_ref, do_ref, do_partner_ref, kv_ref, m_own_ref, l_own_ref, o_own_ref,
    p_ref, m_prev_ref, stats_ref, dot_ref, out_ref, sent_ref, s_ref,
):
    sets, width, head_dim = qs_ref.shape
    heads = width // block_rows
    tiles = p_ref.shape[1]
    exponent_scale = log2_e * float(head_dim) ** (-0.5)
    has_prev = has_ref[0] > 0
    for at in range(sets):
        peak = jnp.full((1, width), masked_score, jnp.float32)
        for tile in range(tiles):
            scores = dot_nt(key_tile(kv_ref, tile, slice(0, head_dim)), qs_ref[at])
            s_ref[at, tile] = scores
            peak = jnp.maximum(peak, jnp.max(scores, axis=0, keepdims=True))
        m_prev_ref[at] = peak
    for at in range(sets):
        peak = m_prev_ref[at]
        total = jnp.zeros((1, width), jnp.float32)
        out = jnp.zeros((head_dim, width), jnp.float32)
        for tile in range(tiles):
            raised = jnp.exp2((s_ref[at, tile] - peak) * exponent_scale)
            total += jnp.sum(raised, axis=0, keepdims=True)
            raised = raised.astype(jnp.bfloat16)
            p_ref[at, tile] = raised
            out += dot_tn(key_tile(kv_ref, tile, slice(head_dim, 2 * head_dim)), raised)
        peak = jnp.where(has_prev, peak, masked_score)
        m_prev_ref[at] = peak
        top = jnp.maximum(peak, m_own_ref[at])
        own_factor = jnp.exp2((m_own_ref[at] - top) * exponent_scale)
        prev_factor = jnp.where(has_prev, jnp.exp2((peak - top) * exponent_scale), 0.0)
        total = own_factor * l_own_ref[at] + prev_factor * total
        out = own_factor * o_own_ref[at] + prev_factor * out
        grad = stack_heads((do_ref, do_partner_ref)[at // 2], at % 2, heads, head_dim)
        grad = grad.astype(jnp.float32).T
        dot_ref[at] = grad.astype(jnp.bfloat16)
        stats_ref[0, at] = top
        stats_ref[1, at] = total
        stats_ref[2, at] = jnp.sum(grad * out, axis=0, keepdims=True)
        if at < 2:
            out_ref[at] = out
        else:
            share = jnp.where(total > 0, 1.0 / total, 0.0)
            sent_ref[at - 2] = (out * share).astype(jnp.bfloat16)


def prev_backward(
    has_ref, qs_ref, dot_ref, kv_ref, p_ref, m_own_ref, m_prev_ref, stats_ref, other_ref,
    terms_ref, dos_ref, shift_ref, dqt_ref, factor_ref, scaled_ref, lower_ref,
):
    sets, width, head_dim = qs_ref.shape
    tiles = p_ref.shape[1]
    span = terms_ref.shape[1]
    per_tile = tile_keys // span
    scale = float(head_dim) ** (-0.5)
    exponent_scale = log2_e * scale
    has_prev = has_ref[0] > 0
    for at in range(sets):
        there = (at + 2) % 4
        top = jnp.maximum(stats_ref[0, at], other_ref[0, there])
        here = jnp.exp2((stats_ref[0, at] - top) * exponent_scale)
        away = jnp.exp2((other_ref[0, there] - top) * exponent_scale)
        inverse = 1.0 / (here * stats_ref[1, at] + away * other_ref[1, there])
        delta = (here * stats_ref[2, at] + away * other_ref[2, there]) * inverse
        if at < 2:
            factor_ref[0, at] = here * inverse
            factor_ref[1, at] = away * other_ref[1, there] * inverse
        own_factor = jnp.exp2((m_own_ref[at] - top) * exponent_scale) * inverse
        prev_factor = jnp.exp2((m_prev_ref[at] - top) * exponent_scale) * inverse
        prev_factor = jnp.where(has_prev, prev_factor, 0.0)
        grad = dot_ref[at].astype(jnp.float32)
        dos_ref[at] = (grad * own_factor).astype(jnp.bfloat16)
        shift_ref[at] = delta * own_factor
        scaled_ref[at] = (grad * prev_factor).astype(jnp.bfloat16)
        lower_ref[at] = delta * prev_factor
    dqt_ref[...] = jnp.zeros(dqt_ref.shape, jnp.float32)
    for tile in range(tiles):
        keys = key_tile(kv_ref, tile, slice(0, head_dim))
        values = key_tile(kv_ref, tile, slice(head_dim, 2 * head_dim))
        key_grad = jnp.zeros((tile_keys, head_dim), jnp.float32)
        value_grad = jnp.zeros((tile_keys, head_dim), jnp.float32)
        for at in range(sets):
            weights = p_ref[at, tile]
            value_grad += dot_nt(weights, scaled_ref[at])
            change = dot_nn(values, scaled_ref[at]) - lower_ref[at]
            change = (weights.astype(jnp.float32) * change).astype(jnp.bfloat16)
            key_grad += dot_nn(change, qs_ref[at])
            dqt_ref[at] += dot_tn(keys, change)
        key_grad = (key_grad * scale).astype(jnp.bfloat16)
        value_grad = value_grad.astype(jnp.bfloat16)
        for j in range(per_tile):
            rows = slice(j * span, (j + 1) * span)
            terms_ref[tile * per_tile + j, :, :head_dim] = key_grad[rows]
            terms_ref[tile * per_tile + j, :, head_dim:] = value_grad[rows]


def own_backward(
    allowed_ref, slots_ref, qs_ref, ks_ref, vs_ref, p_ref, dos_ref, shift_ref, dqt_ref,
    out_ref, got_ref, factor_ref,
    att_ref, dq_ref, dq_partner_ref, terms_ref, acc_ref, dqa_ref,
):
    steps, _, width = p_ref.shape
    group, span, _ = terms_ref.shape
    head_dim = ks_ref.shape[1]
    heads = width // block_rows
    blocks = 2 * group
    tiles = blocks * block_rows // tile_keys
    scale = float(head_dim) ** (-0.5)

    def store_heads(target_ref, half, block):
        rows = slice(half * block_rows, (half + 1) * block_rows)
        for h in range(heads):
            target_ref[rows, h * head_dim : (h + 1) * head_dim] = block[
                h * block_rows : (h + 1) * block_rows
            ].astype(target_ref.dtype)

    acc_ref[...] = jnp.zeros(acc_ref.shape, jnp.float32)
    dqa_ref[...] = dqt_ref[...]
    for step in range(steps):
        at, tile = own_tile(step, allowed_ref)
        start = pl.multiple_of(jnp.minimum(tile, tiles - 1) * tile_keys, tile_keys)
        window = pl.ds(start, tile_keys)
        weights = p_ref[step]
        grad = dos_ref[at]
        acc_ref[window, head_dim:] += dot_nt(weights, grad)
        change = dot_nn(vs_ref[window, :], grad) - shift_ref[at]
        change = (weights.astype(jnp.float32) * change).astype(jnp.bfloat16)
        acc_ref[window, :head_dim] += dot_nn(change, qs_ref[at]) * scale
        dqa_ref[at] += dot_tn(ks_ref[window, :], change)
    for g in range(group):
        slot = slots_ref[g]
        for half, place in ((0, slot), (1, blocks - 1 - slot)):
            source = pl.ds(pl.multiple_of(place * block_rows, block_rows), block_rows)
            terms_ref[g, half * block_rows : (half + 1) * block_rows, :] = acc_ref[
                source, :
            ].astype(jnp.bfloat16)
    for half in range(2):
        out = factor_ref[0, half] * out_ref[half] + factor_ref[1, half] * got_ref[half].astype(jnp.float32)
        store_heads(att_ref, half, out.T)
        store_heads(dq_ref, half, dqa_ref[half].T * scale)
        store_heads(dq_partner_ref, half, dqa_ref[2 + half].T * scale)


def call(kernel, name, outs, in_smem, scratch, out_smem=(), flops=0):
    vmem = pl.BlockSpec(memory_space=pltpu.VMEM)
    smem = pl.BlockSpec(memory_space=pltpu.SMEM)

    def run(*operands):
        return pl.pallas_call(
            kernel,
            name=name,
            out_shape=[jax.ShapeDtypeStruct(shape, dtype) for shape, dtype in outs],
            in_specs=[smem if i in in_smem else vmem for i in range(len(operands))],
            out_specs=[smem if i in out_smem else vmem for i in range(len(outs))],
            scratch_shapes=[pltpu.VMEM(shape, dtype) for shape, dtype in scratch],
            compiler_params=pltpu.CompilerParams(vmem_limit_bytes=32 * 1024 * 1024),
            cost_estimate=pl.CostEstimate(flops=flops, bytes_accessed=4 << 20, transcendentals=0),
        )(*operands)

    return run


def body(queries, key_vectors, value_vectors, grad_output, positions):
    tok_rows, full_width = queries.shape
    head_dim = key_vectors.shape[1]
    heads = full_width // head_dim
    group = lax.axis_size("inner") // 2
    segment = 2 * group * tok_rows
    span_rows = group * tok_rows
    width = heads * block_rows
    steps = 10
    bf16, f32 = jnp.bfloat16, jnp.float32
    block = (positions[:1] % segment) // block_rows
    query_partner = to_partner(queries, "inner")
    grad_partner = to_partner(grad_output, "inner")
    both_blocks = jnp.concatenate([block, (to_partner(positions, "inner")[:1] % segment) // block_rows])
    tag = jnp.broadcast_to(block.astype(bf16)[:, None], (tag_rows, 2 * head_dim))
    key_value = jnp.concatenate([jnp.concatenate([key_vectors, value_vectors], axis=1), tag], axis=0)
    group_kv = exchange(jnp.broadcast_to(key_value[None], (group,) + key_value.shape), "inner")
    prev_kv = from_behind(group_kv, "outer", 1)
    has_prev = (lax.axis_index("outer") > 0).astype(jnp.int32).reshape(1)

    unit = 2 * tile_keys * width * head_dim
    row_stat = ((4, 1, width), f32)
    by_query = ((4, head_dim, width), f32)
    by_query_16 = ((4, head_dim, width), bf16)
    tokens = ((tok_rows, full_width), bf16)
    terms_shape = ((group, tok_rows, 2 * head_dim), bf16)
    tiles = span_rows // tile_keys
    qs, ks, vs, slots, allowed, p_own, m_own, l_own, o_own = call(
        own_forward,
        "own_forward",
        [
            ((4, width, head_dim), bf16),
            ((span_rows, head_dim), bf16),
            ((span_rows, head_dim), bf16),
            ((group,), jnp.int32),
            ((4,), jnp.int32),
            ((steps, tile_keys, width), bf16),
            row_stat,
            row_stat,
            by_query,
        ],
        (0,),
        [((steps, tile_keys, width), f32)],
        out_smem=(3, 4),
        flops=2 * steps * unit,
    )(both_blocks, queries, query_partner, group_kv)
    p_prev, m_prev, stats, dot, out, sent = call(
        prev_forward,
        "prev_forward",
        [
            ((4, tiles, tile_keys, width), bf16),
            row_stat,
            ((3, 4, 1, width), f32),
            by_query_16,
            ((2, head_dim, width), f32),
            ((2, head_dim, width), bf16),
        ],
        (0,),
        [((4, tiles, tile_keys, width), f32)],
        flops=2 * 4 * tiles * unit,
    )(has_prev, qs, grad_output, grad_partner, prev_kv, m_own, l_own, o_own)
    other = to_partner(stats, "inner")
    got = to_partner(sent, "inner")
    prev_terms, dos, shift, dqt, factor = call(
        prev_backward,
        "prev_backward",
        [terms_shape, by_query_16, row_stat, by_query, ((2, 2, 1, width), f32)],
        (0,),
        [by_query_16, row_stat],
        flops=4 * 4 * tiles * unit,
    )(has_prev, qs, dot, prev_kv, p_prev, m_own, m_prev, stats, other)
    returned = from_behind(prev_terms, "outer", -1)
    attended, dq, dq_partner, own_terms = call(
        own_backward,
        "own_backward",
        [tokens, ((tok_rows, full_width), f32), tokens, terms_shape],
        (0, 1),
        [((span_rows, 2 * head_dim), f32), by_query],
        flops=4 * steps * unit,
    )(allowed, slots, qs, ks, vs, p_own, dos, shift, dqt, out, got, factor)
    dq_other = to_partner(dq_partner, "inner")
    terms = (own_terms.astype(f32) + returned.astype(f32)).astype(bf16)
    key_grads = jnp.sum(exchange(terms, "inner").astype(f32), axis=0)
    grad_queries = (dq + dq_other.astype(f32)).astype(bf16)
    grad_keys = key_grads[:, :head_dim].astype(bf16)
    grad_values = key_grads[:, head_dim:].astype(bf16)
    return (attended, grad_queries, grad_keys, grad_values)


def solution(mesh):
    rows = P(("outer", "inner"), None)
    return jax.shard_map(
        body,
        mesh=mesh,
        in_specs=(rows, rows, rows, rows, P(("outer", "inner"))),
        out_specs=(rows, rows, rows, rows),
        check_vma=False,
    )
```

```python
import jax
import jax.numpy as jnp
from jax import lax
from jax.experimental import pallas as pl
from jax.experimental.pallas import tpu as pltpu
from jax.sharding import PartitionSpec as P

masked_score = -1e30
tile_keys = 256
log2_e = 1.4426950408889634
block_rows = 64
tag_rows = 16


def from_behind(block, axis, distance):
    devices = range(lax.axis_size(axis))
    route = [(i - distance, i) for i in devices if i - distance in devices]
    return lax.ppermute(block, axis, route)


def to_partner(block, axis):
    return lax.ppermute(block, axis, [(i, i ^ 1) for i in range(lax.axis_size(axis))])


def exchange(parts, axis):
    count = lax.axis_size(axis)
    groups = [list(range(first, count, 2)) for first in range(2)]
    return lax.all_to_all(parts, axis, 0, 0, axis_index_groups=groups, tiled=True)


def dot_nn(a, b):
    return lax.dot_general(a, b, (((1,), (0,)), ((), ())), preferred_element_type=jnp.float32)


def dot_nt(a, b):
    return lax.dot_general(a, b, (((1,), (1,)), ((), ())), preferred_element_type=jnp.float32)


def dot_tn(a, b):
    return lax.dot_general(a, b, (((0,), (0,)), ((), ())), preferred_element_type=jnp.float32)


def stack_heads(source, half, heads, head_dim):
    rows = slice(half * block_rows, (half + 1) * block_rows)
    return jnp.concatenate(
        [source[rows, h * head_dim : (h + 1) * head_dim] for h in range(heads)], axis=0
    )


def store_heads(target_ref, half, block):
    rows = slice(half * block_rows, (half + 1) * block_rows)
    head_dim = block.shape[1]
    for h in range(block.shape[0] // block_rows):
        target_ref[rows, h * head_dim : (h + 1) * head_dim] = block[
            h * block_rows : (h + 1) * block_rows
        ].astype(target_ref.dtype)


def pack(position_ref, key_ref, value_ref, packed_ref):
    count, rows, both = packed_ref.shape
    span = key_ref.shape[0]
    segment = 2 * count * span
    tag = (lax.rem(position_ref[0], segment) // block_rows).astype(jnp.float32)
    tag = jnp.full((rows - span, both), tag, jnp.float32).astype(packed_ref.dtype)
    for g in range(count):
        packed_ref[g, :span, : both // 2] = key_ref[...]
        packed_ref[g, :span, both // 2 :] = value_ref[...]
        packed_ref[g, span:, :] = tag


def stack_pair(q_ref, q_partner_ref, do_ref, do_partner_ref, qs_ref, dot_ref):
    _, width, head_dim = qs_ref.shape
    heads = width // block_rows
    for j, (query, grad) in enumerate(((q_ref, do_ref), (q_partner_ref, do_partner_ref))):
        for half in range(2):
            qs_ref[2 * j + half] = stack_heads(query, half, heads, head_dim)
            stacked = stack_heads(grad, half, heads, head_dim).astype(jnp.float32)
            dot_ref[2 * j + half] = stacked.T.astype(jnp.bfloat16)


def merge_attended(out_ref, got_ref, factor_ref, att_ref):
    for half in range(2):
        out = factor_ref[0, half] * out_ref[half]
        out = out + factor_ref[1, half] * got_ref[half].astype(jnp.float32)
        store_heads(att_ref, half, out.T)


def own_tile(step, allowed_ref):
    low = 0 if step < 5 else 2
    local = step % 5
    per_tile = tile_keys // block_rows
    low_tiles = (allowed_ref[low] + per_tile - 1) // per_tile
    high = jnp.where(local >= low_tiles, 1, 0)
    tile = local - high * low_tiles
    return low + high, tile


def own_forward(
    block_ref, qs_ref, kv_ref,
    ks_ref, vs_ref, slots_ref, allowed_ref, p_ref, m_ref, l_ref, o_ref, s_ref,
):
    group, _, both = kv_ref.shape
    head_dim = both // 2
    span = 2 * block_rows
    steps, _, width = p_ref.shape
    blocks = 2 * group
    tiles = blocks * block_rows // tile_keys
    exponent_scale = log2_e * float(head_dim) ** (-0.5)
    tags = [jnp.max(kv_ref[g, span:, :].astype(jnp.float32)).astype(jnp.int32) for g in range(group)]

    def count(test):
        return sum(jnp.where(test(tag), 1, 0) for tag in tags)

    for j in range(2):
        mine = block_ref[j]
        allowed_ref[2 * j] = count(lambda tag: tag <= mine)
        allowed_ref[2 * j + 1] = blocks - count(lambda tag: tag < mine)
    for g in range(group):
        slot = count(lambda tag: tag < tags[g])
        slots_ref[g] = slot
        for half, place in ((0, slot), (1, blocks - 1 - slot)):
            target = pl.ds(pl.multiple_of(place * block_rows, block_rows), block_rows)
            rows = slice(half * block_rows, (half + 1) * block_rows)
            ks_ref[target, :] = kv_ref[g, rows, :head_dim]
            vs_ref[target, :] = kv_ref[g, rows, head_dim:]
    m_ref[...] = jnp.full(m_ref.shape, masked_score, jnp.float32)
    l_ref[...] = jnp.zeros(l_ref.shape, jnp.float32)
    o_ref[...] = jnp.zeros(o_ref.shape, jnp.float32)
    key_row = lax.broadcasted_iota(jnp.int32, (tile_keys, width), 0)
    query_row = lax.rem(lax.broadcasted_iota(jnp.int32, (1, width), 1), block_rows)
    for step in range(steps):
        at, tile = own_tile(step, allowed_ref)
        start = pl.multiple_of(jnp.minimum(tile, tiles - 1) * tile_keys, tile_keys)
        scores = dot_nt(ks_ref[pl.ds(start, tile_keys), :], qs_ref[at])
        last = query_row if step < 5 else block_rows - 1
        limit = (allowed_ref[at] - 1) * block_rows + last - tile * tile_keys
        scores = jnp.where(key_row <= limit, scores, masked_score)
        s_ref[step] = scores
        m_ref[at] = jnp.maximum(m_ref[at], jnp.max(scores, axis=0, keepdims=True))
    for step in range(steps):
        at, tile = own_tile(step, allowed_ref)
        start = pl.multiple_of(jnp.minimum(tile, tiles - 1) * tile_keys, tile_keys)
        raised = jnp.exp2((s_ref[step] - m_ref[at]) * exponent_scale)
        l_ref[at] += jnp.sum(raised, axis=0, keepdims=True)
        raised = raised.astype(jnp.bfloat16)
        p_ref[step] = raised
        o_ref[at] += dot_tn(vs_ref[pl.ds(start, tile_keys), :], raised)


def key_tile(ref, tile, columns):
    per_tile = tile_keys // (2 * block_rows)
    return jnp.concatenate(
        [ref[tile * per_tile + j, : 2 * block_rows, columns] for j in range(per_tile)], axis=0
    )


def prev_forward(
    has_ref, qs_ref, dot_ref, kv_ref, m_own_ref, l_own_ref, o_own_ref,
    p_ref, m_prev_ref, stats_ref, out_ref, sent_ref, s_ref,
):
    sets, width, head_dim = qs_ref.shape
    tiles = p_ref.shape[1]
    exponent_scale = log2_e * float(head_dim) ** (-0.5)
    has_prev = has_ref[0] > 0
    for at in range(sets):
        peak = jnp.full((1, width), masked_score, jnp.float32)
        for tile in range(tiles):
            scores = dot_nt(key_tile(kv_ref, tile, slice(0, head_dim)), qs_ref[at])
            s_ref[at, tile] = scores
            peak = jnp.maximum(peak, jnp.max(scores, axis=0, keepdims=True))
        m_prev_ref[at] = peak
    for at in range(sets):
        peak = m_prev_ref[at]
        total = jnp.zeros((1, width), jnp.float32)
        out = jnp.zeros((head_dim, width), jnp.float32)
        for tile in range(tiles):
            raised = jnp.exp2((s_ref[at, tile] - peak) * exponent_scale)
            total += jnp.sum(raised, axis=0, keepdims=True)
            raised = raised.astype(jnp.bfloat16)
            p_ref[at, tile] = raised
            out += dot_tn(key_tile(kv_ref, tile, slice(head_dim, 2 * head_dim)), raised)
        peak = jnp.where(has_prev, peak, masked_score)
        m_prev_ref[at] = peak
        top = jnp.maximum(peak, m_own_ref[at])
        own_factor = jnp.exp2((m_own_ref[at] - top) * exponent_scale)
        prev_factor = jnp.where(has_prev, jnp.exp2((peak - top) * exponent_scale), 0.0)
        total = own_factor * l_own_ref[at] + prev_factor * total
        out = own_factor * o_own_ref[at] + prev_factor * out
        grad = dot_ref[at].astype(jnp.float32)
        stats_ref[0, at] = top
        stats_ref[1, at] = total
        stats_ref[2, at] = jnp.sum(grad * out, axis=0, keepdims=True)
        if at < 2:
            out_ref[at] = out
        else:
            share = jnp.where(total > 0, 1.0 / total, 0.0)
            sent_ref[at - 2] = (out * share).astype(jnp.bfloat16)


def prev_backward(
    has_ref, qs_ref, dot_ref, kv_ref, p_ref, m_own_ref, m_prev_ref, stats_ref, other_ref,
    terms_ref, dos_ref, shift_ref, dqt_ref, factor_ref, scaled_ref, lower_ref,
):
    sets, width, head_dim = qs_ref.shape
    tiles = p_ref.shape[1]
    span = terms_ref.shape[1]
    per_tile = tile_keys // span
    scale = float(head_dim) ** (-0.5)
    exponent_scale = log2_e * scale
    has_prev = has_ref[0] > 0
    for at in range(sets):
        there = (at + 2) % 4
        top = jnp.maximum(stats_ref[0, at], other_ref[0, there])
        here = jnp.exp2((stats_ref[0, at] - top) * exponent_scale)
        away = jnp.exp2((other_ref[0, there] - top) * exponent_scale)
        inverse = 1.0 / (here * stats_ref[1, at] + away * other_ref[1, there])
        delta = (here * stats_ref[2, at] + away * other_ref[2, there]) * inverse
        if at < 2:
            factor_ref[0, at] = here * inverse
            factor_ref[1, at] = away * other_ref[1, there] * inverse
        own_factor = jnp.exp2((m_own_ref[at] - top) * exponent_scale) * inverse
        prev_factor = jnp.exp2((m_prev_ref[at] - top) * exponent_scale) * inverse
        prev_factor = jnp.where(has_prev, prev_factor, 0.0)
        grad = dot_ref[at].astype(jnp.float32)
        dos_ref[at] = (grad * own_factor).astype(jnp.bfloat16)
        shift_ref[at] = delta * own_factor
        scaled_ref[at] = (grad * prev_factor).astype(jnp.bfloat16)
        lower_ref[at] = delta * prev_factor
    dqt_ref[...] = jnp.zeros(dqt_ref.shape, jnp.float32)
    for tile in range(tiles):
        keys = key_tile(kv_ref, tile, slice(0, head_dim))
        values = key_tile(kv_ref, tile, slice(head_dim, 2 * head_dim))
        key_grad = jnp.zeros((tile_keys, head_dim), jnp.float32)
        value_grad = jnp.zeros((tile_keys, head_dim), jnp.float32)
        for at in range(sets):
            weights = p_ref[at, tile]
            value_grad += dot_nt(weights, scaled_ref[at])
            change = dot_nn(values, scaled_ref[at]) - lower_ref[at]
            change = (weights.astype(jnp.float32) * change).astype(jnp.bfloat16)
            key_grad += dot_nn(change, qs_ref[at])
            dqt_ref[at] += dot_tn(keys, change)
        key_grad = (key_grad * scale).astype(jnp.bfloat16)
        value_grad = value_grad.astype(jnp.bfloat16)
        for j in range(per_tile):
            rows = slice(j * span, (j + 1) * span)
            terms_ref[tile * per_tile + j, :, :head_dim] = key_grad[rows]
            terms_ref[tile * per_tile + j, :, head_dim:] = value_grad[rows]


def own_backward(
    allowed_ref, slots_ref, qs_ref, ks_ref, vs_ref, p_ref, dos_ref, shift_ref, dqt_ref,
    dq_ref, dq_partner_ref, terms_ref, acc_ref, dqa_ref,
):
    steps, _, width = p_ref.shape
    group, span, _ = terms_ref.shape
    head_dim = ks_ref.shape[1]
    blocks = 2 * group
    tiles = blocks * block_rows // tile_keys
    scale = float(head_dim) ** (-0.5)

    acc_ref[...] = jnp.zeros(acc_ref.shape, jnp.float32)
    dqa_ref[...] = dqt_ref[...]
    for step in range(steps):
        at, tile = own_tile(step, allowed_ref)
        start = pl.multiple_of(jnp.minimum(tile, tiles - 1) * tile_keys, tile_keys)
        window = pl.ds(start, tile_keys)
        weights = p_ref[step]
        grad = dos_ref[at]
        acc_ref[window, head_dim:] += dot_nt(weights, grad)
        change = dot_nn(vs_ref[window, :], grad) - shift_ref[at]
        change = (weights.astype(jnp.float32) * change).astype(jnp.bfloat16)
        acc_ref[window, :head_dim] += dot_nn(change, qs_ref[at]) * scale
        dqa_ref[at] += dot_tn(ks_ref[window, :], change)
    for g in range(group):
        slot = slots_ref[g]
        for half, place in ((0, slot), (1, blocks - 1 - slot)):
            source = pl.ds(pl.multiple_of(place * block_rows, block_rows), block_rows)
            terms_ref[g, half * block_rows : (half + 1) * block_rows, :] = acc_ref[
                source, :
            ].astype(jnp.bfloat16)
    for half in range(2):
        store_heads(dq_ref, half, dqa_ref[half].T * scale)
        store_heads(dq_partner_ref, half, dqa_ref[2 + half].T * scale)


def call(kernel, name, outs, in_smem, scratch, out_smem=(), flops=0):
    vmem = pl.BlockSpec(memory_space=pltpu.VMEM)
    smem = pl.BlockSpec(memory_space=pltpu.SMEM)

    def run(*operands):
        return pl.pallas_call(
            kernel,
            name=name,
            out_shape=[jax.ShapeDtypeStruct(shape, dtype) for shape, dtype in outs],
            in_specs=[smem if i in in_smem else vmem for i in range(len(operands))],
            out_specs=[smem if i in out_smem else vmem for i in range(len(outs))],
            scratch_shapes=[pltpu.VMEM(shape, dtype) for shape, dtype in scratch],
            compiler_params=pltpu.CompilerParams(vmem_limit_bytes=32 * 1024 * 1024),
            cost_estimate=pl.CostEstimate(flops=flops, bytes_accessed=4 << 20, transcendentals=0),
        )(*operands)

    return run


def body(queries, key_vectors, value_vectors, grad_output, positions):
    tok_rows, full_width = queries.shape
    head_dim = key_vectors.shape[1]
    heads = full_width // head_dim
    group = lax.axis_size("inner") // 2
    segment = 2 * group * tok_rows
    span_rows = group * tok_rows
    width = heads * block_rows
    steps = 10
    bf16, f32 = jnp.bfloat16, jnp.float32
    block = (positions[:1] % segment) // block_rows
    query_partner = to_partner(queries, "inner")
    grad_partner = to_partner(grad_output, "inner")
    both_blocks = jnp.concatenate([block, (to_partner(positions, "inner")[:1] % segment) // block_rows])
    (packed,) = call(
        pack,
        "pack",
        [((group, tok_rows + tag_rows, 2 * head_dim), bf16)],
        (0,),
        [],
    )(positions, key_vectors, value_vectors)
    group_kv = exchange(packed, "inner")
    prev_kv = from_behind(group_kv, "outer", 1)
    has_prev = (lax.axis_index("outer") > 0).astype(jnp.int32).reshape(1)

    unit = 2 * tile_keys * width * head_dim
    row_stat = ((4, 1, width), f32)
    by_query = ((4, head_dim, width), f32)
    by_query_16 = ((4, head_dim, width), bf16)
    tokens = ((tok_rows, full_width), bf16)
    terms_shape = ((group, tok_rows, 2 * head_dim), bf16)
    tiles = span_rows // tile_keys
    qs, dot = call(
        stack_pair,
        "stack_pair",
        [((4, width, head_dim), bf16), by_query_16],
        (),
        [],
        flops=4 * 10**9,
    )(queries, query_partner, grad_output, grad_partner)
    ks, vs, slots, allowed, p_own, m_own, l_own, o_own = call(
        own_forward,
        "own_forward",
        [
            ((span_rows, head_dim), bf16),
            ((span_rows, head_dim), bf16),
            ((group,), jnp.int32),
            ((4,), jnp.int32),
            ((steps, tile_keys, width), bf16),
            row_stat,
            row_stat,
            by_query,
        ],
        (0,),
        [((steps, tile_keys, width), f32)],
        out_smem=(2, 3),
        flops=2 * steps * unit,
    )(both_blocks, qs, group_kv)
    p_prev, m_prev, stats, out, sent = call(
        prev_forward,
        "prev_forward",
        [
            ((4, tiles, tile_keys, width), bf16),
            row_stat,
            ((3, 4, 1, width), f32),
            ((2, head_dim, width), f32),
            ((2, head_dim, width), bf16),
        ],
        (0,),
        [((4, tiles, tile_keys, width), f32)],
        flops=2 * 4 * tiles * unit,
    )(has_prev, qs, dot, prev_kv, m_own, l_own, o_own)
    other = to_partner(stats, "inner")
    got = to_partner(sent, "inner")
    prev_terms, dos, shift, dqt, factor = call(
        prev_backward,
        "prev_backward",
        [terms_shape, by_query_16, row_stat, by_query, ((2, 2, 1, width), f32)],
        (0,),
        [by_query_16, row_stat],
        flops=4 * 4 * tiles * unit,
    )(has_prev, qs, dot, prev_kv, p_prev, m_own, m_prev, stats, other)
    returned = from_behind(prev_terms, "outer", -1)
    dq, dq_partner, own_terms = call(
        own_backward,
        "own_backward",
        [((tok_rows, full_width), f32), tokens, terms_shape],
        (0, 1),
        [((span_rows, 2 * head_dim), f32), by_query],
        flops=4 * steps * unit,
    )(allowed, slots, qs, ks, vs, p_own, dos, shift, dqt)
    (attended,) = call(merge_attended, "merge_attended", [tokens], (), [])(out, got, factor)
    dq_other = to_partner(dq_partner, "inner")
    terms = (own_terms.astype(f32) + returned.astype(f32)).astype(bf16)
    key_grads = jnp.sum(exchange(terms, "inner").astype(f32), axis=0)
    grad_queries = (dq + dq_other.astype(f32)).astype(bf16)
    grad_keys = key_grads[:, :head_dim].astype(bf16)
    grad_values = key_grads[:, head_dim:].astype(bf16)
    return (attended, grad_queries, grad_keys, grad_values)


def solution(mesh):
    rows = P(("outer", "inner"), None)
    return jax.shard_map(
        body,
        mesh=mesh,
        in_specs=(rows, rows, rows, rows, P(("outer", "inner"))),
        out_specs=(rows, rows, rows, rows),
        check_vma=False,
    )
```

```python
import functools

import jax
import jax.numpy as jnp
from jax import lax
from jax.experimental import pallas as pl
from jax.experimental.pallas import tpu as pltpu
from jax.sharding import PartitionSpec as P

masked_score = -1e30
tile_keys = 256
log2_e = 1.4426950408889634
block_rows = 64
tag_rows = 16


def from_behind(block, axis, distance):
    devices = range(lax.axis_size(axis))
    route = [(i - distance, i) for i in devices if i - distance in devices]
    return lax.ppermute(block, axis, route)


def to_partner(block, axis):
    return lax.ppermute(block, axis, [(i, i ^ 1) for i in range(lax.axis_size(axis))])


def exchange(parts, axis):
    count = lax.axis_size(axis)
    groups = [list(range(first, count, 2)) for first in range(2)]
    return lax.all_to_all(parts, axis, 0, 0, axis_index_groups=groups, tiled=True)


def dot_nn(a, b):
    return lax.dot_general(a, b, (((1,), (0,)), ((), ())), preferred_element_type=jnp.float32)


def dot_nt(a, b):
    return lax.dot_general(a, b, (((1,), (1,)), ((), ())), preferred_element_type=jnp.float32)


def dot_tn(a, b):
    return lax.dot_general(a, b, (((0,), (0,)), ((), ())), preferred_element_type=jnp.float32)


def stack_heads(source, half, heads, head_dim):
    rows = slice(half * block_rows, (half + 1) * block_rows)
    return jnp.concatenate(
        [source[rows, h * head_dim : (h + 1) * head_dim] for h in range(heads)], axis=0
    )


def store_heads(target_ref, half, block):
    rows = slice(half * block_rows, (half + 1) * block_rows)
    head_dim = block.shape[1]
    for h in range(block.shape[0] // block_rows):
        target_ref[rows, h * head_dim : (h + 1) * head_dim] = block[
            h * block_rows : (h + 1) * block_rows
        ].astype(target_ref.dtype)


def pack(position_ref, key_ref, value_ref, packed_ref):
    count, rows, both = packed_ref.shape
    span = key_ref.shape[0]
    tag = (lax.rem(position_ref[0], 2 * count * span) // block_rows).astype(jnp.float32)
    tag = jnp.full((rows - span, both), tag, jnp.float32).astype(packed_ref.dtype)
    for g in range(count):
        packed_ref[g, :span, : both // 2] = key_ref[...]
        packed_ref[g, :span, both // 2 :] = value_ref[...]
        packed_ref[g, span:, :] = tag


def stack_pair(
    segment, position_ref, position_partner_ref, q_ref, q_partner_ref, do_ref, do_partner_ref,
    block_ref, qs_ref, dot_ref,
):
    _, width, head_dim = qs_ref.shape
    heads = width // block_rows
    block_ref[0] = lax.rem(position_ref[0], segment) // block_rows
    block_ref[1] = lax.rem(position_partner_ref[0], segment) // block_rows
    for j, (query, grad) in enumerate(((q_ref, do_ref), (q_partner_ref, do_partner_ref))):
        for half in range(2):
            qs_ref[2 * j + half] = stack_heads(query, half, heads, head_dim)
            stacked = stack_heads(grad, half, heads, head_dim).astype(jnp.float32)
            dot_ref[2 * j + half] = stacked.T.astype(jnp.bfloat16)


def merge_attended(out_ref, got_ref, factor_ref, att_ref):
    for half in range(2):
        out = factor_ref[0, half] * out_ref[half]
        out = out + factor_ref[1, half] * got_ref[half].astype(jnp.float32)
        store_heads(att_ref, half, out.T)


def own_tile(step, allowed_ref):
    low = 0 if step < 5 else 2
    local = step % 5
    per_tile = tile_keys // block_rows
    low_tiles = (allowed_ref[low] + per_tile - 1) // per_tile
    high = jnp.where(local >= low_tiles, 1, 0)
    tile = local - high * low_tiles
    return low + high, tile


def own_forward(
    block_ref, qs_ref, kv_ref,
    ks_ref, vs_ref, slots_ref, allowed_ref, p_ref, m_ref, l_ref, o_ref, s_ref,
):
    group, _, both = kv_ref.shape
    head_dim = both // 2
    span = 2 * block_rows
    steps, _, width = p_ref.shape
    blocks = 2 * group
    tiles = blocks * block_rows // tile_keys
    exponent_scale = log2_e * float(head_dim) ** (-0.5)
    tags = [jnp.max(kv_ref[g, span:, :].astype(jnp.float32)).astype(jnp.int32) for g in range(group)]

    def count(test):
        return sum(jnp.where(test(tag), 1, 0) for tag in tags)

    for j in range(2):
        mine = block_ref[j]
        allowed_ref[2 * j] = count(lambda tag: tag <= mine)
        allowed_ref[2 * j + 1] = blocks - count(lambda tag: tag < mine)
    for g in range(group):
        slot = count(lambda tag: tag < tags[g])
        slots_ref[g] = slot
        for half, place in ((0, slot), (1, blocks - 1 - slot)):
            target = pl.ds(pl.multiple_of(place * block_rows, block_rows), block_rows)
            rows = slice(half * block_rows, (half + 1) * block_rows)
            ks_ref[target, :] = kv_ref[g, rows, :head_dim]
            vs_ref[target, :] = kv_ref[g, rows, head_dim:]
    m_ref[...] = jnp.full(m_ref.shape, masked_score, jnp.float32)
    l_ref[...] = jnp.zeros(l_ref.shape, jnp.float32)
    o_ref[...] = jnp.zeros(o_ref.shape, jnp.float32)
    key_row = lax.broadcasted_iota(jnp.int32, (tile_keys, width), 0)
    query_row = lax.rem(lax.broadcasted_iota(jnp.int32, (1, width), 1), block_rows)
    for step in range(steps):
        at, tile = own_tile(step, allowed_ref)
        start = pl.multiple_of(jnp.minimum(tile, tiles - 1) * tile_keys, tile_keys)
        scores = dot_nt(ks_ref[pl.ds(start, tile_keys), :], qs_ref[at])
        last = query_row if step < 5 else block_rows - 1
        limit = (allowed_ref[at] - 1) * block_rows + last - tile * tile_keys
        scores = jnp.where(key_row <= limit, scores, masked_score)
        s_ref[step] = scores
        m_ref[at] = jnp.maximum(m_ref[at], jnp.max(scores, axis=0, keepdims=True))
    for step in range(steps):
        at, tile = own_tile(step, allowed_ref)
        start = pl.multiple_of(jnp.minimum(tile, tiles - 1) * tile_keys, tile_keys)
        raised = jnp.exp2((s_ref[step] - m_ref[at]) * exponent_scale)
        l_ref[at] += jnp.sum(raised, axis=0, keepdims=True)
        raised = raised.astype(jnp.bfloat16)
        p_ref[step] = raised
        o_ref[at] += dot_tn(vs_ref[pl.ds(start, tile_keys), :], raised)


def key_tile(ref, tile, columns):
    per_tile = tile_keys // (2 * block_rows)
    return jnp.concatenate(
        [ref[tile * per_tile + j, : 2 * block_rows, columns] for j in range(per_tile)], axis=0
    )


def prev_forward(
    first, has_ref, qs_ref, dot_ref, kv_ref, m_own_ref, l_own_ref, o_own_ref,
    p_ref, m_prev_ref, stats_ref, out_ref, s_ref,
):
    _, width, head_dim = qs_ref.shape
    sets, tiles = p_ref.shape[:2]
    exponent_scale = log2_e * float(head_dim) ** (-0.5)
    has_prev = has_ref[0] > 0
    for at in range(sets):
        peak = jnp.full((1, width), masked_score, jnp.float32)
        for tile in range(tiles):
            scores = dot_nt(key_tile(kv_ref, tile, slice(0, head_dim)), qs_ref[first + at])
            s_ref[at, tile] = scores
            peak = jnp.maximum(peak, jnp.max(scores, axis=0, keepdims=True))
        m_prev_ref[at] = peak
    for at in range(sets):
        peak = m_prev_ref[at]
        total = jnp.zeros((1, width), jnp.float32)
        out = jnp.zeros((head_dim, width), jnp.float32)
        for tile in range(tiles):
            raised = jnp.exp2((s_ref[at, tile] - peak) * exponent_scale)
            total += jnp.sum(raised, axis=0, keepdims=True)
            raised = raised.astype(jnp.bfloat16)
            p_ref[at, tile] = raised
            out += dot_tn(key_tile(kv_ref, tile, slice(head_dim, 2 * head_dim)), raised)
        peak = jnp.where(has_prev, peak, masked_score)
        m_prev_ref[at] = peak
        top = jnp.maximum(peak, m_own_ref[first + at])
        own_factor = jnp.exp2((m_own_ref[first + at] - top) * exponent_scale)
        prev_factor = jnp.where(has_prev, jnp.exp2((peak - top) * exponent_scale), 0.0)
        total = own_factor * l_own_ref[first + at] + prev_factor * total
        out = own_factor * o_own_ref[first + at] + prev_factor * out
        grad = dot_ref[first + at].astype(jnp.float32)
        stats_ref[0, at] = top
        stats_ref[1, at] = total
        stats_ref[2, at] = jnp.sum(grad * out, axis=0, keepdims=True)
        if first == 0:
            out_ref[at] = out
        else:
            share = jnp.where(total > 0, 1.0 / total, 0.0)
            out_ref[at] = (out * share).astype(jnp.bfloat16)


def prev_backward(first, has_ref, qs_ref, dot_ref, kv_ref, p_ref, m_own_ref, m_prev_ref, stats_ref, other_ref, *rest):
    if first == 0:
        terms_ref, dos_ref, shift_ref, dqt_ref, factor_ref, scaled_ref, lower_ref = rest
    else:
        before_ref, terms_ref, dos_ref, shift_ref, dqt_ref, scaled_ref, lower_ref = rest
    _, width, head_dim = qs_ref.shape
    sets, tiles = p_ref.shape[:2]
    span = 2 * block_rows
    per_tile = tile_keys // span
    scale = float(head_dim) ** (-0.5)
    exponent_scale = log2_e * scale
    has_prev = has_ref[0] > 0
    for at in range(sets):
        top = jnp.maximum(stats_ref[0, at], other_ref[0, at])
        here = jnp.exp2((stats_ref[0, at] - top) * exponent_scale)
        away = jnp.exp2((other_ref[0, at] - top) * exponent_scale)
        inverse = 1.0 / (here * stats_ref[1, at] + away * other_ref[1, at])
        delta = (here * stats_ref[2, at] + away * other_ref[2, at]) * inverse
        if first == 0:
            factor_ref[0, at] = here * inverse
            factor_ref[1, at] = away * other_ref[1, at] * inverse
        own_factor = jnp.exp2((m_own_ref[first + at] - top) * exponent_scale) * inverse
        prev_factor = jnp.exp2((m_prev_ref[at] - top) * exponent_scale) * inverse
        prev_factor = jnp.where(has_prev, prev_factor, 0.0)
        grad = dot_ref[first + at].astype(jnp.float32)
        dos_ref[at] = (grad * own_factor).astype(jnp.bfloat16)
        shift_ref[at] = delta * own_factor
        scaled_ref[at] = (grad * prev_factor).astype(jnp.bfloat16)
        lower_ref[at] = delta * prev_factor
    for tile in range(tiles):
        keys = key_tile(kv_ref, tile, slice(0, head_dim))
        values = key_tile(kv_ref, tile, slice(head_dim, 2 * head_dim))
        key_grad = jnp.zeros((tile_keys, head_dim), jnp.float32)
        value_grad = jnp.zeros((tile_keys, head_dim), jnp.float32)
        for at in range(sets):
            weights = p_ref[at, tile]
            value_grad += dot_nt(weights, scaled_ref[at])
            change = dot_nn(values, scaled_ref[at]) - lower_ref[at]
            change = (weights.astype(jnp.float32) * change).astype(jnp.bfloat16)
            key_grad += dot_nn(change, qs_ref[first + at])
            dqt = dot_tn(keys, change)
            dqt_ref[at] = dqt if tile == 0 else dqt_ref[at] + dqt
        key_grad = key_grad * scale
        if first == 0:
            rows = slice(tile * tile_keys, (tile + 1) * tile_keys)
            terms_ref[rows, :head_dim] = key_grad
            terms_ref[rows, head_dim:] = value_grad
        else:
            rows = slice(tile * tile_keys, (tile + 1) * tile_keys)
            key_grad = (key_grad + before_ref[rows, :head_dim]).astype(jnp.bfloat16)
            value_grad = (value_grad + before_ref[rows, head_dim:]).astype(jnp.bfloat16)
            for j in range(per_tile):
                rows = slice(j * span, (j + 1) * span)
                terms_ref[tile * per_tile + j, :, :head_dim] = key_grad[rows]
                terms_ref[tile * per_tile + j, :, head_dim:] = value_grad[rows]


def own_backward(
    allowed_ref, slots_ref, qs_ref, ks_ref, vs_ref, p_ref,
    dos_mine_ref, shift_mine_ref, dqt_mine_ref, dos_theirs_ref, shift_theirs_ref, dqt_theirs_ref,
    dq_ref, dq_partner_ref, terms_ref, acc_ref, dqa_ref,
):
    steps, _, width = p_ref.shape
    group, span, _ = terms_ref.shape
    head_dim = ks_ref.shape[1]
    blocks = 2 * group
    tiles = blocks * block_rows // tile_keys
    scale = float(head_dim) ** (-0.5)

    acc_ref[...] = jnp.zeros(acc_ref.shape, jnp.float32)
    dqa_ref[:2] = dqt_mine_ref[...]
    dqa_ref[2:] = dqt_theirs_ref[...]
    for step in range(steps):
        at, tile = own_tile(step, allowed_ref)
        start = pl.multiple_of(jnp.minimum(tile, tiles - 1) * tile_keys, tile_keys)
        window = pl.ds(start, tile_keys)
        weights = p_ref[step]
        dos_ref, shift_ref, first = (
            (dos_mine_ref, shift_mine_ref, 0) if step < 5 else (dos_theirs_ref, shift_theirs_ref, 2)
        )
        grad = dos_ref[at - first]
        acc_ref[window, head_dim:] += dot_nt(weights, grad)
        change = dot_nn(vs_ref[window, :], grad) - shift_ref[at - first]
        change = (weights.astype(jnp.float32) * change).astype(jnp.bfloat16)
        acc_ref[window, :head_dim] += dot_nn(change, qs_ref[at]) * scale
        dqa_ref[at] += dot_tn(ks_ref[window, :], change)
    for g in range(group):
        slot = slots_ref[g]
        for half, place in ((0, slot), (1, blocks - 1 - slot)):
            source = pl.ds(pl.multiple_of(place * block_rows, block_rows), block_rows)
            terms_ref[g, half * block_rows : (half + 1) * block_rows, :] = acc_ref[
                source, :
            ].astype(jnp.bfloat16)
    for half in range(2):
        store_heads(dq_ref, half, dqa_ref[half].T * scale)
        store_heads(dq_partner_ref, half, dqa_ref[2 + half].T * scale)


def call(kernel, name, outs, in_smem, scratch, out_smem=(), flops=0, stream=()):
    vmem = pl.BlockSpec(memory_space=pltpu.VMEM)
    smem = pl.BlockSpec(memory_space=pltpu.SMEM)

    def spec(at, operand):
        if at in in_smem:
            return smem
        if at in stream:
            return pl.BlockSpec(operand.shape, lambda step: (0,) * operand.ndim)
        return vmem

    def run(*operands):
        return pl.pallas_call(
            kernel,
            name=name,
            grid=(1,) if stream else (),
            out_shape=[jax.ShapeDtypeStruct(shape, dtype) for shape, dtype in outs],
            in_specs=[spec(i, operand) for i, operand in enumerate(operands)],
            out_specs=[smem if i in out_smem else vmem for i in range(len(outs))],
            scratch_shapes=[pltpu.VMEM(shape, dtype) for shape, dtype in scratch],
            compiler_params=pltpu.CompilerParams(vmem_limit_bytes=16 * 1024 * 1024),
            cost_estimate=pl.CostEstimate(flops=flops, bytes_accessed=4 << 20, transcendentals=0),
        )(*operands)

    return run


def body(queries, key_vectors, value_vectors, grad_output, positions):
    tok_rows, full_width = queries.shape
    head_dim = key_vectors.shape[1]
    heads = full_width // head_dim
    group = lax.axis_size("inner") // 2
    segment = 2 * group * tok_rows
    span_rows = group * tok_rows
    width = heads * block_rows
    steps = 10
    bf16, f32 = jnp.bfloat16, jnp.float32
    query_partner = to_partner(queries, "inner")
    grad_partner = to_partner(grad_output, "inner")
    position_partner = to_partner(positions, "inner")
    (packed,) = call(
        pack,
        "pack",
        [((group, tok_rows + tag_rows, 2 * head_dim), bf16)],
        (0,),
        [],
        stream=(1, 2),
    )(positions, key_vectors, value_vectors)
    group_kv = exchange(packed, "inner")
    prev_kv = from_behind(group_kv, "outer", 1)
    has_prev = (lax.axis_index("outer") > 0).astype(jnp.int32).reshape(1)

    unit = 2 * tile_keys * width * head_dim
    row_stat = ((4, 1, width), f32)
    by_query = ((4, head_dim, width), f32)
    by_query_16 = ((4, head_dim, width), bf16)
    tokens = ((tok_rows, full_width), bf16)
    terms_shape = ((group, tok_rows, 2 * head_dim), bf16)
    tiles = span_rows // tile_keys
    both_blocks, qs, dot = call(
        functools.partial(stack_pair, segment),
        "stack_pair",
        [((2,), jnp.int32), ((4, width, head_dim), bf16), by_query_16],
        (0, 1),
        [],
        out_smem=(0,),
        flops=4 * 10**9,
        stream=(2, 4),
    )(positions, position_partner, queries, query_partner, grad_output, grad_partner)
    ks, vs, slots, allowed, p_own, m_own, l_own, o_own = call(
        own_forward,
        "own_forward",
        [
            ((span_rows, head_dim), bf16),
            ((span_rows, head_dim), bf16),
            ((group,), jnp.int32),
            ((4,), jnp.int32),
            ((steps, tile_keys, width), bf16),
            row_stat,
            row_stat,
            by_query,
        ],
        (0,),
        [((steps, tile_keys, width), f32)],
        out_smem=(2, 3),
        flops=2 * steps * unit,
    )(both_blocks, qs, group_kv)
    half_stat = ((2, 1, width), f32)
    half_query = ((2, head_dim, width), f32)
    half_query_16 = ((2, head_dim, width), bf16)

    def forward(first, name):
        return call(
            functools.partial(prev_forward, first),
            name,
            [
                ((2, tiles, tile_keys, width), bf16),
                half_stat,
                ((3, 2, 1, width), f32),
                half_query if first == 0 else half_query_16,
            ],
            (0,),
            [((2, tiles, tile_keys, width), f32)],
            flops=2 * 2 * tiles * unit,
        )(has_prev, qs, dot, prev_kv, m_own, l_own, o_own)

    p_theirs, m_theirs, stats_theirs, sent = forward(2, "prev_forward_theirs")
    other_mine = to_partner(stats_theirs, "inner")
    got = to_partner(sent, "inner")
    p_mine, m_mine, stats_mine, out = forward(0, "prev_forward_mine")
    other_theirs = to_partner(stats_mine, "inner")
    first_terms, dos_mine, shift_mine, dqt_mine, factor = call(
        functools.partial(prev_backward, 0),
        "prev_backward_mine",
        [((span_rows, 2 * head_dim), f32), half_query_16, half_stat, half_query, ((2, 2, 1, width), f32)],
        (0,),
        [half_query_16, half_stat],
        flops=4 * 2 * tiles * unit,
    )(has_prev, qs, dot, prev_kv, p_mine, m_own, m_mine, stats_mine, other_mine)
    prev_terms, dos_theirs, shift_theirs, dqt_theirs = call(
        functools.partial(prev_backward, 2),
        "prev_backward_theirs",
        [terms_shape, half_query_16, half_stat, half_query],
        (0,),
        [half_query_16, half_stat],
        flops=4 * 2 * tiles * unit,
    )(has_prev, qs, dot, prev_kv, p_theirs, m_own, m_theirs, stats_theirs, other_theirs, first_terms)
    returned = from_behind(prev_terms, "outer", -1)
    dq, dq_partner, own_terms = call(
        own_backward,
        "own_backward",
        [((tok_rows, full_width), f32), tokens, terms_shape],
        (0, 1),
        [((span_rows, 2 * head_dim), f32), by_query],
        flops=4 * steps * unit,
    )(allowed, slots, qs, ks, vs, p_own, dos_mine, shift_mine, dqt_mine, dos_theirs, shift_theirs, dqt_theirs)
    (attended,) = call(merge_attended, "merge_attended", [tokens], (), [])(out, got, factor)
    dq_other = to_partner(dq_partner, "inner")
    terms = (own_terms.astype(f32) + returned.astype(f32)).astype(bf16)
    key_grads = jnp.sum(exchange(terms, "inner").astype(f32), axis=0)
    grad_queries = (dq + dq_other.astype(f32)).astype(bf16)
    grad_keys = key_grads[:, :head_dim].astype(bf16)
    grad_values = key_grads[:, head_dim:].astype(bf16)
    return (attended, grad_queries, grad_keys, grad_values)


def solution(mesh):
    rows = P(("outer", "inner"), None)
    return jax.shard_map(
        body,
        mesh=mesh,
        in_specs=(rows, rows, rows, rows, P(("outer", "inner"))),
        out_specs=(rows, rows, rows, rows),
        check_vma=False,
    )
```

```python
import functools

import jax
import jax.numpy as jnp
from jax import lax
from jax.experimental import pallas as pl
from jax.experimental.pallas import tpu as pltpu
from jax.sharding import PartitionSpec as P

masked_score = -1e30
tile_keys = 256
log2_e = 1.4426950408889634
block_rows = 64
tag_rows = 16


def from_behind(block, axis, distance):
    devices = range(lax.axis_size(axis))
    route = [(i - distance, i) for i in devices if i - distance in devices]
    return lax.ppermute(block, axis, route)


def to_partner(block, axis):
    return lax.ppermute(block, axis, [(i, i ^ 1) for i in range(lax.axis_size(axis))])


def exchange(parts, axis):
    count = lax.axis_size(axis)
    groups = [list(range(first, count, 2)) for first in range(2)]
    return lax.all_to_all(parts, axis, 0, 0, axis_index_groups=groups, tiled=True)


def dot_nn(a, b):
    return lax.dot_general(a, b, (((1,), (0,)), ((), ())), preferred_element_type=jnp.float32)


def dot_nt(a, b):
    return lax.dot_general(a, b, (((1,), (1,)), ((), ())), preferred_element_type=jnp.float32)


def dot_tn(a, b):
    return lax.dot_general(a, b, (((0,), (0,)), ((), ())), preferred_element_type=jnp.float32)


def stack_heads(source, half, heads, head_dim):
    rows = slice(half * block_rows, (half + 1) * block_rows)
    return jnp.concatenate(
        [source[rows, h * head_dim : (h + 1) * head_dim] for h in range(heads)], axis=0
    )


def store_heads(target_ref, half, block):
    rows = slice(half * block_rows, (half + 1) * block_rows)
    head_dim = block.shape[1]
    for h in range(block.shape[0] // block_rows):
        target_ref[rows, h * head_dim : (h + 1) * head_dim] = block[
            h * block_rows : (h + 1) * block_rows
        ].astype(target_ref.dtype)


def pack(position_ref, key_ref, value_ref, packed_ref, place_ref, block_ref, in_sems, out_sems):
    count, rows, both = packed_ref.shape
    span = key_ref.shape[0]
    loads = [
        pltpu.make_async_copy(position_ref, place_ref, in_sems.at[0]),
        pltpu.make_async_copy(key_ref, block_ref.at[pl.ds(0, span), pl.ds(0, both // 2)], in_sems.at[1]),
        pltpu.make_async_copy(
            value_ref, block_ref.at[pl.ds(0, span), pl.ds(both // 2, both // 2)], in_sems.at[2]
        ),
    ]
    for load in loads:
        load.start()
    loads[0].wait()
    tag = (lax.rem(place_ref[0], 2 * count * span) // block_rows).astype(jnp.float32)
    block_ref[span:, :] = jnp.full((rows - span, both), tag, jnp.float32).astype(packed_ref.dtype)
    loads[1].wait()
    loads[2].wait()
    stores = [
        pltpu.make_async_copy(block_ref, packed_ref.at[g], out_sems.at[g]) for g in range(count)
    ]
    for store in stores:
        store.start()
    for store in stores:
        store.wait()


def stack_pair(
    segment, position_ref, position_partner_ref, q_ref, q_partner_ref, do_ref, do_partner_ref,
    block_ref, qs_ref, dot_ref,
):
    _, width, head_dim = qs_ref.shape
    heads = width // block_rows
    block_ref[0] = lax.rem(position_ref[0], segment) // block_rows
    block_ref[1] = lax.rem(position_partner_ref[0], segment) // block_rows
    for j, (query, grad) in enumerate(((q_ref, do_ref), (q_partner_ref, do_partner_ref))):
        for half in range(2):
            qs_ref[2 * j + half] = stack_heads(query, half, heads, head_dim)
            stacked = stack_heads(grad, half, heads, head_dim).astype(jnp.float32)
            dot_ref[2 * j + half] = stacked.T.astype(jnp.bfloat16)


def merge_attended(out_ref, got_ref, factor_ref, att_ref):
    for half in range(2):
        out = factor_ref[0, half] * out_ref[half]
        out = out + factor_ref[1, half] * got_ref[half].astype(jnp.float32)
        store_heads(att_ref, half, out.T)


def own_tile(step, allowed_ref):
    low = 0 if step < 5 else 2
    local = step % 5
    per_tile = tile_keys // block_rows
    low_tiles = (allowed_ref[low] + per_tile - 1) // per_tile
    high = jnp.where(local >= low_tiles, 1, 0)
    tile = local - high * low_tiles
    return low + high, tile


def own_forward(
    block_ref, qs_ref, kv_ref,
    ks_ref, vs_ref, slots_ref, allowed_ref, p_ref, m_ref, l_ref, o_ref, s_ref,
):
    group, _, both = kv_ref.shape
    head_dim = both // 2
    span = 2 * block_rows
    steps, _, width = p_ref.shape
    blocks = 2 * group
    tiles = blocks * block_rows // tile_keys
    exponent_scale = log2_e * float(head_dim) ** (-0.5)
    tags = [jnp.max(kv_ref[g, span:, :].astype(jnp.float32)).astype(jnp.int32) for g in range(group)]

    def count(test):
        return sum(jnp.where(test(tag), 1, 0) for tag in tags)

    for j in range(2):
        mine = block_ref[j]
        allowed_ref[2 * j] = count(lambda tag: tag <= mine)
        allowed_ref[2 * j + 1] = blocks - count(lambda tag: tag < mine)
    for g in range(group):
        slot = count(lambda tag: tag < tags[g])
        slots_ref[g] = slot
        for half, place in ((0, slot), (1, blocks - 1 - slot)):
            target = pl.ds(pl.multiple_of(place * block_rows, block_rows), block_rows)
            rows = slice(half * block_rows, (half + 1) * block_rows)
            ks_ref[target, :] = kv_ref[g, rows, :head_dim]
            vs_ref[target, :] = kv_ref[g, rows, head_dim:]
    m_ref[...] = jnp.full(m_ref.shape, masked_score, jnp.float32)
    l_ref[...] = jnp.zeros(l_ref.shape, jnp.float32)
    o_ref[...] = jnp.zeros(o_ref.shape, jnp.float32)
    key_row = lax.broadcasted_iota(jnp.int32, (tile_keys, width), 0)
    query_row = lax.rem(lax.broadcasted_iota(jnp.int32, (1, width), 1), block_rows)
    for step in range(steps):
        at, tile = own_tile(step, allowed_ref)
        start = pl.multiple_of(jnp.minimum(tile, tiles - 1) * tile_keys, tile_keys)
        scores = dot_nt(ks_ref[pl.ds(start, tile_keys), :], qs_ref[at])
        last = query_row if step < 5 else block_rows - 1
        limit = (allowed_ref[at] - 1) * block_rows + last - tile * tile_keys
        scores = jnp.where(key_row <= limit, scores, masked_score)
        s_ref[step] = scores
        m_ref[at] = jnp.maximum(m_ref[at], jnp.max(scores, axis=0, keepdims=True))
    for step in range(steps):
        at, tile = own_tile(step, allowed_ref)
        start = pl.multiple_of(jnp.minimum(tile, tiles - 1) * tile_keys, tile_keys)
        raised = jnp.exp2((s_ref[step] - m_ref[at]) * exponent_scale)
        l_ref[at] += jnp.sum(raised, axis=0, keepdims=True)
        raised = raised.astype(jnp.bfloat16)
        p_ref[step] = raised
        o_ref[at] += dot_tn(vs_ref[pl.ds(start, tile_keys), :], raised)


def key_tile(ref, tile, columns):
    per_tile = tile_keys // (2 * block_rows)
    return jnp.concatenate(
        [ref[tile * per_tile + j, : 2 * block_rows, columns] for j in range(per_tile)], axis=0
    )


def prev_forward(
    first, has_ref, qs_ref, dot_ref, kv_ref, m_own_ref, l_own_ref, o_own_ref,
    p_ref, m_prev_ref, stats_ref, out_ref, s_ref,
):
    _, width, head_dim = qs_ref.shape
    sets, tiles = p_ref.shape[:2]
    exponent_scale = log2_e * float(head_dim) ** (-0.5)
    has_prev = has_ref[0] > 0
    for at in range(sets):
        peak = jnp.full((1, width), masked_score, jnp.float32)
        for tile in range(tiles):
            scores = dot_nt(key_tile(kv_ref, tile, slice(0, head_dim)), qs_ref[first + at])
            s_ref[at, tile] = scores
            peak = jnp.maximum(peak, jnp.max(scores, axis=0, keepdims=True))
        m_prev_ref[at] = peak
    for at in range(sets):
        peak = m_prev_ref[at]
        total = jnp.zeros((1, width), jnp.float32)
        out = jnp.zeros((head_dim, width), jnp.float32)
        for tile in range(tiles):
            raised = jnp.exp2((s_ref[at, tile] - peak) * exponent_scale)
            total += jnp.sum(raised, axis=0, keepdims=True)
            raised = raised.astype(jnp.bfloat16)
            p_ref[at, tile] = raised
            out += dot_tn(key_tile(kv_ref, tile, slice(head_dim, 2 * head_dim)), raised)
        peak = jnp.where(has_prev, peak, masked_score)
        m_prev_ref[at] = peak
        top = jnp.maximum(peak, m_own_ref[first + at])
        own_factor = jnp.exp2((m_own_ref[first + at] - top) * exponent_scale)
        prev_factor = jnp.where(has_prev, jnp.exp2((peak - top) * exponent_scale), 0.0)
        total = own_factor * l_own_ref[first + at] + prev_factor * total
        out = own_factor * o_own_ref[first + at] + prev_factor * out
        grad = dot_ref[first + at].astype(jnp.float32)
        stats_ref[0, at] = top
        stats_ref[1, at] = total
        stats_ref[2, at] = jnp.sum(grad * out, axis=0, keepdims=True)
        if first == 0:
            out_ref[at] = out
        else:
            share = jnp.where(total > 0, 1.0 / total, 0.0)
            out_ref[at] = (out * share).astype(jnp.bfloat16)


def prev_backward(first, has_ref, qs_ref, dot_ref, kv_ref, p_ref, m_own_ref, m_prev_ref, stats_ref, other_ref, *rest):
    if first == 0:
        terms_ref, dos_ref, shift_ref, dqt_ref, factor_ref, scaled_ref, lower_ref = rest
    else:
        before_ref, terms_ref, dos_ref, shift_ref, dqt_ref, scaled_ref, lower_ref = rest
    _, width, head_dim = qs_ref.shape
    sets, tiles = p_ref.shape[:2]
    span = 2 * block_rows
    per_tile = tile_keys // span
    scale = float(head_dim) ** (-0.5)
    exponent_scale = log2_e * scale
    has_prev = has_ref[0] > 0
    for at in range(sets):
        top = jnp.maximum(stats_ref[0, at], other_ref[0, at])
        here = jnp.exp2((stats_ref[0, at] - top) * exponent_scale)
        away = jnp.exp2((other_ref[0, at] - top) * exponent_scale)
        inverse = 1.0 / (here * stats_ref[1, at] + away * other_ref[1, at])
        delta = (here * stats_ref[2, at] + away * other_ref[2, at]) * inverse
        if first == 0:
            factor_ref[0, at] = here * inverse
            factor_ref[1, at] = away * other_ref[1, at] * inverse
        own_factor = jnp.exp2((m_own_ref[first + at] - top) * exponent_scale) * inverse
        prev_factor = jnp.exp2((m_prev_ref[at] - top) * exponent_scale) * inverse
        prev_factor = jnp.where(has_prev, prev_factor, 0.0)
        grad = dot_ref[first + at].astype(jnp.float32)
        dos_ref[at] = (grad * own_factor).astype(jnp.bfloat16)
        shift_ref[at] = delta * own_factor
        scaled_ref[at] = (grad * prev_factor).astype(jnp.bfloat16)
        lower_ref[at] = delta * prev_factor
    for tile in range(tiles):
        keys = key_tile(kv_ref, tile, slice(0, head_dim))
        values = key_tile(kv_ref, tile, slice(head_dim, 2 * head_dim))
        key_grad = jnp.zeros((tile_keys, head_dim), jnp.float32)
        value_grad = jnp.zeros((tile_keys, head_dim), jnp.float32)
        for at in range(sets):
            weights = p_ref[at, tile]
            value_grad += dot_nt(weights, scaled_ref[at])
            change = dot_nn(values, scaled_ref[at]) - lower_ref[at]
            change = (weights.astype(jnp.float32) * change).astype(jnp.bfloat16)
            key_grad += dot_nn(change, qs_ref[first + at])
            dqt = dot_tn(keys, change)
            dqt_ref[at] = dqt if tile == 0 else dqt_ref[at] + dqt
        key_grad = key_grad * scale
        if first == 0:
            rows = slice(tile * tile_keys, (tile + 1) * tile_keys)
            terms_ref[rows, :head_dim] = key_grad
            terms_ref[rows, head_dim:] = value_grad
        else:
            rows = slice(tile * tile_keys, (tile + 1) * tile_keys)
            key_grad = (key_grad + before_ref[rows, :head_dim]).astype(jnp.bfloat16)
            value_grad = (value_grad + before_ref[rows, head_dim:]).astype(jnp.bfloat16)
            for j in range(per_tile):
                rows = slice(j * span, (j + 1) * span)
                terms_ref[tile * per_tile + j, :, :head_dim] = key_grad[rows]
                terms_ref[tile * per_tile + j, :, head_dim:] = value_grad[rows]


def own_backward(
    allowed_ref, slots_ref, qs_ref, ks_ref, vs_ref, p_ref,
    dos_mine_ref, shift_mine_ref, dqt_mine_ref, dos_theirs_ref, shift_theirs_ref, dqt_theirs_ref,
    dq_ref, dq_partner_ref, terms_ref, acc_ref, dqa_ref,
):
    steps, _, width = p_ref.shape
    group, span, _ = terms_ref.shape
    head_dim = ks_ref.shape[1]
    blocks = 2 * group
    tiles = blocks * block_rows // tile_keys
    scale = float(head_dim) ** (-0.5)

    acc_ref[...] = jnp.zeros(acc_ref.shape, jnp.float32)
    dqa_ref[:2] = dqt_mine_ref[...]
    dqa_ref[2:] = dqt_theirs_ref[...]
    for step in range(steps):
        at, tile = own_tile(step, allowed_ref)
        start = pl.multiple_of(jnp.minimum(tile, tiles - 1) * tile_keys, tile_keys)
        window = pl.ds(start, tile_keys)
        weights = p_ref[step]
        dos_ref, shift_ref, first = (
            (dos_mine_ref, shift_mine_ref, 0) if step < 5 else (dos_theirs_ref, shift_theirs_ref, 2)
        )
        grad = dos_ref[at - first]
        acc_ref[window, head_dim:] += dot_nt(weights, grad)
        change = dot_nn(vs_ref[window, :], grad) - shift_ref[at - first]
        change = (weights.astype(jnp.float32) * change).astype(jnp.bfloat16)
        acc_ref[window, :head_dim] += dot_nn(change, qs_ref[at]) * scale
        dqa_ref[at] += dot_tn(ks_ref[window, :], change)
    for g in range(group):
        slot = slots_ref[g]
        for half, place in ((0, slot), (1, blocks - 1 - slot)):
            source = pl.ds(pl.multiple_of(place * block_rows, block_rows), block_rows)
            terms_ref[g, half * block_rows : (half + 1) * block_rows, :] = acc_ref[
                source, :
            ].astype(jnp.bfloat16)
    for half in range(2):
        store_heads(dq_ref, half, dqa_ref[half].T * scale)
        store_heads(dq_partner_ref, half, dqa_ref[2 + half].T * scale)


def call(kernel, name, outs, in_smem, scratch, out_smem=(), flops=0, stream=()):
    vmem = pl.BlockSpec(memory_space=pltpu.VMEM)
    smem = pl.BlockSpec(memory_space=pltpu.SMEM)

    def spec(at, operand):
        if at in in_smem:
            return smem
        if at in stream:
            return pl.BlockSpec(operand.shape, lambda step: (0,) * operand.ndim)
        return vmem

    def run(*operands):
        return pl.pallas_call(
            kernel,
            name=name,
            grid=(1,) if stream else (),
            out_shape=[jax.ShapeDtypeStruct(shape, dtype) for shape, dtype in outs],
            in_specs=[spec(i, operand) for i, operand in enumerate(operands)],
            out_specs=[smem if i in out_smem else vmem for i in range(len(outs))],
            scratch_shapes=[pltpu.VMEM(shape, dtype) for shape, dtype in scratch],
            compiler_params=pltpu.CompilerParams(vmem_limit_bytes=16 * 1024 * 1024),
            cost_estimate=pl.CostEstimate(flops=flops, bytes_accessed=4 << 20, transcendentals=0),
        )(*operands)

    return run


def body(queries, key_vectors, value_vectors, grad_output, positions):
    tok_rows, full_width = queries.shape
    head_dim = key_vectors.shape[1]
    heads = full_width // head_dim
    group = lax.axis_size("inner") // 2
    segment = 2 * group * tok_rows
    span_rows = group * tok_rows
    width = heads * block_rows
    steps = 10
    bf16, f32 = jnp.bfloat16, jnp.float32
    query_partner = to_partner(queries, "inner")
    grad_partner = to_partner(grad_output, "inner")
    position_partner = to_partner(positions, "inner")
    anywhere = pl.BlockSpec(memory_space=pl.ANY)
    packed = pl.pallas_call(
        pack,
        name="pack",
        out_shape=jax.ShapeDtypeStruct((group, tok_rows + tag_rows, 2 * head_dim), bf16),
        in_specs=[anywhere] * 3,
        out_specs=anywhere,
        scratch_shapes=[
            pltpu.SMEM(positions.shape, jnp.int32),
            pltpu.VMEM((tok_rows + tag_rows, 2 * head_dim), bf16),
            pltpu.SemaphoreType.DMA((3,)),
            pltpu.SemaphoreType.DMA((group,)),
        ],
        compiler_params=pltpu.CompilerParams(vmem_limit_bytes=60 * 1024 * 1024),
    )(positions, key_vectors, value_vectors)
    group_kv = exchange(packed, "inner")
    has_prev = (lax.axis_index("outer") > 0).astype(jnp.int32).reshape(1)

    unit = 2 * tile_keys * width * head_dim
    row_stat = ((4, 1, width), f32)
    by_query = ((4, head_dim, width), f32)
    by_query_16 = ((4, head_dim, width), bf16)
    tokens = ((tok_rows, full_width), bf16)
    terms_shape = ((group, tok_rows, 2 * head_dim), bf16)
    tiles = span_rows // tile_keys
    both_blocks, qs, dot = call(
        functools.partial(stack_pair, segment),
        "stack_pair",
        [((2,), jnp.int32), ((4, width, head_dim), bf16), by_query_16],
        (0, 1),
        [],
        out_smem=(0,),
        flops=4 * 10**9,
        stream=(2, 4),
    )(positions, position_partner, queries, query_partner, grad_output, grad_partner)
    group_kv, qs, dot, both_blocks = lax.optimization_barrier((group_kv, qs, dot, both_blocks))
    prev_kv = from_behind(group_kv, "outer", 1)
    ks, vs, slots, allowed, p_own, m_own, l_own, o_own = call(
        own_forward,
        "own_forward",
        [
            ((span_rows, head_dim), bf16),
            ((span_rows, head_dim), bf16),
            ((group,), jnp.int32),
            ((4,), jnp.int32),
            ((steps, tile_keys, width), bf16),
            row_stat,
            row_stat,
            by_query,
        ],
        (0,),
        [((steps, tile_keys, width), f32)],
        out_smem=(2, 3),
        flops=2 * steps * unit,
    )(both_blocks, qs, group_kv)
    half_stat = ((2, 1, width), f32)
    half_query = ((2, head_dim, width), f32)
    half_query_16 = ((2, head_dim, width), bf16)

    def forward(first, name):
        return call(
            functools.partial(prev_forward, first),
            name,
            [
                ((2, tiles, tile_keys, width), bf16),
                half_stat,
                ((3, 2, 1, width), f32),
                half_query if first == 0 else half_query_16,
            ],
            (0,),
            [((2, tiles, tile_keys, width), f32)],
            flops=2 * 2 * tiles * unit,
        )(has_prev, qs, dot, prev_kv, m_own, l_own, o_own)

    p_theirs, m_theirs, stats_theirs, sent = forward(2, "prev_forward_theirs")
    other_mine = to_partner(stats_theirs, "inner")
    got = to_partner(sent, "inner")
    p_mine, m_mine, stats_mine, out = forward(0, "prev_forward_mine")
    other_theirs = to_partner(stats_mine, "inner")
    first_terms, dos_mine, shift_mine, dqt_mine, factor = call(
        functools.partial(prev_backward, 0),
        "prev_backward_mine",
        [((span_rows, 2 * head_dim), f32), half_query_16, half_stat, half_query, ((2, 2, 1, width), f32)],
        (0,),
        [half_query_16, half_stat],
        flops=4 * 2 * tiles * unit,
    )(has_prev, qs, dot, prev_kv, p_mine, m_own, m_mine, stats_mine, other_mine)
    first_terms, got = lax.optimization_barrier((first_terms, got))
    prev_terms, dos_theirs, shift_theirs, dqt_theirs = call(
        functools.partial(prev_backward, 2),
        "prev_backward_theirs",
        [terms_shape, half_query_16, half_stat, half_query],
        (0,),
        [half_query_16, half_stat],
        flops=4 * 2 * tiles * unit,
    )(has_prev, qs, dot, prev_kv, p_theirs, m_own, m_theirs, stats_theirs, other_theirs, first_terms)
    returned = from_behind(prev_terms, "outer", -1)
    dq, dq_partner, own_terms = call(
        own_backward,
        "own_backward",
        [((tok_rows, full_width), f32), tokens, terms_shape],
        (0, 1),
        [((span_rows, 2 * head_dim), f32), by_query],
        flops=4 * steps * unit,
    )(allowed, slots, qs, ks, vs, p_own, dos_mine, shift_mine, dqt_mine, dos_theirs, shift_theirs, dqt_theirs)
    (attended,) = call(merge_attended, "merge_attended", [tokens], (), [])(out, got, factor)
    dq_other = to_partner(dq_partner, "inner")
    terms = (own_terms.astype(f32) + returned.astype(f32)).astype(bf16)
    key_grads = jnp.sum(exchange(terms, "inner").astype(f32), axis=0)
    grad_queries = (dq + dq_other.astype(f32)).astype(bf16)
    grad_keys = key_grads[:, :head_dim].astype(bf16)
    grad_values = key_grads[:, head_dim:].astype(bf16)
    return (attended, grad_queries, grad_keys, grad_values)


def solution(mesh):
    rows = P(("outer", "inner"), None)
    return jax.shard_map(
        body,
        mesh=mesh,
        in_specs=(rows, rows, rows, rows, P(("outer", "inner"))),
        out_specs=(rows, rows, rows, rows),
        check_vma=False,
    )
```

```python
import functools

import jax
import jax.numpy as jnp
from jax import lax
from jax.experimental import pallas as pl
from jax.experimental.pallas import tpu as pltpu
from jax.sharding import PartitionSpec as P

masked_score = -1e30
tile_keys = 256
log2_e = 1.4426950408889634
block_rows = 64
tag_rows = 16


def from_behind(block, axis, distance):
    devices = range(lax.axis_size(axis))
    route = [(i - distance, i) for i in devices if i - distance in devices]
    return lax.ppermute(block, axis, route)


def to_partner(block, axis):
    return lax.ppermute(block, axis, [(i, i ^ 1) for i in range(lax.axis_size(axis))])


def exchange(parts, axis):
    count = lax.axis_size(axis)
    groups = [list(range(first, count, 2)) for first in range(2)]
    return lax.all_to_all(parts, axis, 0, 0, axis_index_groups=groups, tiled=True)


def dot_nn(a, b):
    return lax.dot_general(a, b, (((1,), (0,)), ((), ())), preferred_element_type=jnp.float32)


def dot_nt(a, b):
    return lax.dot_general(a, b, (((1,), (1,)), ((), ())), preferred_element_type=jnp.float32)


def dot_tn(a, b):
    return lax.dot_general(a, b, (((0,), (0,)), ((), ())), preferred_element_type=jnp.float32)


def stack_heads(source, half, heads, head_dim):
    rows = slice(half * block_rows, (half + 1) * block_rows)
    return jnp.concatenate(
        [source[rows, h * head_dim : (h + 1) * head_dim] for h in range(heads)], axis=0
    )


def store_heads(target_ref, half, block):
    rows = slice(half * block_rows, (half + 1) * block_rows)
    head_dim = block.shape[1]
    for h in range(block.shape[0] // block_rows):
        target_ref[rows, h * head_dim : (h + 1) * head_dim] = block[
            h * block_rows : (h + 1) * block_rows
        ].astype(target_ref.dtype)


def pack(position_ref, key_ref, value_ref, packed_ref, place_ref, block_ref, in_sems, out_sems):
    count, rows, head_dim = packed_ref.shape
    span = key_ref.shape[0]
    loads = [
        pltpu.make_async_copy(position_ref, place_ref, in_sems.at[0]),
        pltpu.make_async_copy(key_ref, block_ref.at[pl.ds(0, span)], in_sems.at[1]),
        pltpu.make_async_copy(value_ref, block_ref.at[pl.ds(span, span)], in_sems.at[2]),
    ]
    for load in loads:
        load.start()
    loads[0].wait()
    tag = (lax.rem(place_ref[0], 2 * count * span) // block_rows).astype(jnp.float32)
    tag = jnp.full((rows - 2 * span, head_dim), tag, jnp.float32)
    block_ref[2 * span :, :] = tag.astype(packed_ref.dtype)
    loads[1].wait()
    loads[2].wait()
    stores = [
        pltpu.make_async_copy(block_ref, packed_ref.at[g], out_sems.at[g]) for g in range(count)
    ]
    for store in stores:
        store.start()
    for store in stores:
        store.wait()


def stack_pair(
    segment, position_ref, position_partner_ref, q_ref, q_partner_ref, do_ref, do_partner_ref,
    block_ref, qs_ref, dot_ref,
):
    _, width, head_dim = qs_ref.shape
    heads = width // block_rows
    block_ref[0] = lax.rem(position_ref[0], segment) // block_rows
    block_ref[1] = lax.rem(position_partner_ref[0], segment) // block_rows
    for j, (query, grad) in enumerate(((q_ref, do_ref), (q_partner_ref, do_partner_ref))):
        for half in range(2):
            qs_ref[2 * j + half] = stack_heads(query, half, heads, head_dim)
            stacked = stack_heads(grad, half, heads, head_dim).astype(jnp.float32)
            dot_ref[2 * j + half] = stacked.T.astype(jnp.bfloat16)


def merge_attended(out_ref, got_ref, factor_ref, att_ref):
    for half in range(2):
        out = factor_ref[0, half] * out_ref[half]
        out = out + factor_ref[1, half] * got_ref[half].astype(jnp.float32)
        store_heads(att_ref, half, out.T)


def own_tile(step, allowed_ref):
    low = 0 if step < 5 else 2
    local = step % 5
    per_tile = tile_keys // block_rows
    low_tiles = (allowed_ref[low] + per_tile - 1) // per_tile
    high = jnp.where(local >= low_tiles, 1, 0)
    tile = local - high * low_tiles
    return low + high, tile


def own_forward(
    block_ref, qs_ref, kv_ref,
    ks_ref, vs_ref, slots_ref, allowed_ref, p_ref, m_ref, l_ref, o_ref, s_ref,
):
    group, _, head_dim = kv_ref.shape
    span = 2 * block_rows
    steps, _, width = p_ref.shape
    blocks = 2 * group
    tiles = blocks * block_rows // tile_keys
    exponent_scale = log2_e * float(head_dim) ** (-0.5)
    tags = [jnp.max(kv_ref[g, 2 * span :, :].astype(jnp.float32)).astype(jnp.int32) for g in range(group)]

    def count(test):
        return sum(jnp.where(test(tag), 1, 0) for tag in tags)

    for j in range(2):
        mine = block_ref[j]
        allowed_ref[2 * j] = count(lambda tag: tag <= mine)
        allowed_ref[2 * j + 1] = blocks - count(lambda tag: tag < mine)
    for g in range(group):
        slot = count(lambda tag: tag < tags[g])
        slots_ref[g] = slot
        for half, place in ((0, slot), (1, blocks - 1 - slot)):
            target = pl.ds(pl.multiple_of(place * block_rows, block_rows), block_rows)
            rows = slice(half * block_rows, (half + 1) * block_rows)
            ks_ref[target, :] = kv_ref[g, rows, :]
            rows = slice(span + half * block_rows, span + (half + 1) * block_rows)
            vs_ref[target, :] = kv_ref[g, rows, :]
    m_ref[...] = jnp.full(m_ref.shape, masked_score, jnp.float32)
    l_ref[...] = jnp.zeros(l_ref.shape, jnp.float32)
    o_ref[...] = jnp.zeros(o_ref.shape, jnp.float32)
    key_row = lax.broadcasted_iota(jnp.int32, (tile_keys, width), 0)
    query_row = lax.rem(lax.broadcasted_iota(jnp.int32, (1, width), 1), block_rows)
    for step in range(steps):
        at, tile = own_tile(step, allowed_ref)
        start = pl.multiple_of(jnp.minimum(tile, tiles - 1) * tile_keys, tile_keys)
        scores = dot_nt(ks_ref[pl.ds(start, tile_keys), :], qs_ref[at])
        last = query_row if step < 5 else block_rows - 1
        limit = (allowed_ref[at] - 1) * block_rows + last - tile * tile_keys
        scores = jnp.where(key_row <= limit, scores, masked_score)
        s_ref[step] = scores
        m_ref[at] = jnp.maximum(m_ref[at], jnp.max(scores, axis=0, keepdims=True))
    for step in range(steps):
        at, tile = own_tile(step, allowed_ref)
        start = pl.multiple_of(jnp.minimum(tile, tiles - 1) * tile_keys, tile_keys)
        raised = jnp.exp2((s_ref[step] - m_ref[at]) * exponent_scale)
        l_ref[at] += jnp.sum(raised, axis=0, keepdims=True)
        raised = raised.astype(jnp.bfloat16)
        p_ref[step] = raised
        o_ref[at] += dot_tn(vs_ref[pl.ds(start, tile_keys), :], raised)


def key_tile(ref, tile, part):
    span = 2 * block_rows
    per_tile = tile_keys // span
    return jnp.concatenate(
        [ref[tile * per_tile + j, part * span : (part + 1) * span, :] for j in range(per_tile)],
        axis=0,
    )


def prev_forward(
    first, has_ref, qs_ref, dot_ref, kv_ref, m_own_ref, l_own_ref, o_own_ref,
    p_ref, m_prev_ref, stats_ref, out_ref, s_ref,
):
    _, width, head_dim = qs_ref.shape
    sets, tiles = p_ref.shape[:2]
    exponent_scale = log2_e * float(head_dim) ** (-0.5)
    has_prev = has_ref[0] > 0
    for at in range(sets):
        peak = jnp.full((1, width), masked_score, jnp.float32)
        for tile in range(tiles):
            scores = dot_nt(key_tile(kv_ref, tile, 0), qs_ref[first + at])
            s_ref[at, tile] = scores
            peak = jnp.maximum(peak, jnp.max(scores, axis=0, keepdims=True))
        m_prev_ref[at] = peak
    for at in range(sets):
        peak = m_prev_ref[at]
        total = jnp.zeros((1, width), jnp.float32)
        out = jnp.zeros((head_dim, width), jnp.float32)
        for tile in range(tiles):
            raised = jnp.exp2((s_ref[at, tile] - peak) * exponent_scale)
            total += jnp.sum(raised, axis=0, keepdims=True)
            raised = raised.astype(jnp.bfloat16)
            p_ref[at, tile] = raised
            out += dot_tn(key_tile(kv_ref, tile, 1), raised)
        peak = jnp.where(has_prev, peak, masked_score)
        m_prev_ref[at] = peak
        top = jnp.maximum(peak, m_own_ref[first + at])
        own_factor = jnp.exp2((m_own_ref[first + at] - top) * exponent_scale)
        prev_factor = jnp.where(has_prev, jnp.exp2((peak - top) * exponent_scale), 0.0)
        total = own_factor * l_own_ref[first + at] + prev_factor * total
        out = own_factor * o_own_ref[first + at] + prev_factor * out
        grad = dot_ref[first + at].astype(jnp.float32)
        stats_ref[0, at] = top
        stats_ref[1, at] = total
        stats_ref[2, at] = jnp.sum(grad * out, axis=0, keepdims=True)
        if first == 0:
            out_ref[at] = out
        else:
            share = jnp.where(total > 0, 1.0 / total, 0.0)
            out_ref[at] = (out * share).astype(jnp.bfloat16)


def prev_backward(first, has_ref, qs_ref, dot_ref, kv_ref, p_ref, m_own_ref, m_prev_ref, stats_ref, other_ref, *rest):
    if first == 0:
        terms_ref, dos_ref, shift_ref, ds_ref, factor_ref, scaled_ref, lower_ref = rest
    else:
        before_ref, terms_ref, dos_ref, shift_ref, ds_ref, scaled_ref, lower_ref = rest
    _, width, head_dim = qs_ref.shape
    sets, tiles = p_ref.shape[:2]
    span = 2 * block_rows
    per_tile = tile_keys // span
    scale = float(head_dim) ** (-0.5)
    exponent_scale = log2_e * scale
    has_prev = has_ref[0] > 0
    for at in range(sets):
        top = jnp.maximum(stats_ref[0, at], other_ref[0, at])
        here = jnp.exp2((stats_ref[0, at] - top) * exponent_scale)
        away = jnp.exp2((other_ref[0, at] - top) * exponent_scale)
        inverse = 1.0 / (here * stats_ref[1, at] + away * other_ref[1, at])
        delta = (here * stats_ref[2, at] + away * other_ref[2, at]) * inverse
        if first == 0:
            factor_ref[0, at] = here * inverse
            factor_ref[1, at] = away * other_ref[1, at] * inverse
        own_factor = jnp.exp2((m_own_ref[first + at] - top) * exponent_scale) * inverse
        prev_factor = jnp.exp2((m_prev_ref[at] - top) * exponent_scale) * inverse
        prev_factor = jnp.where(has_prev, prev_factor, 0.0)
        grad = dot_ref[first + at].astype(jnp.float32)
        dos_ref[at] = (grad * own_factor).astype(jnp.bfloat16)
        shift_ref[at] = delta * own_factor
        scaled_ref[at] = (grad * prev_factor).astype(jnp.bfloat16)
        lower_ref[at] = delta * prev_factor
    for tile in range(tiles):
        values = key_tile(kv_ref, tile, 1)
        key_grad = jnp.zeros((tile_keys, head_dim), jnp.float32)
        value_grad = jnp.zeros((tile_keys, head_dim), jnp.float32)
        for at in range(sets):
            weights = p_ref[at, tile]
            value_grad += dot_nt(weights, scaled_ref[at])
            change = dot_nn(values, scaled_ref[at]) - lower_ref[at]
            change = (weights.astype(jnp.float32) * change).astype(jnp.bfloat16)
            key_grad += dot_nn(change, qs_ref[first + at])
            ds_ref[at, tile] = change
        key_grad = key_grad * scale
        if first == 0:
            rows = slice(tile * tile_keys, (tile + 1) * tile_keys)
            terms_ref[rows, :head_dim] = key_grad
            terms_ref[rows, head_dim:] = value_grad
        else:
            rows = slice(tile * tile_keys, (tile + 1) * tile_keys)
            key_grad = (key_grad + before_ref[rows, :head_dim]).astype(jnp.bfloat16)
            value_grad = (value_grad + before_ref[rows, head_dim:]).astype(jnp.bfloat16)
            for j in range(per_tile):
                rows = slice(j * span, (j + 1) * span)
                terms_ref[tile * per_tile + j, :, :head_dim] = key_grad[rows]
                terms_ref[tile * per_tile + j, :, head_dim:] = value_grad[rows]


def own_backward(
    allowed_ref, slots_ref, qs_ref, ks_ref, vs_ref, p_ref,
    dos_mine_ref, shift_mine_ref, ds_mine_ref, dos_theirs_ref, shift_theirs_ref, ds_theirs_ref, kv_ref,
    dq_ref, dq_partner_ref, terms_ref, acc_ref, dqa_ref,
):
    steps, _, width = p_ref.shape
    group, span, _ = terms_ref.shape
    head_dim = ks_ref.shape[1]
    blocks = 2 * group
    tiles = blocks * block_rows // tile_keys
    scale = float(head_dim) ** (-0.5)

    acc_ref[...] = jnp.zeros(acc_ref.shape, jnp.float32)
    for at in range(4):
        changes = (ds_mine_ref, ds_theirs_ref)[at // 2]
        dqa_ref[at] = sum(
            dot_tn(key_tile(kv_ref, tile, 0), changes[at % 2, tile]) for tile in range(tiles)
        )
    for step in range(steps):
        at, tile = own_tile(step, allowed_ref)
        start = pl.multiple_of(jnp.minimum(tile, tiles - 1) * tile_keys, tile_keys)
        window = pl.ds(start, tile_keys)
        weights = p_ref[step]
        dos_ref, shift_ref, first = (
            (dos_mine_ref, shift_mine_ref, 0) if step < 5 else (dos_theirs_ref, shift_theirs_ref, 2)
        )
        grad = dos_ref[at - first]
        acc_ref[window, head_dim:] += dot_nt(weights, grad)
        change = dot_nn(vs_ref[window, :], grad) - shift_ref[at - first]
        change = (weights.astype(jnp.float32) * change).astype(jnp.bfloat16)
        acc_ref[window, :head_dim] += dot_nn(change, qs_ref[at]) * scale
        dqa_ref[at] += dot_tn(ks_ref[window, :], change)
    for g in range(group):
        slot = slots_ref[g]
        for half, place in ((0, slot), (1, blocks - 1 - slot)):
            source = pl.ds(pl.multiple_of(place * block_rows, block_rows), block_rows)
            terms_ref[g, half * block_rows : (half + 1) * block_rows, :] = acc_ref[
                source, :
            ].astype(jnp.bfloat16)
    for half in range(2):
        store_heads(dq_ref, half, dqa_ref[half].T * scale)
        store_heads(dq_partner_ref, half, dqa_ref[2 + half].T * scale)


def call(kernel, name, outs, in_smem, scratch, out_smem=(), flops=0, stream=()):
    vmem = pl.BlockSpec(memory_space=pltpu.VMEM)
    smem = pl.BlockSpec(memory_space=pltpu.SMEM)

    def spec(at, operand):
        if at in in_smem:
            return smem
        if at in stream:
            return pl.BlockSpec(operand.shape, lambda step: (0,) * operand.ndim)
        return vmem

    def run(*operands):
        return pl.pallas_call(
            kernel,
            name=name,
            grid=(1,) if stream else (),
            out_shape=[jax.ShapeDtypeStruct(shape, dtype) for shape, dtype in outs],
            in_specs=[spec(i, operand) for i, operand in enumerate(operands)],
            out_specs=[smem if i in out_smem else vmem for i in range(len(outs))],
            scratch_shapes=[pltpu.VMEM(shape, dtype) for shape, dtype in scratch],
            compiler_params=pltpu.CompilerParams(vmem_limit_bytes=16 * 1024 * 1024),
            cost_estimate=pl.CostEstimate(flops=flops, bytes_accessed=4 << 20, transcendentals=0),
        )(*operands)

    return run


def body(queries, key_vectors, value_vectors, grad_output, positions):
    tok_rows, full_width = queries.shape
    head_dim = key_vectors.shape[1]
    heads = full_width // head_dim
    group = lax.axis_size("inner") // 2
    segment = 2 * group * tok_rows
    span_rows = group * tok_rows
    width = heads * block_rows
    steps = 10
    bf16, f32 = jnp.bfloat16, jnp.float32
    query_partner = to_partner(queries, "inner")
    grad_partner = to_partner(grad_output, "inner")
    position_partner = to_partner(positions, "inner")
    anywhere = pl.BlockSpec(memory_space=pl.ANY)
    packed = pl.pallas_call(
        pack,
        name="pack",
        out_shape=jax.ShapeDtypeStruct((group, 2 * tok_rows + tag_rows, head_dim), bf16),
        in_specs=[anywhere] * 3,
        out_specs=anywhere,
        scratch_shapes=[
            pltpu.SMEM(positions.shape, jnp.int32),
            pltpu.VMEM((2 * tok_rows + tag_rows, head_dim), bf16),
            pltpu.SemaphoreType.DMA((3,)),
            pltpu.SemaphoreType.DMA((group,)),
        ],
        compiler_params=pltpu.CompilerParams(vmem_limit_bytes=60 * 1024 * 1024),
    )(positions, key_vectors, value_vectors)
    group_kv = exchange(packed, "inner")
    has_prev = (lax.axis_index("outer") > 0).astype(jnp.int32).reshape(1)

    unit = 2 * tile_keys * width * head_dim
    row_stat = ((4, 1, width), f32)
    by_query = ((4, head_dim, width), f32)
    by_query_16 = ((4, head_dim, width), bf16)
    tokens = ((tok_rows, full_width), bf16)
    terms_shape = ((group, tok_rows, 2 * head_dim), bf16)
    tiles = span_rows // tile_keys
    both_blocks, qs, dot = call(
        functools.partial(stack_pair, segment),
        "stack_pair",
        [((2,), jnp.int32), ((4, width, head_dim), bf16), by_query_16],
        (0, 1),
        [],
        out_smem=(0,),
        flops=4 * 10**9,
        stream=(2, 4),
    )(positions, position_partner, queries, query_partner, grad_output, grad_partner)
    group_kv, qs, dot, both_blocks = lax.optimization_barrier((group_kv, qs, dot, both_blocks))
    prev_kv = from_behind(group_kv, "outer", 1)
    ks, vs, slots, allowed, p_own, m_own, l_own, o_own = call(
        own_forward,
        "own_forward",
        [
            ((span_rows, head_dim), bf16),
            ((span_rows, head_dim), bf16),
            ((group,), jnp.int32),
            ((4,), jnp.int32),
            ((steps, tile_keys, width), bf16),
            row_stat,
            row_stat,
            by_query,
        ],
        (0,),
        [((steps, tile_keys, width), f32)],
        out_smem=(2, 3),
        flops=2 * steps * unit,
    )(both_blocks, qs, group_kv)
    half_stat = ((2, 1, width), f32)
    half_query = ((2, head_dim, width), f32)
    changes = ((2, tiles, tile_keys, width), bf16)
    half_query_16 = ((2, head_dim, width), bf16)

    def forward(first, name):
        return call(
            functools.partial(prev_forward, first),
            name,
            [
                ((2, tiles, tile_keys, width), bf16),
                half_stat,
                ((3, 2, 1, width), f32),
                half_query if first == 0 else half_query_16,
            ],
            (0,),
            [((2, tiles, tile_keys, width), f32)],
            flops=2 * 2 * tiles * unit,
        )(has_prev, qs, dot, prev_kv, m_own, l_own, o_own)

    p_theirs, m_theirs, stats_theirs, sent = forward(2, "prev_forward_theirs")
    other_mine = to_partner(stats_theirs, "inner")
    got = to_partner(sent, "inner")
    p_mine, m_mine, stats_mine, out = forward(0, "prev_forward_mine")
    other_theirs = to_partner(stats_mine, "inner")
    first_terms, dos_mine, shift_mine, ds_mine, factor = call(
        functools.partial(prev_backward, 0),
        "prev_backward_mine",
        [((span_rows, 2 * head_dim), f32), half_query_16, half_stat, changes, ((2, 2, 1, width), f32)],
        (0,),
        [half_query_16, half_stat],
        flops=4 * 2 * tiles * unit,
    )(has_prev, qs, dot, prev_kv, p_mine, m_own, m_mine, stats_mine, other_mine)
    prev_terms, dos_theirs, shift_theirs, ds_theirs = call(
        functools.partial(prev_backward, 2),
        "prev_backward_theirs",
        [terms_shape, half_query_16, half_stat, changes],
        (0,),
        [half_query_16, half_stat],
        flops=4 * 2 * tiles * unit,
    )(has_prev, qs, dot, prev_kv, p_theirs, m_own, m_theirs, stats_theirs, other_theirs, first_terms)
    returned = from_behind(prev_terms, "outer", -1)
    dq, dq_partner, own_terms = call(
        own_backward,
        "own_backward",
        [((tok_rows, full_width), f32), tokens, terms_shape],
        (0, 1),
        [((span_rows, 2 * head_dim), f32), by_query],
        flops=4 * steps * unit,
    )(allowed, slots, qs, ks, vs, p_own, dos_mine, shift_mine, ds_mine, dos_theirs, shift_theirs, ds_theirs, prev_kv)
    (attended,) = call(merge_attended, "merge_attended", [tokens], (), [])(out, got, factor)
    dq_other = to_partner(dq_partner, "inner")
    terms = (own_terms.astype(f32) + returned.astype(f32)).astype(bf16)
    key_grads = jnp.sum(exchange(terms, "inner").astype(f32), axis=0)
    grad_queries = (dq + dq_other.astype(f32)).astype(bf16)
    grad_keys = key_grads[:, :head_dim].astype(bf16)
    grad_values = key_grads[:, head_dim:].astype(bf16)
    return (attended, grad_queries, grad_keys, grad_values)


def solution(mesh):
    rows = P(("outer", "inner"), None)
    return jax.shard_map(
        body,
        mesh=mesh,
        in_specs=(rows, rows, rows, rows, P(("outer", "inner"))),
        out_specs=(rows, rows, rows, rows),
        check_vma=False,
    )
```

```python
import functools

import jax
import jax.numpy as jnp
from jax import lax
from jax.experimental import pallas as pl
from jax.experimental.pallas import tpu as pltpu
from jax.sharding import PartitionSpec as P

masked_score = -1e30
tile_keys = 256
log2_e = 1.4426950408889634
block_rows = 64
tag_rows = 16


def from_behind(block, axis, distance):
    devices = range(lax.axis_size(axis))
    route = [(i - distance, i) for i in devices if i - distance in devices]
    return lax.ppermute(block, axis, route)


def to_partner(block, axis):
    return lax.ppermute(block, axis, [(i, i ^ 1) for i in range(lax.axis_size(axis))])


def exchange(parts, axis):
    count = lax.axis_size(axis)
    groups = [list(range(first, count, 2)) for first in range(2)]
    return lax.all_to_all(parts, axis, 0, 0, axis_index_groups=groups, tiled=True)


def dot_nn(a, b):
    return lax.dot_general(a, b, (((1,), (0,)), ((), ())), preferred_element_type=jnp.float32)


def dot_nt(a, b):
    return lax.dot_general(a, b, (((1,), (1,)), ((), ())), preferred_element_type=jnp.float32)


def dot_tn(a, b):
    return lax.dot_general(a, b, (((0,), (0,)), ((), ())), preferred_element_type=jnp.float32)


def stack_heads(source, half, heads, head_dim):
    rows = slice(half * block_rows, (half + 1) * block_rows)
    return jnp.concatenate(
        [source[rows, h * head_dim : (h + 1) * head_dim] for h in range(heads)], axis=0
    )


def store_heads(target_ref, half, block):
    rows = slice(half * block_rows, (half + 1) * block_rows)
    head_dim = block.shape[1]
    for h in range(block.shape[0] // block_rows):
        target_ref[rows, h * head_dim : (h + 1) * head_dim] = block[
            h * block_rows : (h + 1) * block_rows
        ].astype(target_ref.dtype)


def pack(position_ref, key_ref, value_ref, packed_ref, place_ref, block_ref, in_sems, out_sems):
    count, rows, head_dim = packed_ref.shape
    span = key_ref.shape[0]
    loads = [
        pltpu.make_async_copy(position_ref, place_ref, in_sems.at[0]),
        pltpu.make_async_copy(key_ref, block_ref.at[pl.ds(0, span)], in_sems.at[1]),
        pltpu.make_async_copy(value_ref, block_ref.at[pl.ds(span, span)], in_sems.at[2]),
    ]
    for load in loads:
        load.start()
    loads[0].wait()
    tag = (lax.rem(place_ref[0], 2 * count * span) // block_rows).astype(jnp.float32)
    tag = jnp.full((rows - 2 * span, head_dim), tag, jnp.float32)
    block_ref[2 * span :, :] = tag.astype(packed_ref.dtype)
    loads[1].wait()
    loads[2].wait()
    stores = [
        pltpu.make_async_copy(block_ref, packed_ref.at[g], out_sems.at[g]) for g in range(count)
    ]
    for store in stores:
        store.start()
    for store in stores:
        store.wait()


def stack_pair(
    segment, position_ref, position_partner_ref, q_ref, q_partner_ref, do_ref, do_partner_ref,
    block_ref, qs_ref, dot_ref,
):
    _, width, head_dim = qs_ref.shape
    heads = width // block_rows
    block_ref[0] = lax.rem(position_ref[0], segment) // block_rows
    block_ref[1] = lax.rem(position_partner_ref[0], segment) // block_rows
    for j, (query, grad) in enumerate(((q_ref, do_ref), (q_partner_ref, do_partner_ref))):
        for half in range(2):
            qs_ref[2 * j + half] = stack_heads(query, half, heads, head_dim)
            stacked = stack_heads(grad, half, heads, head_dim).astype(jnp.float32)
            dot_ref[2 * j + half] = stacked.T.astype(jnp.bfloat16)


def merge_attended(out_ref, got_ref, factor_ref, att_ref):
    for half in range(2):
        out = factor_ref[0, half] * out_ref[half]
        out = out + factor_ref[1, half] * got_ref[half].astype(jnp.float32)
        store_heads(att_ref, half, out.T)


def own_tile(step, allowed_ref):
    low = 0 if step < 5 else 2
    local = step % 5
    per_tile = tile_keys // block_rows
    low_tiles = (allowed_ref[low] + per_tile - 1) // per_tile
    high = jnp.where(local >= low_tiles, 1, 0)
    tile = local - high * low_tiles
    return low + high, tile


def own_forward(
    block_ref, qs_ref, kv_ref,
    ks_ref, vs_ref, slots_ref, allowed_ref, p_ref, m_ref, l_ref, o_ref, s_ref,
):
    group, _, head_dim = kv_ref.shape
    span = 2 * block_rows
    steps, _, width = p_ref.shape
    blocks = 2 * group
    tiles = blocks * block_rows // tile_keys
    exponent_scale = log2_e * float(head_dim) ** (-0.5)
    tags = [jnp.max(kv_ref[g, 2 * span :, :].astype(jnp.float32)).astype(jnp.int32) for g in range(group)]

    def count(test):
        return sum(jnp.where(test(tag), 1, 0) for tag in tags)

    for j in range(2):
        mine = block_ref[j]
        allowed_ref[2 * j] = count(lambda tag: tag <= mine)
        allowed_ref[2 * j + 1] = blocks - count(lambda tag: tag < mine)
    for g in range(group):
        slot = count(lambda tag: tag < tags[g])
        slots_ref[g] = slot
        for half, place in ((0, slot), (1, blocks - 1 - slot)):
            target = pl.ds(pl.multiple_of(place * block_rows, block_rows), block_rows)
            rows = slice(half * block_rows, (half + 1) * block_rows)
            ks_ref[target, :] = kv_ref[g, rows, :]
            rows = slice(span + half * block_rows, span + (half + 1) * block_rows)
            vs_ref[target, :] = kv_ref[g, rows, :]
    m_ref[...] = jnp.full(m_ref.shape, masked_score, jnp.float32)
    l_ref[...] = jnp.zeros(l_ref.shape, jnp.float32)
    o_ref[...] = jnp.zeros(o_ref.shape, jnp.float32)
    key_row = lax.broadcasted_iota(jnp.int32, (tile_keys, width), 0)
    query_row = lax.rem(lax.broadcasted_iota(jnp.int32, (1, width), 1), block_rows)
    for step in range(steps):
        at, tile = own_tile(step, allowed_ref)
        start = pl.multiple_of(jnp.minimum(tile, tiles - 1) * tile_keys, tile_keys)
        scores = dot_nt(ks_ref[pl.ds(start, tile_keys), :], qs_ref[at])
        last = query_row if step < 5 else block_rows - 1
        limit = (allowed_ref[at] - 1) * block_rows + last - tile * tile_keys
        scores = jnp.where(key_row <= limit, scores, masked_score)
        s_ref[step] = scores
        m_ref[at] = jnp.maximum(m_ref[at], jnp.max(scores, axis=0, keepdims=True))
    for step in range(steps):
        at, tile = own_tile(step, allowed_ref)
        start = pl.multiple_of(jnp.minimum(tile, tiles - 1) * tile_keys, tile_keys)
        raised = jnp.exp2((s_ref[step] - m_ref[at]) * exponent_scale)
        l_ref[at] += jnp.sum(raised, axis=0, keepdims=True)
        raised = raised.astype(jnp.bfloat16)
        p_ref[step] = raised
        o_ref[at] += dot_tn(vs_ref[pl.ds(start, tile_keys), :], raised)


def key_tile(ref, tile, part):
    span = 2 * block_rows
    per_tile = tile_keys // span
    return jnp.concatenate(
        [ref[tile * per_tile + j, part * span : (part + 1) * span, :] for j in range(per_tile)],
        axis=0,
    )


def prev_forward(
    first, has_ref, qs_ref, dot_ref, kv_ref, m_own_ref, l_own_ref, o_own_ref,
    p_ref, m_prev_ref, stats_ref, out_ref, s_ref,
):
    _, width, head_dim = qs_ref.shape
    sets, tiles = p_ref.shape[:2]
    exponent_scale = log2_e * float(head_dim) ** (-0.5)
    has_prev = has_ref[0] > 0
    for at in range(sets):
        peak = jnp.full((1, width), masked_score, jnp.float32)
        for tile in range(tiles):
            scores = dot_nt(key_tile(kv_ref, tile, 0), qs_ref[first + at])
            s_ref[at, tile] = scores
            peak = jnp.maximum(peak, jnp.max(scores, axis=0, keepdims=True))
        m_prev_ref[at] = peak
    for at in range(sets):
        peak = m_prev_ref[at]
        total = jnp.zeros((1, width), jnp.float32)
        out = jnp.zeros((head_dim, width), jnp.float32)
        for tile in range(tiles):
            raised = jnp.exp2((s_ref[at, tile] - peak) * exponent_scale)
            total += jnp.sum(raised, axis=0, keepdims=True)
            raised = raised.astype(jnp.bfloat16)
            p_ref[at, tile] = raised
            out += dot_tn(key_tile(kv_ref, tile, 1), raised)
        peak = jnp.where(has_prev, peak, masked_score)
        m_prev_ref[at] = peak
        top = jnp.maximum(peak, m_own_ref[first + at])
        own_factor = jnp.exp2((m_own_ref[first + at] - top) * exponent_scale)
        prev_factor = jnp.where(has_prev, jnp.exp2((peak - top) * exponent_scale), 0.0)
        total = own_factor * l_own_ref[first + at] + prev_factor * total
        out = own_factor * o_own_ref[first + at] + prev_factor * out
        grad = dot_ref[first + at].astype(jnp.float32)
        stats_ref[0, at] = top
        stats_ref[1, at] = total
        stats_ref[2, at] = jnp.sum(grad * out, axis=0, keepdims=True)
        if first == 0:
            out_ref[at] = out
        else:
            share = jnp.where(total > 0, 1.0 / total, 0.0)
            out_ref[at] = (out * share).astype(jnp.bfloat16)


def prev_backward(first, has_ref, qs_ref, dot_ref, kv_ref, p_ref, m_own_ref, m_prev_ref, stats_ref, other_ref, *rest):
    if first == 0:
        terms_ref, dos_ref, shift_ref, ds_ref, factor_ref, scaled_ref, lower_ref = rest
    else:
        before_ref, terms_ref, dos_ref, shift_ref, ds_ref, scaled_ref, lower_ref = rest
    _, width, head_dim = qs_ref.shape
    sets, tiles = p_ref.shape[:2]
    span = 2 * block_rows
    per_tile = tile_keys // span
    scale = float(head_dim) ** (-0.5)
    exponent_scale = log2_e * scale
    has_prev = has_ref[0] > 0
    for at in range(sets):
        top = jnp.maximum(stats_ref[0, at], other_ref[0, at])
        here = jnp.exp2((stats_ref[0, at] - top) * exponent_scale)
        away = jnp.exp2((other_ref[0, at] - top) * exponent_scale)
        inverse = 1.0 / (here * stats_ref[1, at] + away * other_ref[1, at])
        delta = (here * stats_ref[2, at] + away * other_ref[2, at]) * inverse
        if first == 0:
            factor_ref[0, at] = here * inverse
            factor_ref[1, at] = away * other_ref[1, at] * inverse
        own_factor = jnp.exp2((m_own_ref[first + at] - top) * exponent_scale) * inverse
        prev_factor = jnp.exp2((m_prev_ref[at] - top) * exponent_scale) * inverse
        prev_factor = jnp.where(has_prev, prev_factor, 0.0)
        grad = dot_ref[first + at].astype(jnp.float32)
        dos_ref[at] = (grad * own_factor).astype(jnp.bfloat16)
        shift_ref[at] = delta * own_factor
        scaled_ref[at] = (grad * prev_factor).astype(jnp.bfloat16)
        lower_ref[at] = delta * prev_factor
    for tile in range(tiles):
        values = key_tile(kv_ref, tile, 1)
        key_grad = jnp.zeros((tile_keys, head_dim), jnp.float32)
        value_grad = jnp.zeros((tile_keys, head_dim), jnp.float32)
        for at in range(sets):
            weights = p_ref[at, tile]
            value_grad += dot_nt(weights, scaled_ref[at])
            change = dot_nn(values, scaled_ref[at]) - lower_ref[at]
            change = (weights.astype(jnp.float32) * change).astype(jnp.bfloat16)
            key_grad += dot_nn(change, qs_ref[first + at])
            ds_ref[at, tile] = change
        key_grad = key_grad * scale
        if first == 0:
            rows = slice(tile * tile_keys, (tile + 1) * tile_keys)
            terms_ref[rows, :head_dim] = key_grad
            terms_ref[rows, head_dim:] = value_grad
        else:
            rows = slice(tile * tile_keys, (tile + 1) * tile_keys)
            key_grad = (key_grad + before_ref[rows, :head_dim]).astype(jnp.bfloat16)
            value_grad = (value_grad + before_ref[rows, head_dim:]).astype(jnp.bfloat16)
            for j in range(per_tile):
                rows = slice(j * span, (j + 1) * span)
                terms_ref[tile * per_tile + j, :, :head_dim] = key_grad[rows]
                terms_ref[tile * per_tile + j, :, head_dim:] = value_grad[rows]


def own_backward(
    allowed_ref, slots_ref, qs_ref, ks_ref, vs_ref, p_ref,
    dos_mine_ref, shift_mine_ref, ds_mine_ref, dos_theirs_ref, shift_theirs_ref, ds_theirs_ref, kv_ref,
    dq_ref, dq_partner_ref, terms_ref, acc_ref, dqa_ref,
):
    steps, _, width = p_ref.shape
    group, span, _ = terms_ref.shape
    head_dim = ks_ref.shape[1]
    blocks = 2 * group
    tiles = blocks * block_rows // tile_keys
    scale = float(head_dim) ** (-0.5)

    acc_ref[...] = jnp.zeros(acc_ref.shape, jnp.float32)
    for at in range(4):
        changes = (ds_mine_ref, ds_theirs_ref)[at // 2]
        dqa_ref[at] = sum(
            dot_tn(key_tile(kv_ref, tile, 0), changes[at % 2, tile]) for tile in range(tiles)
        )
    for step in range(steps):
        at, tile = own_tile(step, allowed_ref)
        start = pl.multiple_of(jnp.minimum(tile, tiles - 1) * tile_keys, tile_keys)
        window = pl.ds(start, tile_keys)
        weights = p_ref[step]
        dos_ref, shift_ref, first = (
            (dos_mine_ref, shift_mine_ref, 0) if step < 5 else (dos_theirs_ref, shift_theirs_ref, 2)
        )
        grad = dos_ref[at - first]
        acc_ref[window, head_dim:] += dot_nt(weights, grad)
        change = dot_nn(vs_ref[window, :], grad) - shift_ref[at - first]
        change = (weights.astype(jnp.float32) * change).astype(jnp.bfloat16)
        acc_ref[window, :head_dim] += dot_nn(change, qs_ref[at]) * scale
        dqa_ref[at] += dot_tn(ks_ref[window, :], change)
    for g in range(group):
        slot = slots_ref[g]
        for half, place in ((0, slot), (1, blocks - 1 - slot)):
            source = pl.ds(pl.multiple_of(place * block_rows, block_rows), block_rows)
            terms_ref[g, half * block_rows : (half + 1) * block_rows, :] = acc_ref[
                source, :
            ].astype(jnp.bfloat16)
    for half in range(2):
        store_heads(dq_ref, half, dqa_ref[half].T * scale)
        store_heads(dq_partner_ref, half, dqa_ref[2 + half].T * scale)


def call(kernel, name, outs, in_smem, scratch, out_smem=(), flops=0, stream=()):
    vmem = pl.BlockSpec(memory_space=pltpu.VMEM)
    smem = pl.BlockSpec(memory_space=pltpu.SMEM)

    def spec(at, operand):
        if at in in_smem:
            return smem
        if at in stream:
            return pl.BlockSpec(operand.shape, lambda step: (0,) * operand.ndim)
        return vmem

    def run(*operands):
        return pl.pallas_call(
            kernel,
            name=name,
            grid=(1,) if stream else (),
            out_shape=[jax.ShapeDtypeStruct(shape, dtype) for shape, dtype in outs],
            in_specs=[spec(i, operand) for i, operand in enumerate(operands)],
            out_specs=[smem if i in out_smem else vmem for i in range(len(outs))],
            scratch_shapes=[pltpu.VMEM(shape, dtype) for shape, dtype in scratch],
            compiler_params=pltpu.CompilerParams(vmem_limit_bytes=16 * 1024 * 1024),
            cost_estimate=pl.CostEstimate(flops=flops, bytes_accessed=4 << 20, transcendentals=0),
        )(*operands)

    return run


def body(queries, key_vectors, value_vectors, grad_output, positions):
    tok_rows, full_width = queries.shape
    head_dim = key_vectors.shape[1]
    heads = full_width // head_dim
    group = lax.axis_size("inner") // 2
    segment = 2 * group * tok_rows
    span_rows = group * tok_rows
    width = heads * block_rows
    steps = 10
    bf16, f32 = jnp.bfloat16, jnp.float32
    query_partner = to_partner(queries, "inner")
    grad_partner = to_partner(grad_output, "inner")
    position_partner = to_partner(positions, "inner")
    anywhere = pl.BlockSpec(memory_space=pl.ANY)
    packed = pl.pallas_call(
        pack,
        name="pack",
        out_shape=jax.ShapeDtypeStruct((group, 2 * tok_rows + tag_rows, head_dim), bf16),
        in_specs=[anywhere] * 3,
        out_specs=anywhere,
        scratch_shapes=[
            pltpu.SMEM(positions.shape, jnp.int32),
            pltpu.VMEM((2 * tok_rows + tag_rows, head_dim), bf16),
            pltpu.SemaphoreType.DMA((3,)),
            pltpu.SemaphoreType.DMA((group,)),
        ],
        compiler_params=pltpu.CompilerParams(vmem_limit_bytes=60 * 1024 * 1024),
    )(positions, key_vectors, value_vectors)
    group_kv = exchange(packed, "inner")
    has_prev = (lax.axis_index("outer") > 0).astype(jnp.int32).reshape(1)

    unit = 2 * tile_keys * width * head_dim
    row_stat = ((4, 1, width), f32)
    by_query = ((4, head_dim, width), f32)
    by_query_16 = ((4, head_dim, width), bf16)
    tokens = ((tok_rows, full_width), bf16)
    terms_shape = ((group, tok_rows, 2 * head_dim), bf16)
    tiles = span_rows // tile_keys
    both_blocks, qs, dot = call(
        functools.partial(stack_pair, segment),
        "stack_pair",
        [((2,), jnp.int32), ((4, width, head_dim), bf16), by_query_16],
        (0, 1),
        [],
        out_smem=(0,),
        flops=4 * 10**9,
        stream=(2, 4),
    )(positions, position_partner, queries, query_partner, grad_output, grad_partner)
    group_kv, qs, dot, both_blocks = lax.optimization_barrier((group_kv, qs, dot, both_blocks))
    prev_kv = from_behind(group_kv, "outer", 1)
    ks, vs, slots, allowed, p_own, m_own, l_own, o_own = call(
        own_forward,
        "own_forward",
        [
            ((span_rows, head_dim), bf16),
            ((span_rows, head_dim), bf16),
            ((group,), jnp.int32),
            ((4,), jnp.int32),
            ((steps, tile_keys, width), bf16),
            row_stat,
            row_stat,
            by_query,
        ],
        (0,),
        [((steps, tile_keys, width), f32)],
        out_smem=(2, 3),
        flops=2 * steps * unit,
    )(both_blocks, qs, group_kv)
    half_stat = ((2, 1, width), f32)
    half_query = ((2, head_dim, width), f32)
    changes = ((2, tiles, tile_keys, width), bf16)
    half_query_16 = ((2, head_dim, width), bf16)

    def forward(first, name):
        return call(
            functools.partial(prev_forward, first),
            name,
            [
                ((2, tiles, tile_keys, width), bf16),
                half_stat,
                ((3, 2, 1, width), f32),
                half_query if first == 0 else half_query_16,
            ],
            (0,),
            [((2, tiles, tile_keys, width), f32)],
            flops=2 * 2 * tiles * unit,
        )(has_prev, qs, dot, prev_kv, m_own, l_own, o_own)

    p_theirs, m_theirs, stats_theirs, sent = forward(2, "prev_forward_theirs")
    other_mine = to_partner(stats_theirs, "inner")
    got = to_partner(sent, "inner")
    p_mine, m_mine, stats_mine, out = forward(0, "prev_forward_mine")
    other_theirs = to_partner(stats_mine, "inner")
    first_terms, dos_mine, shift_mine, ds_mine, factor = call(
        functools.partial(prev_backward, 0),
        "prev_backward_mine",
        [((span_rows, 2 * head_dim), f32), half_query_16, half_stat, changes, ((2, 2, 1, width), f32)],
        (0,),
        [half_query_16, half_stat],
        flops=4 * 2 * tiles * unit,
    )(has_prev, qs, dot, prev_kv, p_mine, m_own, m_mine, stats_mine, other_mine)
    prev_terms, dos_theirs, shift_theirs, ds_theirs = call(
        functools.partial(prev_backward, 2),
        "prev_backward_theirs",
        [terms_shape, half_query_16, half_stat, changes],
        (0,),
        [half_query_16, half_stat],
        flops=4 * 2 * tiles * unit,
    )(has_prev, qs, dot, prev_kv, p_theirs, m_own, m_theirs, stats_theirs, other_theirs, first_terms)
    returned = from_behind(prev_terms, "outer", -1)
    dq, dq_partner, own_terms = call(
        own_backward,
        "own_backward",
        [((tok_rows, full_width), f32), tokens, terms_shape],
        (0, 1),
        [((span_rows, 2 * head_dim), f32), by_query],
        flops=4 * steps * unit,
    )(allowed, slots, qs, ks, vs, p_own, dos_mine, shift_mine, ds_mine, dos_theirs, shift_theirs, ds_theirs, prev_kv)
    own_terms, got, dq_partner = lax.optimization_barrier((own_terms, got, dq_partner))
    terms = (own_terms.astype(f32) + returned.astype(f32)).astype(bf16)
    (attended,) = call(merge_attended, "merge_attended", [tokens], (), [])(out, got, factor)
    dq_other = to_partner(dq_partner, "inner")
    key_grads = jnp.sum(exchange(terms, "inner").astype(f32), axis=0)
    grad_queries = (dq + dq_other.astype(f32)).astype(bf16)
    grad_keys = key_grads[:, :head_dim].astype(bf16)
    grad_values = key_grads[:, head_dim:].astype(bf16)
    return (attended, grad_queries, grad_keys, grad_values)


def solution(mesh):
    rows = P(("outer", "inner"), None)
    return jax.shard_map(
        body,
        mesh=mesh,
        in_specs=(rows, rows, rows, rows, P(("outer", "inner"))),
        out_specs=(rows, rows, rows, rows),
        check_vma=False,
    )
```

```python
import functools

import jax
import jax.numpy as jnp
from jax import lax
from jax.experimental import pallas as pl
from jax.experimental.pallas import tpu as pltpu
from jax.sharding import PartitionSpec as P

masked_score = -1e30
tile_keys = 256
log2_e = 1.4426950408889634
block_rows = 64
tag_rows = 16


def from_behind(block, axis, distance):
    devices = range(lax.axis_size(axis))
    route = [(i - distance, i) for i in devices if i - distance in devices]
    return lax.ppermute(block, axis, route)


def to_partner(block, axis):
    return lax.ppermute(block, axis, [(i, i ^ 1) for i in range(lax.axis_size(axis))])


def turn(block, axis, distance):
    count = lax.axis_size(axis)
    return lax.ppermute(block, axis, [(i, (i + 2 * distance) % count) for i in range(count)])


def exchange(parts, axis):
    count = lax.axis_size(axis)
    groups = [list(range(first, count, 2)) for first in range(2)]
    return lax.all_to_all(parts, axis, 0, 0, axis_index_groups=groups, tiled=True)


def dot_nn(a, b):
    return lax.dot_general(a, b, (((1,), (0,)), ((), ())), preferred_element_type=jnp.float32)


def dot_nt(a, b):
    return lax.dot_general(a, b, (((1,), (1,)), ((), ())), preferred_element_type=jnp.float32)


def dot_tn(a, b):
    return lax.dot_general(a, b, (((0,), (0,)), ((), ())), preferred_element_type=jnp.float32)


def stack_heads(source, half, heads, head_dim):
    rows = slice(half * block_rows, (half + 1) * block_rows)
    return jnp.concatenate(
        [source[rows, h * head_dim : (h + 1) * head_dim] for h in range(heads)], axis=0
    )


def store_heads(target_ref, half, block):
    rows = slice(half * block_rows, (half + 1) * block_rows)
    head_dim = block.shape[1]
    for h in range(block.shape[0] // block_rows):
        target_ref[rows, h * head_dim : (h + 1) * head_dim] = block[
            h * block_rows : (h + 1) * block_rows
        ].astype(target_ref.dtype)


def pack(segment, position_ref, key_ref, value_ref, packed_ref, place_ref, block_ref, in_sems, out_sem):
    rows, head_dim = packed_ref.shape
    span = key_ref.shape[0]
    loads = [
        pltpu.make_async_copy(position_ref, place_ref, in_sems.at[0]),
        pltpu.make_async_copy(key_ref, block_ref.at[pl.ds(0, span)], in_sems.at[1]),
        pltpu.make_async_copy(value_ref, block_ref.at[pl.ds(span, span)], in_sems.at[2]),
    ]
    for load in loads:
        load.start()
    loads[0].wait()
    tag = (lax.rem(place_ref[0], segment) // block_rows).astype(jnp.float32)
    tag = jnp.full((rows - 2 * span, head_dim), tag, jnp.float32)
    block_ref[2 * span :, :] = tag.astype(packed_ref.dtype)
    loads[1].wait()
    loads[2].wait()
    store = pltpu.make_async_copy(block_ref, packed_ref, out_sem.at[0])
    store.start()
    store.wait()


def stack_pair(
    segment, position_ref, position_partner_ref, q_ref, q_partner_ref, do_ref, do_partner_ref,
    block_ref, qs_ref, dot_ref,
):
    _, width, head_dim = qs_ref.shape
    heads = width // block_rows
    block_ref[0] = lax.rem(position_ref[0], segment) // block_rows
    block_ref[1] = lax.rem(position_partner_ref[0], segment) // block_rows
    for j, (query, grad) in enumerate(((q_ref, do_ref), (q_partner_ref, do_partner_ref))):
        for half in range(2):
            qs_ref[2 * j + half] = stack_heads(query, half, heads, head_dim)
            stacked = stack_heads(grad, half, heads, head_dim).astype(jnp.float32)
            dot_ref[2 * j + half] = stacked.T.astype(jnp.bfloat16)


def merge_attended(out_ref, got_ref, factor_ref, att_ref):
    for half in range(2):
        out = factor_ref[0, half] * out_ref[half]
        out = out + factor_ref[1, half] * got_ref[half].astype(jnp.float32)
        store_heads(att_ref, half, out.T)


def own_tile(step, allowed_ref):
    low = 0 if step < 5 else 2
    local = step % 5
    per_tile = tile_keys // block_rows
    low_tiles = (allowed_ref[low] + per_tile - 1) // per_tile
    high = jnp.where(local >= low_tiles, 1, 0)
    tile = local - high * low_tiles
    return low + high, tile


def own_forward(group, block_ref, qs_ref, *rest):
    kv, rest = rest[:group], rest[group:]
    ks_ref, vs_ref, slots_ref, allowed_ref, p_ref, m_ref, l_ref, o_ref, s_ref = rest
    head_dim = kv[0].shape[1]
    span = 2 * block_rows
    steps, _, width = p_ref.shape
    blocks = 2 * group
    tiles = blocks * block_rows // tile_keys
    exponent_scale = log2_e * float(head_dim) ** (-0.5)
    tags = [jnp.max(kv[g][2 * span :, :].astype(jnp.float32)).astype(jnp.int32) for g in range(group)]

    def count(test):
        return sum(jnp.where(test(tag), 1, 0) for tag in tags)

    for j in range(2):
        mine = block_ref[j]
        allowed_ref[2 * j] = count(lambda tag: tag <= mine)
        allowed_ref[2 * j + 1] = blocks - count(lambda tag: tag < mine)
    for g in range(group):
        slot = count(lambda tag: tag < tags[g])
        slots_ref[g] = slot
        for half, place in ((0, slot), (1, blocks - 1 - slot)):
            target = pl.ds(pl.multiple_of(place * block_rows, block_rows), block_rows)
            rows = slice(half * block_rows, (half + 1) * block_rows)
            ks_ref[target, :] = kv[g][rows, :]
            rows = slice(span + half * block_rows, span + (half + 1) * block_rows)
            vs_ref[target, :] = kv[g][rows, :]
    m_ref[...] = jnp.full(m_ref.shape, masked_score, jnp.float32)
    l_ref[...] = jnp.zeros(l_ref.shape, jnp.float32)
    o_ref[...] = jnp.zeros(o_ref.shape, jnp.float32)
    key_row = lax.broadcasted_iota(jnp.int32, (tile_keys, width), 0)
    query_row = lax.rem(lax.broadcasted_iota(jnp.int32, (1, width), 1), block_rows)
    for step in range(steps):
        at, tile = own_tile(step, allowed_ref)
        start = pl.multiple_of(jnp.minimum(tile, tiles - 1) * tile_keys, tile_keys)
        scores = dot_nt(ks_ref[pl.ds(start, tile_keys), :], qs_ref[at])
        last = query_row if step < 5 else block_rows - 1
        limit = (allowed_ref[at] - 1) * block_rows + last - tile * tile_keys
        scores = jnp.where(key_row <= limit, scores, masked_score)
        s_ref[step] = scores
        m_ref[at] = jnp.maximum(m_ref[at], jnp.max(scores, axis=0, keepdims=True))
    for step in range(steps):
        at, tile = own_tile(step, allowed_ref)
        start = pl.multiple_of(jnp.minimum(tile, tiles - 1) * tile_keys, tile_keys)
        raised = jnp.exp2((s_ref[step] - m_ref[at]) * exponent_scale)
        l_ref[at] += jnp.sum(raised, axis=0, keepdims=True)
        raised = raised.astype(jnp.bfloat16)
        p_ref[step] = raised
        o_ref[at] += dot_tn(vs_ref[pl.ds(start, tile_keys), :], raised)


def key_tile(kv, tile, part):
    span = 2 * block_rows
    per_tile = tile_keys // span
    return jnp.concatenate(
        [kv[tile * per_tile + j][part * span : (part + 1) * span, :] for j in range(per_tile)],
        axis=0,
    )


def prev_forward(first, group, has_ref, qs_ref, dot_ref, m_own_ref, l_own_ref, o_own_ref, *rest):
    kv, rest = rest[:group], rest[group:]
    p_ref, m_prev_ref, stats_ref, out_ref, s_ref = rest
    _, width, head_dim = qs_ref.shape
    sets, tiles = p_ref.shape[:2]
    exponent_scale = log2_e * float(head_dim) ** (-0.5)
    has_prev = has_ref[0] > 0
    for at in range(sets):
        peak = jnp.full((1, width), masked_score, jnp.float32)
        for tile in range(tiles):
            scores = dot_nt(key_tile(kv, tile, 0), qs_ref[first + at])
            s_ref[at, tile] = scores
            peak = jnp.maximum(peak, jnp.max(scores, axis=0, keepdims=True))
        m_prev_ref[at] = peak
    for at in range(sets):
        peak = m_prev_ref[at]
        total = jnp.zeros((1, width), jnp.float32)
        out = jnp.zeros((head_dim, width), jnp.float32)
        for tile in range(tiles):
            raised = jnp.exp2((s_ref[at, tile] - peak) * exponent_scale)
            total += jnp.sum(raised, axis=0, keepdims=True)
            raised = raised.astype(jnp.bfloat16)
            p_ref[at, tile] = raised
            out += dot_tn(key_tile(kv, tile, 1), raised)
        peak = jnp.where(has_prev, peak, masked_score)
        m_prev_ref[at] = peak
        top = jnp.maximum(peak, m_own_ref[first + at])
        own_factor = jnp.exp2((m_own_ref[first + at] - top) * exponent_scale)
        prev_factor = jnp.where(has_prev, jnp.exp2((peak - top) * exponent_scale), 0.0)
        total = own_factor * l_own_ref[first + at] + prev_factor * total
        out = own_factor * o_own_ref[first + at] + prev_factor * out
        grad = dot_ref[first + at].astype(jnp.float32)
        stats_ref[0, at] = top
        stats_ref[1, at] = total
        stats_ref[2, at] = jnp.sum(grad * out, axis=0, keepdims=True)
        if first == 0:
            out_ref[at] = out
        else:
            share = jnp.where(total > 0, 1.0 / total, 0.0)
            out_ref[at] = (out * share).astype(jnp.bfloat16)


def prev_backward(
    first, group, has_ref, place_ref, qs_ref, dot_ref, p_ref, m_own_ref, m_prev_ref, stats_ref, other_ref, *rest
):
    kv, rest = rest[:group], rest[group:]
    if first == 0:
        terms_ref, dos_ref, shift_ref, ds_ref, factor_ref, scaled_ref, lower_ref = rest
    else:
        before_ref, terms_ref, dos_ref, shift_ref, ds_ref, scaled_ref, lower_ref = rest
    _, width, head_dim = qs_ref.shape
    sets, tiles = p_ref.shape[:2]
    span = 2 * block_rows
    per_tile = tile_keys // span
    scale = float(head_dim) ** (-0.5)
    exponent_scale = log2_e * scale
    has_prev = has_ref[0] > 0
    for at in range(sets):
        top = jnp.maximum(stats_ref[0, at], other_ref[0, at])
        here = jnp.exp2((stats_ref[0, at] - top) * exponent_scale)
        away = jnp.exp2((other_ref[0, at] - top) * exponent_scale)
        inverse = 1.0 / (here * stats_ref[1, at] + away * other_ref[1, at])
        delta = (here * stats_ref[2, at] + away * other_ref[2, at]) * inverse
        if first == 0:
            factor_ref[0, at] = here * inverse
            factor_ref[1, at] = away * other_ref[1, at] * inverse
        own_factor = jnp.exp2((m_own_ref[first + at] - top) * exponent_scale) * inverse
        prev_factor = jnp.exp2((m_prev_ref[at] - top) * exponent_scale) * inverse
        prev_factor = jnp.where(has_prev, prev_factor, 0.0)
        grad = dot_ref[first + at].astype(jnp.float32)
        dos_ref[at] = (grad * own_factor).astype(jnp.bfloat16)
        shift_ref[at] = delta * own_factor
        scaled_ref[at] = (grad * prev_factor).astype(jnp.bfloat16)
        lower_ref[at] = delta * prev_factor
    for tile in range(tiles):
        values = key_tile(kv, tile, 1)
        key_grad = jnp.zeros((tile_keys, head_dim), jnp.float32)
        value_grad = jnp.zeros((tile_keys, head_dim), jnp.float32)
        for at in range(sets):
            weights = p_ref[at, tile]
            value_grad += dot_nt(weights, scaled_ref[at])
            change = dot_nn(values, scaled_ref[at]) - lower_ref[at]
            change = (weights.astype(jnp.float32) * change).astype(jnp.bfloat16)
            key_grad += dot_nn(change, qs_ref[first + at])
            ds_ref[at, tile] = change
        key_grad = key_grad * scale
        if first == 0:
            rows = slice(tile * tile_keys, (tile + 1) * tile_keys)
            terms_ref[rows, :head_dim] = key_grad
            terms_ref[rows, head_dim:] = value_grad
        else:
            rows = slice(tile * tile_keys, (tile + 1) * tile_keys)
            key_grad = (key_grad + before_ref[rows, :head_dim]).astype(jnp.bfloat16)
            value_grad = (value_grad + before_ref[rows, head_dim:]).astype(jnp.bfloat16)
            for j in range(per_tile):
                rows = slice(j * span, (j + 1) * span)
                place = place_ref[tile * per_tile + j]
                terms_ref[place, :, :head_dim] = key_grad[rows]
                terms_ref[place, :, head_dim:] = value_grad[rows]


def own_backward(
    allowed_ref, slots_ref, place_ref, qs_ref, ks_ref, vs_ref, p_ref,
    dos_mine_ref, shift_mine_ref, ds_mine_ref, dos_theirs_ref, shift_theirs_ref, ds_theirs_ref, *rest
):
    kv, rest = rest[: slots_ref.shape[0]], rest[slots_ref.shape[0] :]
    dq_ref, dq_partner_ref, terms_ref, acc_ref, dqa_ref = rest
    steps, _, width = p_ref.shape
    group, span, _ = terms_ref.shape
    head_dim = ks_ref.shape[1]
    blocks = 2 * group
    tiles = blocks * block_rows // tile_keys
    scale = float(head_dim) ** (-0.5)

    acc_ref[...] = jnp.zeros(acc_ref.shape, jnp.float32)
    for at in range(4):
        changes = (ds_mine_ref, ds_theirs_ref)[at // 2]
        dqa_ref[at] = sum(
            dot_tn(key_tile(kv, tile, 0), changes[at % 2, tile]) for tile in range(tiles)
        )
    for step in range(steps):
        at, tile = own_tile(step, allowed_ref)
        start = pl.multiple_of(jnp.minimum(tile, tiles - 1) * tile_keys, tile_keys)
        window = pl.ds(start, tile_keys)
        weights = p_ref[step]
        dos_ref, shift_ref, first = (
            (dos_mine_ref, shift_mine_ref, 0) if step < 5 else (dos_theirs_ref, shift_theirs_ref, 2)
        )
        grad = dos_ref[at - first]
        acc_ref[window, head_dim:] += dot_nt(weights, grad)
        change = dot_nn(vs_ref[window, :], grad) - shift_ref[at - first]
        change = (weights.astype(jnp.float32) * change).astype(jnp.bfloat16)
        acc_ref[window, :head_dim] += dot_nn(change, qs_ref[at]) * scale
        dqa_ref[at] += dot_tn(ks_ref[window, :], change)
    for g in range(group):
        slot = slots_ref[g]
        for half, place in ((0, slot), (1, blocks - 1 - slot)):
            source = pl.ds(pl.multiple_of(place * block_rows, block_rows), block_rows)
            terms_ref[place_ref[g], half * block_rows : (half + 1) * block_rows, :] = acc_ref[
                source, :
            ].astype(jnp.bfloat16)
    for half in range(2):
        store_heads(dq_ref, half, dqa_ref[half].T * scale)
        store_heads(dq_partner_ref, half, dqa_ref[2 + half].T * scale)


def call(kernel, name, outs, in_smem, scratch, out_smem=(), flops=0, stream=()):
    vmem = pl.BlockSpec(memory_space=pltpu.VMEM)
    smem = pl.BlockSpec(memory_space=pltpu.SMEM)

    def spec(at, operand):
        if at in in_smem:
            return smem
        if at in stream:
            return pl.BlockSpec(operand.shape, lambda step: (0,) * operand.ndim)
        return vmem

    def run(*operands):
        return pl.pallas_call(
            kernel,
            name=name,
            grid=(1,) if stream else (),
            out_shape=[jax.ShapeDtypeStruct(shape, dtype) for shape, dtype in outs],
            in_specs=[spec(i, operand) for i, operand in enumerate(operands)],
            out_specs=[smem if i in out_smem else vmem for i in range(len(outs))],
            scratch_shapes=[pltpu.VMEM(shape, dtype) for shape, dtype in scratch],
            compiler_params=pltpu.CompilerParams(vmem_limit_bytes=16 * 1024 * 1024),
            cost_estimate=pl.CostEstimate(flops=flops, bytes_accessed=4 << 20, transcendentals=0),
        )(*operands)

    return run


def body(queries, key_vectors, value_vectors, grad_output, positions):
    tok_rows, full_width = queries.shape
    head_dim = key_vectors.shape[1]
    heads = full_width // head_dim
    group = lax.axis_size("inner") // 2
    segment = 2 * group * tok_rows
    span_rows = group * tok_rows
    width = heads * block_rows
    steps = 10
    bf16, f32 = jnp.bfloat16, jnp.float32
    query_partner = to_partner(queries, "inner")
    grad_partner = to_partner(grad_output, "inner")
    position_partner = to_partner(positions, "inner")
    anywhere = pl.BlockSpec(memory_space=pl.ANY)
    packed = pl.pallas_call(
        functools.partial(pack, segment),
        name="pack",
        out_shape=jax.ShapeDtypeStruct((2 * tok_rows + tag_rows, head_dim), bf16),
        in_specs=[anywhere] * 3,
        out_specs=anywhere,
        scratch_shapes=[
            pltpu.SMEM(positions.shape, jnp.int32),
            pltpu.VMEM((2 * tok_rows + tag_rows, head_dim), bf16),
            pltpu.SemaphoreType.DMA((3,)),
            pltpu.SemaphoreType.DMA((1,)),
        ],
        compiler_params=pltpu.CompilerParams(vmem_limit_bytes=60 * 1024 * 1024),
    )(positions, key_vectors, value_vectors)
    turns = [0] + [d if group // 2 >= d else d - group for d in range(1, group)]
    turns.sort(key=abs, reverse=False)
    turns.remove(0)
    turns.insert(0, 0)
    own_kv = [packed if d == 0 else turn(packed, "inner", d) for d in turns]
    place = (lax.axis_index("inner") // 2 - jnp.array(turns, jnp.int32)) % group
    prev_kv = [from_behind(block, "outer", 1) for block in own_kv]
    has_prev = (lax.axis_index("outer") > 0).astype(jnp.int32).reshape(1)

    unit = 2 * tile_keys * width * head_dim
    row_stat = ((4, 1, width), f32)
    by_query = ((4, head_dim, width), f32)
    by_query_16 = ((4, head_dim, width), bf16)
    tokens = ((tok_rows, full_width), bf16)
    terms_shape = ((group, tok_rows, 2 * head_dim), bf16)
    tiles = span_rows // tile_keys
    both_blocks, qs, dot = call(
        functools.partial(stack_pair, segment),
        "stack_pair",
        [((2,), jnp.int32), ((4, width, head_dim), bf16), by_query_16],
        (0, 1),
        [],
        out_smem=(0,),
        flops=4 * 10**9,
        stream=(2, 4),
    )(positions, position_partner, queries, query_partner, grad_output, grad_partner)
    ks, vs, slots, allowed, p_own, m_own, l_own, o_own = call(
        functools.partial(own_forward, group),
        "own_forward",
        [
            ((span_rows, head_dim), bf16),
            ((span_rows, head_dim), bf16),
            ((group,), jnp.int32),
            ((4,), jnp.int32),
            ((steps, tile_keys, width), bf16),
            row_stat,
            row_stat,
            by_query,
        ],
        (0,),
        [((steps, tile_keys, width), f32)],
        out_smem=(2, 3),
        flops=2 * steps * unit,
    )(both_blocks, qs, *own_kv)
    half_stat = ((2, 1, width), f32)
    half_query = ((2, head_dim, width), f32)
    changes = ((2, tiles, tile_keys, width), bf16)
    half_query_16 = ((2, head_dim, width), bf16)

    def forward(first, name):
        return call(
            functools.partial(prev_forward, first, group),
            name,
            [
                ((2, tiles, tile_keys, width), bf16),
                half_stat,
                ((3, 2, 1, width), f32),
                half_query if first == 0 else half_query_16,
            ],
            (0,),
            [((2, tiles, tile_keys, width), f32)],
            flops=2 * 2 * tiles * unit,
        )(has_prev, qs, dot, m_own, l_own, o_own, *prev_kv)

    p_theirs, m_theirs, stats_theirs, sent = forward(2, "prev_forward_theirs")
    other_mine = to_partner(stats_theirs, "inner")
    got = to_partner(sent, "inner")
    p_mine, m_mine, stats_mine, out = forward(0, "prev_forward_mine")
    other_theirs = to_partner(stats_mine, "inner")
    first_terms, dos_mine, shift_mine, ds_mine, factor = call(
        functools.partial(prev_backward, 0, group),
        "prev_backward_mine",
        [((span_rows, 2 * head_dim), f32), half_query_16, half_stat, changes, ((2, 2, 1, width), f32)],
        (0, 1),
        [half_query_16, half_stat],
        flops=4 * 2 * tiles * unit,
    )(has_prev, place, qs, dot, p_mine, m_own, m_mine, stats_mine, other_mine, *prev_kv)
    prev_terms, dos_theirs, shift_theirs, ds_theirs = call(
        functools.partial(prev_backward, 2, group),
        "prev_backward_theirs",
        [terms_shape, half_query_16, half_stat, changes],
        (0, 1),
        [half_query_16, half_stat],
        flops=4 * 2 * tiles * unit,
    )(
        has_prev, place, qs, dot, p_theirs, m_own, m_theirs, stats_theirs, other_theirs, *prev_kv, first_terms
    )
    returned = from_behind(prev_terms, "outer", -1)
    dq, dq_partner, own_terms = call(
        own_backward,
        "own_backward",
        [((tok_rows, full_width), f32), tokens, terms_shape],
        (0, 1, 2),
        [((span_rows, 2 * head_dim), f32), by_query],
        flops=4 * steps * unit,
    )(allowed, slots, place, qs, ks, vs, p_own, dos_mine, shift_mine, ds_mine, dos_theirs, shift_theirs, ds_theirs, *prev_kv)
    (attended,) = call(merge_attended, "merge_attended", [tokens], (), [])(out, got, factor)
    dq_other = to_partner(dq_partner, "inner")
    terms = (own_terms.astype(f32) + returned.astype(f32)).astype(bf16)
    key_grads = jnp.sum(exchange(terms, "inner").astype(f32), axis=0)
    grad_queries = (dq + dq_other.astype(f32)).astype(bf16)
    grad_keys = key_grads[:, :head_dim].astype(bf16)
    grad_values = key_grads[:, head_dim:].astype(bf16)
    return (attended, grad_queries, grad_keys, grad_values)


def solution(mesh):
    rows = P(("outer", "inner"), None)
    return jax.shard_map(
        body,
        mesh=mesh,
        in_specs=(rows, rows, rows, rows, P(("outer", "inner"))),
        out_specs=(rows, rows, rows, rows),
        check_vma=False,
    )
```

```python
import functools

import jax
import jax.numpy as jnp
from jax import lax
from jax.experimental import pallas as pl
from jax.experimental.pallas import tpu as pltpu
from jax.sharding import PartitionSpec as P

masked_score = -1e30
tile_keys = 256
log2_e = 1.4426950408889634
block_rows = 64
tag_rows = 16


def from_behind(block, axis, distance):
    devices = range(lax.axis_size(axis))
    route = [(i - distance, i) for i in devices if i - distance in devices]
    return lax.ppermute(block, axis, route)


def to_partner(block, axis):
    return lax.ppermute(block, axis, [(i, i ^ 1) for i in range(lax.axis_size(axis))])


def to_corner(block, distance):
    outer, inner = lax.axis_size("outer"), lax.axis_size("inner")
    route = [
        (o * inner + i, (o + distance) * inner + (i ^ 1))
        for o in range(outer)
        for i in range(inner)
        if o + distance in range(outer)
    ]
    return lax.ppermute(block, ("outer", "inner"), route)


def exchange(parts, axis):
    count = lax.axis_size(axis)
    groups = [list(range(first, count, 2)) for first in range(2)]
    return lax.all_to_all(parts, axis, 0, 0, axis_index_groups=groups, tiled=True)


def dot_nn(a, b):
    return lax.dot_general(a, b, (((1,), (0,)), ((), ())), preferred_element_type=jnp.float32)


def dot_nt(a, b):
    return lax.dot_general(a, b, (((1,), (1,)), ((), ())), preferred_element_type=jnp.float32)


def dot_tn(a, b):
    return lax.dot_general(a, b, (((0,), (0,)), ((), ())), preferred_element_type=jnp.float32)


def stack_heads(source, start, heads, head_dim):
    rows = slice(start, start + block_rows)
    return jnp.concatenate(
        [source[rows, h * head_dim : (h + 1) * head_dim] for h in range(heads)], axis=0
    )


def store_heads(target_ref, half, block):
    rows = slice(half * block_rows, (half + 1) * block_rows)
    head_dim = block.shape[1]
    for h in range(block.shape[0] // block_rows):
        target_ref[rows, h * head_dim : (h + 1) * head_dim] = block[
            h * block_rows : (h + 1) * block_rows
        ].astype(target_ref.dtype)


def pack(position_ref, key_ref, value_ref, packed_ref, place_ref, block_ref, in_sems, out_sems):
    count, rows, head_dim = packed_ref.shape
    span = key_ref.shape[0]
    loads = [
        pltpu.make_async_copy(position_ref, place_ref, in_sems.at[0]),
        pltpu.make_async_copy(key_ref, block_ref.at[pl.ds(0, span)], in_sems.at[1]),
        pltpu.make_async_copy(value_ref, block_ref.at[pl.ds(span, span)], in_sems.at[2]),
    ]
    for load in loads:
        load.start()
    loads[0].wait()
    tag = (lax.rem(place_ref[0], 2 * count * span) // block_rows).astype(jnp.float32)
    tag = jnp.full((rows - 2 * span, head_dim), tag, jnp.float32)
    block_ref[2 * span :, :] = tag.astype(packed_ref.dtype)
    loads[1].wait()
    loads[2].wait()
    stores = [
        pltpu.make_async_copy(block_ref, packed_ref.at[g], out_sems.at[g]) for g in range(count)
    ]
    for store in stores:
        store.start()
    for store in stores:
        store.wait()


def stack_pair(both_ref, partner_ref, qs_ref, dot_ref):
    _, width, head_dim = qs_ref.shape
    heads = width // block_rows
    span = 2 * block_rows
    for j, source in enumerate((both_ref, partner_ref)):
        for half in range(2):
            start = half * block_rows
            qs_ref[2 * j + half] = stack_heads(source, start, heads, head_dim)
            stacked = stack_heads(source, span + start, heads, head_dim).astype(jnp.float32)
            dot_ref[2 * j + half] = stacked.T.astype(jnp.bfloat16)


def merge_attended(out_ref, got_pair_ref, got_next_ref, got_corner_ref, factor_ref, att_ref):
    for half in range(2):
        out = factor_ref[0, half] * out_ref[half]
        for k, got_ref in enumerate((got_pair_ref, got_next_ref, got_corner_ref)):
            out = out + factor_ref[1 + k, half] * got_ref[half].astype(jnp.float32)
        store_heads(att_ref, half, out.T)


def combine(stats, at, exponent_scale, valid=None):
    places = [at, (at + 2) % 4, at, (at + 2) % 4]
    peaks = [ref[0, place] for ref, place in zip(stats, places)]
    if valid is not None:
        peaks[2:] = [jnp.where(valid, peak, masked_score) for peak in peaks[2:]]
    top = functools.reduce(jnp.maximum, peaks)
    factors = [jnp.exp2((peak - top) * exponent_scale) for peak in peaks]
    totals = [factor * ref[1, place] for factor, ref, place in zip(factors, stats, places)]
    inverse = 1.0 / sum(totals)
    delta = sum(factor * ref[2, place] for factor, ref, place in zip(factors, stats, places)) * inverse
    return factors[0] * inverse, [total * inverse for total in totals], delta


def put_stats(stats_ref, at, peak, total, out, grad):
    stats_ref[0, at] = peak
    stats_ref[1, at] = total
    stats_ref[2, at] = jnp.sum(grad.astype(jnp.float32) * out, axis=0, keepdims=True)
    return (out * jnp.where(total > 0, 1.0 / total, 0.0)).astype(jnp.bfloat16)


def own_tile(step, allowed_ref):
    low = 0 if step < 5 else 2
    local = step % 5
    per_tile = tile_keys // block_rows
    low_tiles = (allowed_ref[low] + per_tile - 1) // per_tile
    high = jnp.where(local >= low_tiles, 1, 0)
    tile = local - high * low_tiles
    return low + high, tile


def own_forward(
    segment, position_ref, position_partner_ref, qs_ref, dot_ref, kv_ref,
    ks_ref, vs_ref, slots_ref, allowed_ref, p_ref, stats_ref, out_ref, sent_ref,
    s_ref, m_ref, l_ref, o_ref,
):
    group, _, head_dim = kv_ref.shape
    span = 2 * block_rows
    steps, _, width = p_ref.shape
    blocks = 2 * group
    tiles = blocks * block_rows // tile_keys
    exponent_scale = log2_e * float(head_dim) ** (-0.5)
    tags = [jnp.max(kv_ref[g, 2 * span :, :].astype(jnp.float32)).astype(jnp.int32) for g in range(group)]

    def count(test):
        return sum(jnp.where(test(tag), 1, 0) for tag in tags)

    for j in range(2):
        mine = lax.rem((position_ref, position_partner_ref)[j][0], segment) // block_rows
        allowed_ref[2 * j] = count(lambda tag: tag <= mine)
        allowed_ref[2 * j + 1] = blocks - count(lambda tag: tag < mine)
    for g in range(group):
        slot = count(lambda tag: tag < tags[g])
        slots_ref[g] = slot
        for half, place in ((0, slot), (1, blocks - 1 - slot)):
            target = pl.ds(pl.multiple_of(place * block_rows, block_rows), block_rows)
            rows = slice(half * block_rows, (half + 1) * block_rows)
            ks_ref[target, :] = kv_ref[g, rows, :]
            rows = slice(span + half * block_rows, span + (half + 1) * block_rows)
            vs_ref[target, :] = kv_ref[g, rows, :]
    m_ref[...] = jnp.full(m_ref.shape, masked_score, jnp.float32)
    l_ref[...] = jnp.zeros(l_ref.shape, jnp.float32)
    o_ref[...] = jnp.zeros(o_ref.shape, jnp.float32)
    key_row = lax.broadcasted_iota(jnp.int32, (tile_keys, width), 0)
    query_row = lax.rem(lax.broadcasted_iota(jnp.int32, (1, width), 1), block_rows)
    for step in range(steps):
        at, tile = own_tile(step, allowed_ref)
        start = pl.multiple_of(jnp.minimum(tile, tiles - 1) * tile_keys, tile_keys)
        scores = dot_nt(ks_ref[pl.ds(start, tile_keys), :], qs_ref[at])
        last = query_row if step < 5 else block_rows - 1
        limit = (allowed_ref[at] - 1) * block_rows + last - tile * tile_keys
        scores = jnp.where(key_row <= limit, scores, masked_score)
        s_ref[step] = scores
        m_ref[at] = jnp.maximum(m_ref[at], jnp.max(scores, axis=0, keepdims=True))
    for step in range(steps):
        at, tile = own_tile(step, allowed_ref)
        start = pl.multiple_of(jnp.minimum(tile, tiles - 1) * tile_keys, tile_keys)
        raised = jnp.exp2((s_ref[step] - m_ref[at]) * exponent_scale)
        l_ref[at] += jnp.sum(raised, axis=0, keepdims=True)
        raised = raised.astype(jnp.bfloat16)
        p_ref[step] = raised
        o_ref[at] += dot_tn(vs_ref[pl.ds(start, tile_keys), :], raised)


    for at in range(4):
        shared = put_stats(stats_ref, at, m_ref[at], l_ref[at], o_ref[at], dot_ref[at])
        if at < 2:
            out_ref[at] = o_ref[at]
        else:
            sent_ref[at - 2] = shared


def next_forward(
    qs_ref, dot_ref, ks_ref, vs_ref, p_ref, stats_ref, sent_ref, sent_corner_ref, s_ref
):
    sets, width, head_dim = qs_ref.shape
    tiles = p_ref.shape[1]
    exponent_scale = log2_e * float(head_dim) ** (-0.5)
    peaks = []
    for at in range(sets):
        peak = jnp.full((1, width), masked_score, jnp.float32)
        for tile in range(tiles):
            scores = dot_nt(ks_ref[tile * tile_keys : (tile + 1) * tile_keys, :], qs_ref[at])
            s_ref[at, tile] = scores
            peak = jnp.maximum(peak, jnp.max(scores, axis=0, keepdims=True))
        peaks.append(peak)
    for at in range(sets):
        total = jnp.zeros((1, width), jnp.float32)
        out = jnp.zeros((head_dim, width), jnp.float32)
        for tile in range(tiles):
            raised = jnp.exp2((s_ref[at, tile] - peaks[at]) * exponent_scale)
            total += jnp.sum(raised, axis=0, keepdims=True)
            raised = raised.astype(jnp.bfloat16)
            p_ref[at, tile] = raised
            out += dot_tn(vs_ref[tile * tile_keys : (tile + 1) * tile_keys, :], raised)
        shared = put_stats(stats_ref, at, peaks[at], total, out, dot_ref[at])
        (sent_ref, sent_corner_ref)[at // 2][at % 2] = shared


def next_backward(
    qs_ref, dot_ref, ks_ref, vs_ref, p_ref, stats_ref, other_ref, ahead_ref, corner_ref,
    terms_ref, dq_ref, dq_corner_ref, scaled_ref, lower_ref, dqa_ref,
):
    sets, width, head_dim = qs_ref.shape
    tiles = p_ref.shape[1]
    scale = float(head_dim) ** (-0.5)
    for at in range(sets):
        factor, _, delta = combine((stats_ref, other_ref, ahead_ref, corner_ref), at, log2_e * scale)
        scaled_ref[at] = (dot_ref[at].astype(jnp.float32) * factor).astype(jnp.bfloat16)
        lower_ref[at] = delta * factor
    for tile in range(tiles):
        rows = slice(tile * tile_keys, (tile + 1) * tile_keys)
        keys, values = ks_ref[rows, :], vs_ref[rows, :]
        key_grad = jnp.zeros((tile_keys, head_dim), jnp.float32)
        value_grad = jnp.zeros((tile_keys, head_dim), jnp.float32)
        for at in range(sets):
            weights = p_ref[at, tile]
            value_grad += dot_nt(weights, scaled_ref[at])
            change = dot_nn(values, scaled_ref[at]) - lower_ref[at]
            change = (weights.astype(jnp.float32) * change).astype(jnp.bfloat16)
            key_grad += dot_nn(change, qs_ref[at])
            query_grad = dot_tn(keys, change)
            dqa_ref[at] = query_grad if tile == 0 else dqa_ref[at] + query_grad
        terms_ref[rows, :head_dim] = key_grad * scale
        terms_ref[rows, head_dim:] = value_grad
    for half in range(2):
        store_heads(dq_ref, half, dqa_ref[half].T * scale)
        store_heads(dq_corner_ref, half, dqa_ref[2 + half].T * scale)


def own_backward(
    has_ref, allowed_ref, slots_ref, qs_ref, dot_ref, ks_ref, vs_ref, p_ref,
    stats_ref, other_ref, behind_ref, corner_ref, next_terms_ref,
    dq_ref, dq_partner_ref, terms_ref, factor_ref, acc_ref, dqa_ref, dos_ref, shift_ref,
):
    steps, _, width = p_ref.shape
    group, span, _ = terms_ref.shape
    head_dim = ks_ref.shape[1]
    blocks = 2 * group
    tiles = blocks * block_rows // tile_keys
    scale = float(head_dim) ** (-0.5)
    has_prev = has_ref[0] > 0
    for at in range(4):
        factor, shares, delta = combine(
            (stats_ref, other_ref, behind_ref, corner_ref), at, log2_e * scale, has_prev
        )
        dos_ref[at] = (dot_ref[at].astype(jnp.float32) * factor).astype(jnp.bfloat16)
        shift_ref[at] = delta * factor
        if at < 2:
            factor_ref[0, at] = factor
            for k in range(1, 4):
                factor_ref[k, at] = shares[k]
    acc_ref[...] = next_terms_ref[...]
    dqa_ref[...] = jnp.zeros(dqa_ref.shape, jnp.float32)
    for step in range(steps):
        at, tile = own_tile(step, allowed_ref)
        start = pl.multiple_of(jnp.minimum(tile, tiles - 1) * tile_keys, tile_keys)
        window = pl.ds(start, tile_keys)
        weights = p_ref[step]
        grad = dos_ref[at]
        acc_ref[window, head_dim:] += dot_nt(weights, grad)
        change = dot_nn(vs_ref[window, :], grad) - shift_ref[at]
        change = (weights.astype(jnp.float32) * change).astype(jnp.bfloat16)
        acc_ref[window, :head_dim] += dot_nn(change, qs_ref[at]) * scale
        dqa_ref[at] += dot_tn(ks_ref[window, :], change)
    for g in range(group):
        slot = slots_ref[g]
        for half, place in ((0, slot), (1, blocks - 1 - slot)):
            source = pl.ds(pl.multiple_of(place * block_rows, block_rows), block_rows)
            terms_ref[g, half * block_rows : (half + 1) * block_rows, :] = acc_ref[
                source, :
            ].astype(jnp.bfloat16)
    for half in range(2):
        store_heads(dq_ref, half, dqa_ref[half].T * scale)
        store_heads(dq_partner_ref, half, dqa_ref[2 + half].T * scale)


def call(kernel, name, outs, in_smem, scratch, out_smem=(), flops=0, stream=()):
    vmem = pl.BlockSpec(memory_space=pltpu.VMEM)
    smem = pl.BlockSpec(memory_space=pltpu.SMEM)

    def spec(at, operand):
        if at in in_smem:
            return smem
        if at in stream:
            return pl.BlockSpec(operand.shape, lambda step: (0,) * operand.ndim)
        return vmem

    def run(*operands):
        return pl.pallas_call(
            kernel,
            name=name,
            grid=(1,) if stream else (),
            out_shape=[jax.ShapeDtypeStruct(shape, dtype) for shape, dtype in outs],
            in_specs=[spec(i, operand) for i, operand in enumerate(operands)],
            out_specs=[smem if i in out_smem else vmem for i in range(len(outs))],
            scratch_shapes=[pltpu.VMEM(shape, dtype) for shape, dtype in scratch],
            compiler_params=pltpu.CompilerParams(vmem_limit_bytes=16 * 1024 * 1024),
            cost_estimate=pl.CostEstimate(flops=flops, bytes_accessed=4 << 20, transcendentals=0),
        )(*operands)

    return run


def body(queries, key_vectors, value_vectors, grad_output, positions):
    tok_rows, full_width = queries.shape
    head_dim = key_vectors.shape[1]
    heads = full_width // head_dim
    group = lax.axis_size("inner") // 2
    segment = 2 * group * tok_rows
    span_rows = group * tok_rows
    width = heads * block_rows
    steps = 10
    bf16, f32 = jnp.bfloat16, jnp.float32
    both = jnp.concatenate([queries, grad_output], axis=0)
    both_partner = to_partner(both, "inner")
    both_next = from_behind(both, "outer", -1)
    both_corner = to_partner(both_next, "inner")
    position_partner = to_partner(positions, "inner")
    anywhere = pl.BlockSpec(memory_space=pl.ANY)
    packed = pl.pallas_call(
        pack,
        name="pack",
        out_shape=jax.ShapeDtypeStruct((group, 2 * tok_rows + tag_rows, head_dim), bf16),
        in_specs=[anywhere] * 3,
        out_specs=anywhere,
        scratch_shapes=[
            pltpu.SMEM(positions.shape, jnp.int32),
            pltpu.VMEM((2 * tok_rows + tag_rows, head_dim), bf16),
            pltpu.SemaphoreType.DMA((3,)),
            pltpu.SemaphoreType.DMA((group,)),
        ],
        compiler_params=pltpu.CompilerParams(vmem_limit_bytes=60 * 1024 * 1024),
    )(positions, key_vectors, value_vectors)
    has_prev = (lax.axis_index("outer") > 0).astype(jnp.int32).reshape(1)
    packed, has_prev = lax.optimization_barrier((packed, has_prev))
    group_kv = exchange(packed, "inner")

    unit = 2 * tile_keys * width * head_dim
    tiles = span_rows // tile_keys
    stats_shape = ((3, 4, 1, width), f32)
    by_query = ((4, head_dim, width), f32)
    by_query_16 = ((4, head_dim, width), bf16)
    half_query = ((2, head_dim, width), f32)
    half_query_16 = ((2, head_dim, width), bf16)
    row_stat = ((4, 1, width), f32)
    stacked = ((4, width, head_dim), bf16)
    tokens = ((tok_rows, full_width), bf16)
    tokens_32 = ((tok_rows, full_width), f32)
    sorted_keys = ((span_rows, head_dim), bf16)
    terms_shape = ((group, tok_rows, 2 * head_dim), bf16)
    sum_shape = ((span_rows, 2 * head_dim), f32)

    qs, dot = call(stack_pair, "stack_pair", [stacked, by_query_16], (), [], flops=4 * 10**9)(
        both, both_partner
    )
    ks, vs, slots, allowed, p_own, stats_own, out, sent_pair = call(
        functools.partial(own_forward, segment),
        "own_forward",
        [
            sorted_keys,
            sorted_keys,
            ((group,), jnp.int32),
            ((4,), jnp.int32),
            ((steps, tile_keys, width), bf16),
            stats_shape,
            half_query,
            half_query_16,
        ],
        (0, 1),
        [((steps, tile_keys, width), f32), row_stat, row_stat, by_query],
        out_smem=(2, 3),
        flops=2 * steps * unit,
    )(positions, position_partner, qs, dot, group_kv)
    own_pair = to_partner(stats_own, "inner")
    own_ahead = from_behind(stats_own, "outer", -1)
    own_corner = to_corner(stats_own, -1)
    qs_next, dot_next = call(stack_pair, "stack_next", [stacked, by_query_16], (), [], flops=10**9)(
        both_next, both_corner
    )
    p_next, stats_next, sent_next, sent_corner = call(
        next_forward,
        "next_forward",
        [((4, tiles, tile_keys, width), bf16), stats_shape, half_query_16, half_query_16],
        (),
        [((4, tiles, tile_keys, width), f32)],
        flops=2 * 4 * tiles * unit,
    )(qs_next, dot_next, ks, vs)
    next_pair = to_partner(stats_next, "inner")
    next_behind = from_behind(stats_next, "outer", 1)
    next_corner = to_corner(stats_next, 1)
    next_terms, dq_next, dq_corner = call(
        next_backward,
        "next_backward",
        [sum_shape, tokens, tokens],
        (),
        [by_query_16, row_stat, by_query],
        flops=4 * 4 * tiles * unit,
    )(qs_next, dot_next, ks, vs, p_next, stats_next, next_pair, own_ahead, own_corner)
    dq, dq_partner, terms, factor = call(
        own_backward,
        "own_backward",
        [tokens_32, tokens, terms_shape, ((4, 2, 1, width), f32)],
        (0, 1, 2),
        [sum_shape, by_query, by_query_16, row_stat],
        flops=4 * steps * unit,
    )(has_prev, allowed, slots, qs, dot, ks, vs, p_own, stats_own, own_pair, next_behind, next_corner, next_terms)
    key_grads = jnp.sum(exchange(terms, "inner").astype(f32), axis=0)
    (attended,) = call(merge_attended, "merge_attended", [tokens], (), [])(
        out,
        to_partner(sent_pair, "inner"),
        from_behind(sent_next, "outer", 1),
        to_corner(sent_corner, 1),
        factor,
    )
    dq = dq + to_partner(dq_partner, "inner").astype(f32)
    dq = dq + from_behind(dq_next, "outer", 1).astype(f32)
    grad_queries = (dq + to_corner(dq_corner, 1).astype(f32)).astype(bf16)
    grad_keys = key_grads[:, :head_dim].astype(bf16)
    grad_values = key_grads[:, head_dim:].astype(bf16)
    return (attended, grad_queries, grad_keys, grad_values)


def solution(mesh):
    rows = P(("outer", "inner"), None)
    return jax.shard_map(
        body,
        mesh=mesh,
        in_specs=(rows, rows, rows, rows, P(("outer", "inner"))),
        out_specs=(rows, rows, rows, rows),
        check_vma=False,
    )
```

```python
import functools

import jax
import jax.numpy as jnp
from jax import lax
from jax.experimental import pallas as pl
from jax.experimental.pallas import tpu as pltpu
from jax.sharding import PartitionSpec as P

masked_score = -1e30
tile_keys = 256
log2_e = 1.4426950408889634
block_rows = 64
tag_rows = 16


def from_behind(block, axis, distance):
    devices = range(lax.axis_size(axis))
    route = [(i - distance, i) for i in devices if i - distance in devices]
    return lax.ppermute(block, axis, route)


def to_partner(block, axis):
    return lax.ppermute(block, axis, [(i, i ^ 1) for i in range(lax.axis_size(axis))])


def exchange(parts, axis):
    count = lax.axis_size(axis)
    groups = [list(range(first, count, 2)) for first in range(2)]
    return lax.all_to_all(parts, axis, 0, 0, axis_index_groups=groups, tiled=True)


def dot_nn(a, b):
    return lax.dot_general(a, b, (((1,), (0,)), ((), ())), preferred_element_type=jnp.float32)


def dot_nt(a, b):
    return lax.dot_general(a, b, (((1,), (1,)), ((), ())), preferred_element_type=jnp.float32)


def dot_tn(a, b):
    return lax.dot_general(a, b, (((0,), (0,)), ((), ())), preferred_element_type=jnp.float32)


def stack_heads(source, half, heads, head_dim):
    rows = slice(half * block_rows, (half + 1) * block_rows)
    return jnp.concatenate(
        [source[rows, h * head_dim : (h + 1) * head_dim] for h in range(heads)], axis=0
    )


def store_heads(target_ref, half, block):
    rows = slice(half * block_rows, (half + 1) * block_rows)
    head_dim = block.shape[1]
    for h in range(block.shape[0] // block_rows):
        target_ref[rows, h * head_dim : (h + 1) * head_dim] = block[
            h * block_rows : (h + 1) * block_rows
        ].astype(target_ref.dtype)


def pack(position_ref, key_ref, value_ref, packed_ref, place_ref, block_ref, in_sems, out_sems):
    count, rows, head_dim = packed_ref.shape
    span = key_ref.shape[0]
    loads = [
        pltpu.make_async_copy(position_ref, place_ref, in_sems.at[0]),
        pltpu.make_async_copy(key_ref, block_ref.at[pl.ds(0, span)], in_sems.at[1]),
        pltpu.make_async_copy(value_ref, block_ref.at[pl.ds(span, span)], in_sems.at[2]),
    ]
    for load in loads:
        load.start()
    loads[0].wait()
    tag = (lax.rem(place_ref[0], 2 * count * span) // block_rows).astype(jnp.float32)
    tag = jnp.full((rows - 2 * span, head_dim), tag, jnp.float32)
    block_ref[2 * span :, :] = tag.astype(packed_ref.dtype)
    loads[1].wait()
    loads[2].wait()
    stores = [
        pltpu.make_async_copy(block_ref, packed_ref.at[g], out_sems.at[g]) for g in range(count)
    ]
    for store in stores:
        store.start()
    for store in stores:
        store.wait()


def stack_pair(
    segment, position_ref, position_partner_ref, q_ref, q_partner_ref, do_ref, do_partner_ref,
    block_ref, qs_ref, dot_ref,
):
    _, width, head_dim = qs_ref.shape
    heads = width // block_rows
    block_ref[0] = lax.rem(position_ref[0], segment) // block_rows
    block_ref[1] = lax.rem(position_partner_ref[0], segment) // block_rows
    for j, (query, grad) in enumerate(((q_ref, do_ref), (q_partner_ref, do_partner_ref))):
        for half in range(2):
            qs_ref[2 * j + half] = stack_heads(query, half, heads, head_dim)
            stacked = stack_heads(grad, half, heads, head_dim).astype(jnp.float32)
            dot_ref[2 * j + half] = stacked.T.astype(jnp.bfloat16)


def merge_attended(out_ref, got_ref, factor_ref, att_ref):
    for half in range(2):
        out = factor_ref[0, half] * out_ref[half]
        out = out + factor_ref[1, half] * got_ref[half].astype(jnp.float32)
        store_heads(att_ref, half, out.T)


def own_tile(step, allowed_ref):
    low = 0 if step < 5 else 2
    local = step % 5
    per_tile = tile_keys // block_rows
    low_tiles = (allowed_ref[low] + per_tile - 1) // per_tile
    high = jnp.where(local >= low_tiles, 1, 0)
    tile = local - high * low_tiles
    return low + high, tile


def own_forward(
    block_ref, qs_ref, kv_ref,
    ks_ref, vs_ref, slots_ref, allowed_ref, p_ref, m_ref, l_ref, o_ref, s_ref,
):
    group, _, head_dim = kv_ref.shape
    span = 2 * block_rows
    steps, _, width = p_ref.shape
    blocks = 2 * group
    tiles = blocks * block_rows // tile_keys
    exponent_scale = log2_e * float(head_dim) ** (-0.5)
    tags = [jnp.max(kv_ref[g, 2 * span :, :].astype(jnp.float32)).astype(jnp.int32) for g in range(group)]

    def count(test):
        return sum(jnp.where(test(tag), 1, 0) for tag in tags)

    for j in range(2):
        mine = block_ref[j]
        allowed_ref[2 * j] = count(lambda tag: tag <= mine)
        allowed_ref[2 * j + 1] = blocks - count(lambda tag: tag < mine)
    for g in range(group):
        slot = count(lambda tag: tag < tags[g])
        slots_ref[g] = slot
        for half, place in ((0, slot), (1, blocks - 1 - slot)):
            target = pl.ds(pl.multiple_of(place * block_rows, block_rows), block_rows)
            rows = slice(half * block_rows, (half + 1) * block_rows)
            ks_ref[target, :] = kv_ref[g, rows, :]
            rows = slice(span + half * block_rows, span + (half + 1) * block_rows)
            vs_ref[target, :] = kv_ref[g, rows, :]
    m_ref[...] = jnp.full(m_ref.shape, masked_score, jnp.float32)
    l_ref[...] = jnp.zeros(l_ref.shape, jnp.float32)
    o_ref[...] = jnp.zeros(o_ref.shape, jnp.float32)
    key_row = lax.broadcasted_iota(jnp.int32, (tile_keys, width), 0)
    query_row = lax.rem(lax.broadcasted_iota(jnp.int32, (1, width), 1), block_rows)
    for step in range(steps):
        at, tile = own_tile(step, allowed_ref)
        start = pl.multiple_of(jnp.minimum(tile, tiles - 1) * tile_keys, tile_keys)
        scores = dot_nt(ks_ref[pl.ds(start, tile_keys), :], qs_ref[at])
        last = query_row if step < 5 else block_rows - 1
        limit = (allowed_ref[at] - 1) * block_rows + last - tile * tile_keys
        scores = jnp.where(key_row <= limit, scores, masked_score)
        s_ref[step] = scores
        m_ref[at] = jnp.maximum(m_ref[at], jnp.max(scores, axis=0, keepdims=True))
    for step in range(steps):
        at, tile = own_tile(step, allowed_ref)
        start = pl.multiple_of(jnp.minimum(tile, tiles - 1) * tile_keys, tile_keys)
        raised = jnp.exp2((s_ref[step] - m_ref[at]) * exponent_scale)
        l_ref[at] += jnp.sum(raised, axis=0, keepdims=True)
        raised = raised.astype(jnp.bfloat16)
        p_ref[step] = raised
        o_ref[at] += dot_tn(vs_ref[pl.ds(start, tile_keys), :], raised)


def key_tile(ref, tile):
    return ref[tile * tile_keys : (tile + 1) * tile_keys, :]


def prev_forward(
    first, has_ref, qs_ref, dot_ref, *rest
):
    if first == 0:
        ks_ref, vs_ref, m_own_ref, l_own_ref, o_own_ref, *rest = rest
        p_ref, m_prev_ref, stats_ref, out_ref, s_ref = rest
    else:
        kv_ref, m_own_ref, l_own_ref, o_own_ref, *rest = rest
        p_ref, m_prev_ref, stats_ref, out_ref, ks_ref, vs_ref, s_ref = rest
        span = 2 * block_rows
        for g in range(kv_ref.shape[0]):
            ks_ref[g * span : (g + 1) * span, :] = kv_ref[g, :span, :]
            vs_ref[g * span : (g + 1) * span, :] = kv_ref[g, span : 2 * span, :]
    _, width, head_dim = qs_ref.shape
    sets, tiles = p_ref.shape[:2]
    exponent_scale = log2_e * float(head_dim) ** (-0.5)
    has_prev = has_ref[0] > 0
    for at in range(sets):
        peak = jnp.full((1, width), masked_score, jnp.float32)
        for tile in range(tiles):
            scores = dot_nt(key_tile(ks_ref, tile), qs_ref[first + at])
            s_ref[at, tile] = scores
            peak = jnp.maximum(peak, jnp.max(scores, axis=0, keepdims=True))
        m_prev_ref[at] = peak
    for at in range(sets):
        peak = m_prev_ref[at]
        total = jnp.zeros((1, width), jnp.float32)
        out = jnp.zeros((head_dim, width), jnp.float32)
        for tile in range(tiles):
            raised = jnp.exp2((s_ref[at, tile] - peak) * exponent_scale)
            total += jnp.sum(raised, axis=0, keepdims=True)
            raised = raised.astype(jnp.bfloat16)
            p_ref[at, tile] = raised
            out += dot_tn(key_tile(vs_ref, tile), raised)
        peak = jnp.where(has_prev, peak, masked_score)
        m_prev_ref[at] = peak
        top = jnp.maximum(peak, m_own_ref[first + at])
        own_factor = jnp.exp2((m_own_ref[first + at] - top) * exponent_scale)
        prev_factor = jnp.where(has_prev, jnp.exp2((peak - top) * exponent_scale), 0.0)
        total = own_factor * l_own_ref[first + at] + prev_factor * total
        out = own_factor * o_own_ref[first + at] + prev_factor * out
        grad = dot_ref[first + at].astype(jnp.float32)
        stats_ref[0, at] = top
        stats_ref[1, at] = total
        stats_ref[2, at] = jnp.sum(grad * out, axis=0, keepdims=True)
        if first == 0:
            out_ref[at] = out
        else:
            share = jnp.where(total > 0, 1.0 / total, 0.0)
            out_ref[at] = (out * share).astype(jnp.bfloat16)


def prev_backward(first, has_ref, qs_ref, dot_ref, ks_ref, vs_ref, p_ref, m_own_ref, m_prev_ref, stats_ref, other_ref, *rest):
    if first == 0:
        key_terms_ref, value_terms_ref, dos_ref, shift_ref, ds_ref, factor_ref, scaled_ref, lower_ref = rest
    else:
        key_before_ref, value_before_ref, key_terms_ref, value_terms_ref = rest[:4]
        dos_ref, shift_ref, ds_ref, scaled_ref, lower_ref = rest[4:]
    _, width, head_dim = qs_ref.shape
    sets, tiles = p_ref.shape[:2]
    span = 2 * block_rows
    per_tile = tile_keys // span
    scale = float(head_dim) ** (-0.5)
    exponent_scale = log2_e * scale
    has_prev = has_ref[0] > 0
    for at in range(sets):
        top = jnp.maximum(stats_ref[0, at], other_ref[0, at])
        here = jnp.exp2((stats_ref[0, at] - top) * exponent_scale)
        away = jnp.exp2((other_ref[0, at] - top) * exponent_scale)
        inverse = 1.0 / (here * stats_ref[1, at] + away * other_ref[1, at])
        delta = (here * stats_ref[2, at] + away * other_ref[2, at]) * inverse
        if first == 0:
            factor_ref[0, at] = here * inverse
            factor_ref[1, at] = away * other_ref[1, at] * inverse
        own_factor = jnp.exp2((m_own_ref[first + at] - top) * exponent_scale) * inverse
        prev_factor = jnp.exp2((m_prev_ref[at] - top) * exponent_scale) * inverse
        prev_factor = jnp.where(has_prev, prev_factor, 0.0)
        grad = dot_ref[first + at].astype(jnp.float32)
        dos_ref[at] = (grad * own_factor).astype(jnp.bfloat16)
        shift_ref[at] = delta * own_factor
        scaled_ref[at] = (grad * prev_factor).astype(jnp.bfloat16)
        lower_ref[at] = delta * prev_factor
    for tile in range(tiles):
        values = key_tile(vs_ref, tile)
        key_grad = jnp.zeros((tile_keys, head_dim), jnp.float32)
        value_grad = jnp.zeros((tile_keys, head_dim), jnp.float32)
        for at in range(sets):
            weights = p_ref[at, tile]
            value_grad += dot_nt(weights, scaled_ref[at])
            change = dot_nn(values, scaled_ref[at]) - lower_ref[at]
            change = (weights.astype(jnp.float32) * change).astype(jnp.bfloat16)
            key_grad += dot_nn(change, qs_ref[first + at])
            ds_ref[at, tile] = change
        key_grad = key_grad * scale
        if first == 0:
            rows = slice(tile * tile_keys, (tile + 1) * tile_keys)
            key_terms_ref[rows, :] = key_grad
            value_terms_ref[rows, :] = value_grad
        else:
            rows = slice(tile * tile_keys, (tile + 1) * tile_keys)
            key_grad = (key_grad + key_before_ref[rows, :]).astype(jnp.bfloat16)
            value_grad = (value_grad + value_before_ref[rows, :]).astype(jnp.bfloat16)
            for j in range(per_tile):
                rows = slice(j * span, (j + 1) * span)
                key_terms_ref[tile * per_tile + j] = key_grad[rows]
                value_terms_ref[tile * per_tile + j] = value_grad[rows]


def own_backward(
    allowed_ref, slots_ref, qs_ref, ks_ref, vs_ref, p_ref,
    dos_mine_ref, shift_mine_ref, ds_mine_ref, dos_theirs_ref, shift_theirs_ref, ds_theirs_ref, prev_ks_ref,
    dq_ref, dq_partner_ref, terms_ref, acc_ref, dqa_ref,
):
    steps, _, width = p_ref.shape
    group, span, _ = terms_ref.shape
    head_dim = ks_ref.shape[1]
    blocks = 2 * group
    tiles = blocks * block_rows // tile_keys
    scale = float(head_dim) ** (-0.5)

    acc_ref[...] = jnp.zeros(acc_ref.shape, jnp.float32)
    for at in range(4):
        changes = (ds_mine_ref, ds_theirs_ref)[at // 2]
        dqa_ref[at] = sum(
            dot_tn(key_tile(prev_ks_ref, tile), changes[at % 2, tile]) for tile in range(tiles)
        )
    for step in range(steps):
        at, tile = own_tile(step, allowed_ref)
        start = pl.multiple_of(jnp.minimum(tile, tiles - 1) * tile_keys, tile_keys)
        window = pl.ds(start, tile_keys)
        weights = p_ref[step]
        dos_ref, shift_ref, first = (
            (dos_mine_ref, shift_mine_ref, 0) if step < 5 else (dos_theirs_ref, shift_theirs_ref, 2)
        )
        grad = dos_ref[at - first]
        acc_ref[window, head_dim:] += dot_nt(weights, grad)
        change = dot_nn(vs_ref[window, :], grad) - shift_ref[at - first]
        change = (weights.astype(jnp.float32) * change).astype(jnp.bfloat16)
        acc_ref[window, :head_dim] += dot_nn(change, qs_ref[at]) * scale
        dqa_ref[at] += dot_tn(ks_ref[window, :], change)
    for g in range(group):
        slot = slots_ref[g]
        for half, place in ((0, slot), (1, blocks - 1 - slot)):
            source = pl.ds(pl.multiple_of(place * block_rows, block_rows), block_rows)
            terms_ref[g, half * block_rows : (half + 1) * block_rows, :] = acc_ref[
                source, :
            ].astype(jnp.bfloat16)
    for half in range(2):
        store_heads(dq_ref, half, dqa_ref[half].T * scale)
        store_heads(dq_partner_ref, half, dqa_ref[2 + half].T * scale)


def call(kernel, name, outs, in_smem, scratch, out_smem=(), flops=0, stream=()):
    vmem = pl.BlockSpec(memory_space=pltpu.VMEM)
    smem = pl.BlockSpec(memory_space=pltpu.SMEM)

    def spec(at, operand):
        if at in in_smem:
            return smem
        if at in stream:
            return pl.BlockSpec(operand.shape, lambda step: (0,) * operand.ndim)
        return vmem

    def run(*operands):
        return pl.pallas_call(
            kernel,
            name=name,
            grid=(1,) if stream else (),
            out_shape=[jax.ShapeDtypeStruct(shape, dtype) for shape, dtype in outs],
            in_specs=[spec(i, operand) for i, operand in enumerate(operands)],
            out_specs=[smem if i in out_smem else vmem for i in range(len(outs))],
            scratch_shapes=[pltpu.VMEM(shape, dtype) for shape, dtype in scratch],
            compiler_params=pltpu.CompilerParams(vmem_limit_bytes=16 * 1024 * 1024),
            cost_estimate=pl.CostEstimate(flops=flops, bytes_accessed=4 << 20, transcendentals=0),
        )(*operands)

    return run


def body(queries, key_vectors, value_vectors, grad_output, positions):
    tok_rows, full_width = queries.shape
    head_dim = key_vectors.shape[1]
    heads = full_width // head_dim
    group = lax.axis_size("inner") // 2
    segment = 2 * group * tok_rows
    span_rows = group * tok_rows
    width = heads * block_rows
    steps = 10
    bf16, f32 = jnp.bfloat16, jnp.float32
    query_partner = to_partner(queries, "inner")
    grad_partner = to_partner(grad_output, "inner")
    position_partner = to_partner(positions, "inner")
    anywhere = pl.BlockSpec(memory_space=pl.ANY)
    packed = pl.pallas_call(
        pack,
        name="pack",
        out_shape=jax.ShapeDtypeStruct((group, 2 * tok_rows + tag_rows, head_dim), bf16),
        in_specs=[anywhere] * 3,
        out_specs=anywhere,
        scratch_shapes=[
            pltpu.SMEM(positions.shape, jnp.int32),
            pltpu.VMEM((2 * tok_rows + tag_rows, head_dim), bf16),
            pltpu.SemaphoreType.DMA((3,)),
            pltpu.SemaphoreType.DMA((group,)),
        ],
        compiler_params=pltpu.CompilerParams(vmem_limit_bytes=60 * 1024 * 1024),
    )(positions, key_vectors, value_vectors)
    group_kv = exchange(packed, "inner")
    has_prev = (lax.axis_index("outer") > 0).astype(jnp.int32).reshape(1)

    unit = 2 * tile_keys * width * head_dim
    row_stat = ((4, 1, width), f32)
    by_query = ((4, head_dim, width), f32)
    by_query_16 = ((4, head_dim, width), bf16)
    tokens = ((tok_rows, full_width), bf16)
    terms_shape = ((group, tok_rows, 2 * head_dim), bf16)
    tiles = span_rows // tile_keys
    both_blocks, qs, dot = call(
        functools.partial(stack_pair, segment),
        "stack_pair",
        [((2,), jnp.int32), ((4, width, head_dim), bf16), by_query_16],
        (0, 1),
        [],
        out_smem=(0,),
        flops=4 * 10**9,
        stream=(2, 4),
    )(positions, position_partner, queries, query_partner, grad_output, grad_partner)
    group_kv, qs, dot, both_blocks = lax.optimization_barrier((group_kv, qs, dot, both_blocks))
    prev_kv = from_behind(group_kv, "outer", 1)
    ks, vs, slots, allowed, p_own, m_own, l_own, o_own = call(
        own_forward,
        "own_forward",
        [
            ((span_rows, head_dim), bf16),
            ((span_rows, head_dim), bf16),
            ((group,), jnp.int32),
            ((4,), jnp.int32),
            ((steps, tile_keys, width), bf16),
            row_stat,
            row_stat,
            by_query,
        ],
        (0,),
        [((steps, tile_keys, width), f32)],
        out_smem=(2, 3),
        flops=2 * steps * unit,
    )(both_blocks, qs, group_kv)
    half_stat = ((2, 1, width), f32)
    half_query = ((2, head_dim, width), f32)
    half_terms = ((group, tok_rows, head_dim), bf16)
    changes = ((2, tiles, tile_keys, width), bf16)
    half_query_16 = ((2, head_dim, width), bf16)

    def forward(first, name, *keys_and_values):
        sorted_out = [((span_rows, head_dim), bf16)] * 2
        return call(
            functools.partial(prev_forward, first),
            name,
            [
                ((2, tiles, tile_keys, width), bf16),
                half_stat,
                ((3, 2, 1, width), f32),
                half_query if first == 0 else half_query_16,
            ]
            + (sorted_out if first else []),
            (0,),
            [((2, tiles, tile_keys, width), f32)],
            flops=2 * 2 * tiles * unit,
        )(has_prev, qs, dot, *keys_and_values, m_own, l_own, o_own)

    p_theirs, m_theirs, stats_theirs, sent, prev_ks, prev_vs = forward(2, "prev_forward_theirs", prev_kv)
    other_mine = to_partner(stats_theirs, "inner")
    got = to_partner(sent, "inner")
    p_mine, m_mine, stats_mine, out = forward(0, "prev_forward_mine", prev_ks, prev_vs)
    other_theirs = to_partner(stats_mine, "inner")
    key_first, value_first, dos_mine, shift_mine, ds_mine, factor = call(
        functools.partial(prev_backward, 0),
        "prev_backward_mine",
        [
            ((span_rows, head_dim), f32),
            ((span_rows, head_dim), f32),
            half_query_16,
            half_stat,
            changes,
            ((2, 2, 1, width), f32),
        ],
        (0,),
        [half_query_16, half_stat],
        flops=4 * 2 * tiles * unit,
    )(has_prev, qs, dot, prev_ks, prev_vs, p_mine, m_own, m_mine, stats_mine, other_mine)
    key_terms, value_terms, dos_theirs, shift_theirs, ds_theirs = call(
        functools.partial(prev_backward, 2),
        "prev_backward_theirs",
        [half_terms, half_terms, half_query_16, half_stat, changes],
        (0,),
        [half_query_16, half_stat],
        flops=4 * 2 * tiles * unit,
    )(has_prev, qs, dot, prev_ks, prev_vs, p_theirs, m_own, m_theirs, stats_theirs, other_theirs, key_first, value_first)
    key_returned = from_behind(key_terms, "outer", -1)
    value_returned = from_behind(value_terms, "outer", -1)
    dq, dq_partner, own_terms = call(
        own_backward,
        "own_backward",
        [((tok_rows, full_width), f32), tokens, terms_shape],
        (0, 1),
        [((span_rows, 2 * head_dim), f32), by_query],
        flops=4 * steps * unit,
    )(allowed, slots, qs, ks, vs, p_own, dos_mine, shift_mine, ds_mine, dos_theirs, shift_theirs, ds_theirs, prev_ks)
    (attended,) = call(merge_attended, "merge_attended", [tokens], (), [])(out, got, factor)
    dq_other = to_partner(dq_partner, "inner")
    returned = jnp.concatenate([key_returned, value_returned], axis=2)
    terms = (own_terms.astype(f32) + returned.astype(f32)).astype(bf16)
    key_grads = jnp.sum(exchange(terms, "inner").astype(f32), axis=0)
    grad_queries = (dq + dq_other.astype(f32)).astype(bf16)
    grad_keys = key_grads[:, :head_dim].astype(bf16)
    grad_values = key_grads[:, head_dim:].astype(bf16)
    return (attended, grad_queries, grad_keys, grad_values)


def solution(mesh):
    rows = P(("outer", "inner"), None)
    return jax.shard_map(
        body,
        mesh=mesh,
        in_specs=(rows, rows, rows, rows, P(("outer", "inner"))),
        out_specs=(rows, rows, rows, rows),
        check_vma=False,
    )
```

```python
import functools

import jax
import jax.numpy as jnp
from jax import lax
from jax.experimental import pallas as pl
from jax.experimental.pallas import tpu as pltpu
from jax.sharding import PartitionSpec as P

masked_score = -1e30
tile_keys = 256
log2_e = 1.4426950408889634
block_rows = 64
tag_rows = 16


def to_segment(block, distance):
    outer, inner = lax.axis_size("outer"), lax.axis_size("inner")
    route = []
    for o in range(outer):
        if o + distance in range(outer):
            crossed = 1 if max(o, o + distance) == outer // 2 else 0
            route += [(o * inner + i, (o + distance) * inner + (i ^ crossed)) for i in range(inner)]
    return lax.ppermute(block, ("outer", "inner"), route)


def to_partner(block, axis):
    return lax.ppermute(block, axis, [(i, i ^ 1) for i in range(lax.axis_size(axis))])


def exchange(parts, axis):
    count = lax.axis_size(axis)
    groups = [list(range(first, count, 2)) for first in range(2)]
    return lax.all_to_all(parts, axis, 0, 0, axis_index_groups=groups, tiled=True)


def dot_nn(a, b):
    return lax.dot_general(a, b, (((1,), (0,)), ((), ())), preferred_element_type=jnp.float32)


def dot_nt(a, b):
    return lax.dot_general(a, b, (((1,), (1,)), ((), ())), preferred_element_type=jnp.float32)


def dot_tn(a, b):
    return lax.dot_general(a, b, (((0,), (0,)), ((), ())), preferred_element_type=jnp.float32)


def stack_heads(source, half, heads, head_dim):
    rows = slice(half * block_rows, (half + 1) * block_rows)
    return jnp.concatenate(
        [source[rows, h * head_dim : (h + 1) * head_dim] for h in range(heads)], axis=0
    )


def store_heads(target_ref, half, block):
    rows = slice(half * block_rows, (half + 1) * block_rows)
    head_dim = block.shape[1]
    for h in range(block.shape[0] // block_rows):
        target_ref[rows, h * head_dim : (h + 1) * head_dim] = block[
            h * block_rows : (h + 1) * block_rows
        ].astype(target_ref.dtype)


def pack(position_ref, key_ref, value_ref, packed_ref, place_ref, block_ref, in_sems, out_sems):
    count, rows, head_dim = packed_ref.shape
    span = key_ref.shape[0]
    loads = [
        pltpu.make_async_copy(position_ref, place_ref, in_sems.at[0]),
        pltpu.make_async_copy(key_ref, block_ref.at[pl.ds(0, span)], in_sems.at[1]),
        pltpu.make_async_copy(value_ref, block_ref.at[pl.ds(span, span)], in_sems.at[2]),
    ]
    for load in loads:
        load.start()
    loads[0].wait()
    tag = (lax.rem(place_ref[0], 2 * count * span) // block_rows).astype(jnp.float32)
    tag = jnp.full((rows - 2 * span, head_dim), tag, jnp.float32)
    block_ref[2 * span :, :] = tag.astype(packed_ref.dtype)
    loads[1].wait()
    loads[2].wait()
    stores = [
        pltpu.make_async_copy(block_ref, packed_ref.at[g], out_sems.at[g]) for g in range(count)
    ]
    for store in stores:
        store.start()
    for store in stores:
        store.wait()


def stack_pair(
    segment, position_ref, position_partner_ref, q_ref, q_partner_ref, do_ref, do_partner_ref,
    block_ref, qs_ref, dot_ref,
):
    _, width, head_dim = qs_ref.shape
    heads = width // block_rows
    block_ref[0] = lax.rem(position_ref[0], segment) // block_rows
    block_ref[1] = lax.rem(position_partner_ref[0], segment) // block_rows
    for j, (query, grad) in enumerate(((q_ref, do_ref), (q_partner_ref, do_partner_ref))):
        for half in range(2):
            qs_ref[2 * j + half] = stack_heads(query, half, heads, head_dim)
            stacked = stack_heads(grad, half, heads, head_dim).astype(jnp.float32)
            dot_ref[2 * j + half] = stacked.T.astype(jnp.bfloat16)


def merge_attended(out_ref, got_ref, factor_ref, att_ref):
    for half in range(2):
        out = factor_ref[0, half] * out_ref[half]
        out = out + factor_ref[1, half] * got_ref[half].astype(jnp.float32)
        store_heads(att_ref, half, out.T)


def own_tile(step, allowed_ref):
    low = 0 if step < 5 else 2
    local = step % 5
    per_tile = tile_keys // block_rows
    low_tiles = (allowed_ref[low] + per_tile - 1) // per_tile
    high = jnp.where(local >= low_tiles, 1, 0)
    tile = local - high * low_tiles
    return low + high, tile


def own_forward(
    block_ref, qs_ref, kv_ref,
    ks_ref, vs_ref, slots_ref, allowed_ref, p_ref, m_ref, l_ref, o_ref, s_ref,
):
    group, _, head_dim = kv_ref.shape
    span = 2 * block_rows
    steps, _, width = p_ref.shape
    blocks = 2 * group
    tiles = blocks * block_rows // tile_keys
    exponent_scale = log2_e * float(head_dim) ** (-0.5)
    tags = [jnp.max(kv_ref[g, 2 * span :, :].astype(jnp.float32)).astype(jnp.int32) for g in range(group)]

    def count(test):
        return sum(jnp.where(test(tag), 1, 0) for tag in tags)

    for j in range(2):
        mine = block_ref[j]
        allowed_ref[2 * j] = count(lambda tag: tag <= mine)
        allowed_ref[2 * j + 1] = blocks - count(lambda tag: tag < mine)
    for g in range(group):
        slot = count(lambda tag: tag < tags[g])
        slots_ref[g] = slot
        for half, place in ((0, slot), (1, blocks - 1 - slot)):
            target = pl.ds(pl.multiple_of(place * block_rows, block_rows), block_rows)
            rows = slice(half * block_rows, (half + 1) * block_rows)
            ks_ref[target, :] = kv_ref[g, rows, :]
            rows = slice(span + half * block_rows, span + (half + 1) * block_rows)
            vs_ref[target, :] = kv_ref[g, rows, :]
    m_ref[...] = jnp.full(m_ref.shape, masked_score, jnp.float32)
    l_ref[...] = jnp.zeros(l_ref.shape, jnp.float32)
    o_ref[...] = jnp.zeros(o_ref.shape, jnp.float32)
    key_row = lax.broadcasted_iota(jnp.int32, (tile_keys, width), 0)
    query_row = lax.rem(lax.broadcasted_iota(jnp.int32, (1, width), 1), block_rows)
    for step in range(steps):
        at, tile = own_tile(step, allowed_ref)
        start = pl.multiple_of(jnp.minimum(tile, tiles - 1) * tile_keys, tile_keys)
        scores = dot_nt(ks_ref[pl.ds(start, tile_keys), :], qs_ref[at])
        last = query_row if step < 5 else block_rows - 1
        limit = (allowed_ref[at] - 1) * block_rows + last - tile * tile_keys
        scores = jnp.where(key_row <= limit, scores, masked_score)
        s_ref[step] = scores
        m_ref[at] = jnp.maximum(m_ref[at], jnp.max(scores, axis=0, keepdims=True))
    for step in range(steps):
        at, tile = own_tile(step, allowed_ref)
        start = pl.multiple_of(jnp.minimum(tile, tiles - 1) * tile_keys, tile_keys)
        raised = jnp.exp2((s_ref[step] - m_ref[at]) * exponent_scale)
        l_ref[at] += jnp.sum(raised, axis=0, keepdims=True)
        raised = raised.astype(jnp.bfloat16)
        p_ref[step] = raised
        o_ref[at] += dot_tn(vs_ref[pl.ds(start, tile_keys), :], raised)


def key_tile(ref, tile, part):
    span = 2 * block_rows
    per_tile = tile_keys // span
    return jnp.concatenate(
        [ref[tile * per_tile + j, part * span : (part + 1) * span, :] for j in range(per_tile)],
        axis=0,
    )


def prev_forward(
    first, has_ref, qs_ref, dot_ref, kv_ref, m_own_ref, l_own_ref, o_own_ref,
    p_ref, m_prev_ref, stats_ref, out_ref, s_ref,
):
    _, width, head_dim = qs_ref.shape
    sets, tiles = p_ref.shape[:2]
    exponent_scale = log2_e * float(head_dim) ** (-0.5)
    has_prev = has_ref[0] > 0
    for at in range(sets):
        peak = jnp.full((1, width), masked_score, jnp.float32)
        for tile in range(tiles):
            scores = dot_nt(key_tile(kv_ref, tile, 0), qs_ref[first + at])
            s_ref[at, tile] = scores
            peak = jnp.maximum(peak, jnp.max(scores, axis=0, keepdims=True))
        m_prev_ref[at] = peak
    for at in range(sets):
        peak = m_prev_ref[at]
        total = jnp.zeros((1, width), jnp.float32)
        out = jnp.zeros((head_dim, width), jnp.float32)
        for tile in range(tiles):
            raised = jnp.exp2((s_ref[at, tile] - peak) * exponent_scale)
            total += jnp.sum(raised, axis=0, keepdims=True)
            raised = raised.astype(jnp.bfloat16)
            p_ref[at, tile] = raised
            out += dot_tn(key_tile(kv_ref, tile, 1), raised)
        peak = jnp.where(has_prev, peak, masked_score)
        m_prev_ref[at] = peak
        top = jnp.maximum(peak, m_own_ref[first + at])
        own_factor = jnp.exp2((m_own_ref[first + at] - top) * exponent_scale)
        prev_factor = jnp.where(has_prev, jnp.exp2((peak - top) * exponent_scale), 0.0)
        total = own_factor * l_own_ref[first + at] + prev_factor * total
        out = own_factor * o_own_ref[first + at] + prev_factor * out
        grad = dot_ref[first + at].astype(jnp.float32)
        stats_ref[0, at] = top
        stats_ref[1, at] = total
        stats_ref[2, at] = jnp.sum(grad * out, axis=0, keepdims=True)
        if first == 0:
            out_ref[at] = out
        else:
            share = jnp.where(total > 0, 1.0 / total, 0.0)
            out_ref[at] = (out * share).astype(jnp.bfloat16)


def prev_backward(first, has_ref, qs_ref, dot_ref, kv_ref, p_ref, m_own_ref, m_prev_ref, stats_ref, other_ref, *rest):
    if first == 0:
        terms_ref, dos_ref, shift_ref, ds_ref, factor_ref, scaled_ref, lower_ref = rest
    else:
        before_ref, terms_ref, dos_ref, shift_ref, ds_ref, scaled_ref, lower_ref = rest
    _, width, head_dim = qs_ref.shape
    sets, tiles = p_ref.shape[:2]
    span = 2 * block_rows
    per_tile = tile_keys // span
    scale = float(head_dim) ** (-0.5)
    exponent_scale = log2_e * scale
    has_prev = has_ref[0] > 0
    for at in range(sets):
        top = jnp.maximum(stats_ref[0, at], other_ref[0, at])
        here = jnp.exp2((stats_ref[0, at] - top) * exponent_scale)
        away = jnp.exp2((other_ref[0, at] - top) * exponent_scale)
        inverse = 1.0 / (here * stats_ref[1, at] + away * other_ref[1, at])
        delta = (here * stats_ref[2, at] + away * other_ref[2, at]) * inverse
        if first == 0:
            factor_ref[0, at] = here * inverse
            factor_ref[1, at] = away * other_ref[1, at] * inverse
        own_factor = jnp.exp2((m_own_ref[first + at] - top) * exponent_scale) * inverse
        prev_factor = jnp.exp2((m_prev_ref[at] - top) * exponent_scale) * inverse
        prev_factor = jnp.where(has_prev, prev_factor, 0.0)
        grad = dot_ref[first + at].astype(jnp.float32)
        dos_ref[at] = (grad * own_factor).astype(jnp.bfloat16)
        shift_ref[at] = delta * own_factor
        scaled_ref[at] = (grad * prev_factor).astype(jnp.bfloat16)
        lower_ref[at] = delta * prev_factor
    for tile in range(tiles):
        values = key_tile(kv_ref, tile, 1)
        key_grad = jnp.zeros((tile_keys, head_dim), jnp.float32)
        value_grad = jnp.zeros((tile_keys, head_dim), jnp.float32)
        for at in range(sets):
            weights = p_ref[at, tile]
            value_grad += dot_nt(weights, scaled_ref[at])
            change = dot_nn(values, scaled_ref[at]) - lower_ref[at]
            change = (weights.astype(jnp.float32) * change).astype(jnp.bfloat16)
            key_grad += dot_nn(change, qs_ref[first + at])
            ds_ref[at, tile] = change
        key_grad = key_grad * scale
        if first == 0:
            rows = slice(tile * tile_keys, (tile + 1) * tile_keys)
            terms_ref[rows, :head_dim] = key_grad
            terms_ref[rows, head_dim:] = value_grad
        else:
            rows = slice(tile * tile_keys, (tile + 1) * tile_keys)
            key_grad = (key_grad + before_ref[rows, :head_dim]).astype(jnp.bfloat16)
            value_grad = (value_grad + before_ref[rows, head_dim:]).astype(jnp.bfloat16)
            for j in range(per_tile):
                rows = slice(j * span, (j + 1) * span)
                terms_ref[tile * per_tile + j, :, :head_dim] = key_grad[rows]
                terms_ref[tile * per_tile + j, :, head_dim:] = value_grad[rows]


def own_backward(
    allowed_ref, slots_ref, qs_ref, ks_ref, vs_ref, p_ref,
    dos_mine_ref, shift_mine_ref, ds_mine_ref, dos_theirs_ref, shift_theirs_ref, ds_theirs_ref, kv_ref,
    dq_ref, dq_partner_ref, terms_ref, acc_ref, dqa_ref,
):
    steps, _, width = p_ref.shape
    group, span, _ = terms_ref.shape
    head_dim = ks_ref.shape[1]
    blocks = 2 * group
    tiles = blocks * block_rows // tile_keys
    scale = float(head_dim) ** (-0.5)

    acc_ref[...] = jnp.zeros(acc_ref.shape, jnp.float32)
    for at in range(4):
        changes = (ds_mine_ref, ds_theirs_ref)[at // 2]
        dqa_ref[at] = sum(
            dot_tn(key_tile(kv_ref, tile, 0), changes[at % 2, tile]) for tile in range(tiles)
        )
    for step in range(steps):
        at, tile = own_tile(step, allowed_ref)
        start = pl.multiple_of(jnp.minimum(tile, tiles - 1) * tile_keys, tile_keys)
        window = pl.ds(start, tile_keys)
        weights = p_ref[step]
        dos_ref, shift_ref, first = (
            (dos_mine_ref, shift_mine_ref, 0) if step < 5 else (dos_theirs_ref, shift_theirs_ref, 2)
        )
        grad = dos_ref[at - first]
        acc_ref[window, head_dim:] += dot_nt(weights, grad)
        change = dot_nn(vs_ref[window, :], grad) - shift_ref[at - first]
        change = (weights.astype(jnp.float32) * change).astype(jnp.bfloat16)
        acc_ref[window, :head_dim] += dot_nn(change, qs_ref[at]) * scale
        dqa_ref[at] += dot_tn(ks_ref[window, :], change)
    for g in range(group):
        slot = slots_ref[g]
        for half, place in ((0, slot), (1, blocks - 1 - slot)):
            source = pl.ds(pl.multiple_of(place * block_rows, block_rows), block_rows)
            terms_ref[g, half * block_rows : (half + 1) * block_rows, :] = acc_ref[
                source, :
            ].astype(jnp.bfloat16)
    for half in range(2):
        store_heads(dq_ref, half, dqa_ref[half].T * scale)
        store_heads(dq_partner_ref, half, dqa_ref[2 + half].T * scale)


def call(kernel, name, outs, in_smem, scratch, out_smem=(), flops=0, stream=()):
    vmem = pl.BlockSpec(memory_space=pltpu.VMEM)
    smem = pl.BlockSpec(memory_space=pltpu.SMEM)

    def spec(at, operand):
        if at in in_smem:
            return smem
        if at in stream:
            return pl.BlockSpec(operand.shape, lambda step: (0,) * operand.ndim)
        return vmem

    def run(*operands):
        return pl.pallas_call(
            kernel,
            name=name,
            grid=(1,) if stream else (),
            out_shape=[jax.ShapeDtypeStruct(shape, dtype) for shape, dtype in outs],
            in_specs=[spec(i, operand) for i, operand in enumerate(operands)],
            out_specs=[smem if i in out_smem else vmem for i in range(len(outs))],
            scratch_shapes=[pltpu.VMEM(shape, dtype) for shape, dtype in scratch],
            compiler_params=pltpu.CompilerParams(vmem_limit_bytes=16 * 1024 * 1024),
            cost_estimate=pl.CostEstimate(flops=flops, bytes_accessed=4 << 20, transcendentals=0),
        )(*operands)

    return run


def body(queries, key_vectors, value_vectors, grad_output, positions):
    tok_rows, full_width = queries.shape
    head_dim = key_vectors.shape[1]
    heads = full_width // head_dim
    group = lax.axis_size("inner") // 2
    segment = 2 * group * tok_rows
    span_rows = group * tok_rows
    width = heads * block_rows
    steps = 10
    bf16, f32 = jnp.bfloat16, jnp.float32
    query_partner = to_partner(queries, "inner")
    grad_partner = to_partner(grad_output, "inner")
    position_partner = to_partner(positions, "inner")
    anywhere = pl.BlockSpec(memory_space=pl.ANY)
    packed = pl.pallas_call(
        pack,
        name="pack",
        out_shape=jax.ShapeDtypeStruct((group, 2 * tok_rows + tag_rows, head_dim), bf16),
        in_specs=[anywhere] * 3,
        out_specs=anywhere,
        scratch_shapes=[
            pltpu.SMEM(positions.shape, jnp.int32),
            pltpu.VMEM((2 * tok_rows + tag_rows, head_dim), bf16),
            pltpu.SemaphoreType.DMA((3,)),
            pltpu.SemaphoreType.DMA((group,)),
        ],
        compiler_params=pltpu.CompilerParams(vmem_limit_bytes=60 * 1024 * 1024),
    )(positions, key_vectors, value_vectors)
    group_kv = exchange(packed, "inner")
    has_prev = (lax.axis_index("outer") > 0).astype(jnp.int32).reshape(1)

    unit = 2 * tile_keys * width * head_dim
    row_stat = ((4, 1, width), f32)
    by_query = ((4, head_dim, width), f32)
    by_query_16 = ((4, head_dim, width), bf16)
    tokens = ((tok_rows, full_width), bf16)
    terms_shape = ((group, tok_rows, 2 * head_dim), bf16)
    tiles = span_rows // tile_keys
    both_blocks, qs, dot = call(
        functools.partial(stack_pair, segment),
        "stack_pair",
        [((2,), jnp.int32), ((4, width, head_dim), bf16), by_query_16],
        (0, 1),
        [],
        out_smem=(0,),
        flops=4 * 10**9,
        stream=(2, 4),
    )(positions, position_partner, queries, query_partner, grad_output, grad_partner)
    group_kv, qs, dot, both_blocks = lax.optimization_barrier((group_kv, qs, dot, both_blocks))
    prev_kv = to_segment(group_kv, 1)
    ks, vs, slots, allowed, p_own, m_own, l_own, o_own = call(
        own_forward,
        "own_forward",
        [
            ((span_rows, head_dim), bf16),
            ((span_rows, head_dim), bf16),
            ((group,), jnp.int32),
            ((4,), jnp.int32),
            ((steps, tile_keys, width), bf16),
            row_stat,
            row_stat,
            by_query,
        ],
        (0,),
        [((steps, tile_keys, width), f32)],
        out_smem=(2, 3),
        flops=2 * steps * unit,
    )(both_blocks, qs, group_kv)
    half_stat = ((2, 1, width), f32)
    half_query = ((2, head_dim, width), f32)
    changes = ((2, tiles, tile_keys, width), bf16)
    half_query_16 = ((2, head_dim, width), bf16)

    def forward(first, name):
        return call(
            functools.partial(prev_forward, first),
            name,
            [
                ((2, tiles, tile_keys, width), bf16),
                half_stat,
                ((3, 2, 1, width), f32),
                half_query if first == 0 else half_query_16,
            ],
            (0,),
            [((2, tiles, tile_keys, width), f32)],
            flops=2 * 2 * tiles * unit,
        )(has_prev, qs, dot, prev_kv, m_own, l_own, o_own)

    p_theirs, m_theirs, stats_theirs, sent = forward(2, "prev_forward_theirs")
    other_mine = to_partner(stats_theirs, "inner")
    got = to_partner(sent, "inner")
    p_mine, m_mine, stats_mine, out = forward(0, "prev_forward_mine")
    other_theirs = to_partner(stats_mine, "inner")
    first_terms, dos_mine, shift_mine, ds_mine, factor = call(
        functools.partial(prev_backward, 0),
        "prev_backward_mine",
        [((span_rows, 2 * head_dim), f32), half_query_16, half_stat, changes, ((2, 2, 1, width), f32)],
        (0,),
        [half_query_16, half_stat],
        flops=4 * 2 * tiles * unit,
    )(has_prev, qs, dot, prev_kv, p_mine, m_own, m_mine, stats_mine, other_mine)
    prev_terms, dos_theirs, shift_theirs, ds_theirs = call(
        functools.partial(prev_backward, 2),
        "prev_backward_theirs",
        [terms_shape, half_query_16, half_stat, changes],
        (0,),
        [half_query_16, half_stat],
        flops=4 * 2 * tiles * unit,
    )(has_prev, qs, dot, prev_kv, p_theirs, m_own, m_theirs, stats_theirs, other_theirs, first_terms)
    returned = to_segment(prev_terms, -1)
    dq, dq_partner, own_terms = call(
        own_backward,
        "own_backward",
        [((tok_rows, full_width), f32), tokens, terms_shape],
        (0, 1),
        [((span_rows, 2 * head_dim), f32), by_query],
        flops=4 * steps * unit,
    )(allowed, slots, qs, ks, vs, p_own, dos_mine, shift_mine, ds_mine, dos_theirs, shift_theirs, ds_theirs, prev_kv)
    (attended,) = call(merge_attended, "merge_attended", [tokens], (), [])(out, got, factor)
    dq_other = to_partner(dq_partner, "inner")
    terms = (own_terms.astype(f32) + returned.astype(f32)).astype(bf16)
    key_grads = jnp.sum(exchange(terms, "inner").astype(f32), axis=0)
    grad_queries = (dq + dq_other.astype(f32)).astype(bf16)
    grad_keys = key_grads[:, :head_dim].astype(bf16)
    grad_values = key_grads[:, head_dim:].astype(bf16)
    return (attended, grad_queries, grad_keys, grad_values)


def solution(mesh):
    rows = P(("outer", "inner"), None)
    return jax.shard_map(
        body,
        mesh=mesh,
        in_specs=(rows, rows, rows, rows, P(("outer", "inner"))),
        out_specs=(rows, rows, rows, rows),
        check_vma=False,
    )
```

```python
import functools

import jax
import jax.numpy as jnp
from jax import lax
from jax.experimental import pallas as pl
from jax.experimental.pallas import tpu as pltpu
from jax.sharding import PartitionSpec as P

masked_score = -1e30
tile_keys = 256
log2_e = 1.4426950408889634
block_rows = 64
tag_rows = 16


def to_segment(block, distance):
    outer, inner = lax.axis_size("outer"), lax.axis_size("inner")
    route = []
    for o in range(outer):
        if o + distance in range(outer):
            crossed = 1 if max(o, o + distance) == outer // 2 else 0
            route += [(o * inner + i, (o + distance) * inner + (i ^ crossed)) for i in range(inner)]
    return lax.ppermute(block, ("outer", "inner"), route)


def to_partner(block, axis):
    return lax.ppermute(block, axis, [(i, i ^ 1) for i in range(lax.axis_size(axis))])


def exchange(parts, axis):
    count = lax.axis_size(axis)
    groups = [list(range(first, count, 2)) for first in range(2)]
    return lax.all_to_all(parts, axis, 0, 0, axis_index_groups=groups, tiled=True)


def dot_nn(a, b):
    return lax.dot_general(a, b, (((1,), (0,)), ((), ())), preferred_element_type=jnp.float32)


def dot_nt(a, b):
    return lax.dot_general(a, b, (((1,), (1,)), ((), ())), preferred_element_type=jnp.float32)


def dot_tn(a, b):
    return lax.dot_general(a, b, (((0,), (0,)), ((), ())), preferred_element_type=jnp.float32)


def stack_heads(source, half, heads, head_dim):
    rows = slice(half * block_rows, (half + 1) * block_rows)
    return jnp.concatenate(
        [source[rows, h * head_dim : (h + 1) * head_dim] for h in range(heads)], axis=0
    )


def store_heads(target_ref, half, block):
    rows = slice(half * block_rows, (half + 1) * block_rows)
    head_dim = block.shape[1]
    for h in range(block.shape[0] // block_rows):
        target_ref[rows, h * head_dim : (h + 1) * head_dim] = block[
            h * block_rows : (h + 1) * block_rows
        ].astype(target_ref.dtype)


def pack(position_ref, key_ref, value_ref, packed_ref, place_ref, block_ref, in_sems, out_sems):
    count, rows, head_dim = packed_ref.shape
    span = key_ref.shape[0]
    loads = [
        pltpu.make_async_copy(position_ref, place_ref, in_sems.at[0]),
        pltpu.make_async_copy(key_ref, block_ref.at[pl.ds(0, span)], in_sems.at[1]),
        pltpu.make_async_copy(value_ref, block_ref.at[pl.ds(span, span)], in_sems.at[2]),
    ]
    for load in loads:
        load.start()
    loads[0].wait()
    tag = (lax.rem(place_ref[0], 2 * count * span) // block_rows).astype(jnp.float32)
    tag = jnp.full((rows - 2 * span, head_dim), tag, jnp.float32)
    block_ref[2 * span :, :] = tag.astype(packed_ref.dtype)
    loads[1].wait()
    loads[2].wait()
    stores = [
        pltpu.make_async_copy(block_ref, packed_ref.at[g], out_sems.at[g]) for g in range(count)
    ]
    for store in stores:
        store.start()
    for store in stores:
        store.wait()


def stack_pair(
    segment, position_ref, position_partner_ref, q_ref, q_partner_ref, do_ref, do_partner_ref,
    block_ref, qs_ref, dot_ref,
):
    _, width, head_dim = qs_ref.shape
    heads = width // block_rows
    block_ref[0] = lax.rem(position_ref[0], segment) // block_rows
    block_ref[1] = lax.rem(position_partner_ref[0], segment) // block_rows
    for j, (query, grad) in enumerate(((q_ref, do_ref), (q_partner_ref, do_partner_ref))):
        for half in range(2):
            qs_ref[2 * j + half] = stack_heads(query, half, heads, head_dim)
            stacked = stack_heads(grad, half, heads, head_dim).astype(jnp.float32)
            dot_ref[2 * j + half] = stacked.T.astype(jnp.bfloat16)


def sum_parts(parts_ref, key_ref, value_ref):
    head_dim = key_ref.shape[1]
    total = sum(parts_ref[g].astype(jnp.float32) for g in range(parts_ref.shape[0]))
    key_ref[...] = total[:, :head_dim].astype(key_ref.dtype)
    value_ref[...] = total[:, head_dim:].astype(value_ref.dtype)


def merge_attended(out_ref, got_ref, factor_ref, att_ref):
    for half in range(2):
        out = factor_ref[0, half] * out_ref[half]
        out = out + factor_ref[1, half] * got_ref[half].astype(jnp.float32)
        store_heads(att_ref, half, out.T)


def own_tile(step, allowed_ref):
    low = 0 if step < 5 else 2
    local = step % 5
    per_tile = tile_keys // block_rows
    low_tiles = (allowed_ref[low] + per_tile - 1) // per_tile
    high = jnp.where(local >= low_tiles, 1, 0)
    tile = local - high * low_tiles
    return low + high, tile


def own_forward(
    block_ref, qs_ref, kv_ref,
    ks_ref, vs_ref, slots_ref, allowed_ref, p_ref, m_ref, l_ref, o_ref, s_ref,
):
    group, _, head_dim = kv_ref.shape
    span = 2 * block_rows
    steps, _, width = p_ref.shape
    blocks = 2 * group
    tiles = blocks * block_rows // tile_keys
    exponent_scale = log2_e * float(head_dim) ** (-0.5)
    tags = [jnp.max(kv_ref[g, 2 * span :, :].astype(jnp.float32)).astype(jnp.int32) for g in range(group)]

    def count(test):
        return sum(jnp.where(test(tag), 1, 0) for tag in tags)

    for j in range(2):
        mine = block_ref[j]
        allowed_ref[2 * j] = count(lambda tag: tag <= mine)
        allowed_ref[2 * j + 1] = blocks - count(lambda tag: tag < mine)
    for g in range(group):
        slot = count(lambda tag: tag < tags[g])
        slots_ref[g] = slot
        for half, place in ((0, slot), (1, blocks - 1 - slot)):
            target = pl.ds(pl.multiple_of(place * block_rows, block_rows), block_rows)
            rows = slice(half * block_rows, (half + 1) * block_rows)
            ks_ref[target, :] = kv_ref[g, rows, :]
            rows = slice(span + half * block_rows, span + (half + 1) * block_rows)
            vs_ref[target, :] = kv_ref[g, rows, :]
    m_ref[...] = jnp.full(m_ref.shape, masked_score, jnp.float32)
    l_ref[...] = jnp.zeros(l_ref.shape, jnp.float32)
    o_ref[...] = jnp.zeros(o_ref.shape, jnp.float32)
    key_row = lax.broadcasted_iota(jnp.int32, (tile_keys, width), 0)
    query_row = lax.rem(lax.broadcasted_iota(jnp.int32, (1, width), 1), block_rows)
    for step in range(steps):
        at, tile = own_tile(step, allowed_ref)
        start = pl.multiple_of(jnp.minimum(tile, tiles - 1) * tile_keys, tile_keys)
        scores = dot_nt(ks_ref[pl.ds(start, tile_keys), :], qs_ref[at])
        last = query_row if step < 5 else block_rows - 1
        limit = (allowed_ref[at] - 1) * block_rows + last - tile * tile_keys
        scores = jnp.where(key_row <= limit, scores, masked_score)
        s_ref[step] = scores
        m_ref[at] = jnp.maximum(m_ref[at], jnp.max(scores, axis=0, keepdims=True))
    for step in range(steps):
        at, tile = own_tile(step, allowed_ref)
        start = pl.multiple_of(jnp.minimum(tile, tiles - 1) * tile_keys, tile_keys)
        raised = jnp.exp2((s_ref[step] - m_ref[at]) * exponent_scale)
        l_ref[at] += jnp.sum(raised, axis=0, keepdims=True)
        raised = raised.astype(jnp.bfloat16)
        p_ref[step] = raised
        o_ref[at] += dot_tn(vs_ref[pl.ds(start, tile_keys), :], raised)


def key_tile(ref, tile, part):
    span = 2 * block_rows
    per_tile = tile_keys // span
    return jnp.concatenate(
        [ref[tile * per_tile + j, part * span : (part + 1) * span, :] for j in range(per_tile)],
        axis=0,
    )


def prev_forward(
    first, has_ref, qs_ref, dot_ref, kv_ref, m_own_ref, l_own_ref, o_own_ref,
    p_ref, m_prev_ref, stats_ref, out_ref, s_ref,
):
    _, width, head_dim = qs_ref.shape
    sets, tiles = p_ref.shape[:2]
    exponent_scale = log2_e * float(head_dim) ** (-0.5)
    has_prev = has_ref[0] > 0
    for at in range(sets):
        peak = jnp.full((1, width), masked_score, jnp.float32)
        for tile in range(tiles):
            scores = dot_nt(key_tile(kv_ref, tile, 0), qs_ref[first + at])
            s_ref[at, tile] = scores
            peak = jnp.maximum(peak, jnp.max(scores, axis=0, keepdims=True))
        m_prev_ref[at] = peak
    for at in range(sets):
        peak = m_prev_ref[at]
        total = jnp.zeros((1, width), jnp.float32)
        out = jnp.zeros((head_dim, width), jnp.float32)
        for tile in range(tiles):
            raised = jnp.exp2((s_ref[at, tile] - peak) * exponent_scale)
            total += jnp.sum(raised, axis=0, keepdims=True)
            raised = raised.astype(jnp.bfloat16)
            p_ref[at, tile] = raised
            out += dot_tn(key_tile(kv_ref, tile, 1), raised)
        peak = jnp.where(has_prev, peak, masked_score)
        m_prev_ref[at] = peak
        top = jnp.maximum(peak, m_own_ref[first + at])
        own_factor = jnp.exp2((m_own_ref[first + at] - top) * exponent_scale)
        prev_factor = jnp.where(has_prev, jnp.exp2((peak - top) * exponent_scale), 0.0)
        total = own_factor * l_own_ref[first + at] + prev_factor * total
        out = own_factor * o_own_ref[first + at] + prev_factor * out
        grad = dot_ref[first + at].astype(jnp.float32)
        stats_ref[0, at] = top
        stats_ref[1, at] = total
        stats_ref[2, at] = jnp.sum(grad * out, axis=0, keepdims=True)
        if first == 0:
            out_ref[at] = out
        else:
            share = jnp.where(total > 0, 1.0 / total, 0.0)
            out_ref[at] = (out * share).astype(jnp.bfloat16)


def prev_backward(first, has_ref, qs_ref, dot_ref, kv_ref, p_ref, m_own_ref, m_prev_ref, stats_ref, other_ref, *rest):
    if first == 0:
        terms_ref, dos_ref, shift_ref, ds_ref, factor_ref, scaled_ref, lower_ref = rest
    else:
        before_ref, terms_ref, dos_ref, shift_ref, ds_ref, scaled_ref, lower_ref = rest
    _, width, head_dim = qs_ref.shape
    sets, tiles = p_ref.shape[:2]
    span = 2 * block_rows
    per_tile = tile_keys // span
    scale = float(head_dim) ** (-0.5)
    exponent_scale = log2_e * scale
    has_prev = has_ref[0] > 0
    for at in range(sets):
        top = jnp.maximum(stats_ref[0, at], other_ref[0, at])
        here = jnp.exp2((stats_ref[0, at] - top) * exponent_scale)
        away = jnp.exp2((other_ref[0, at] - top) * exponent_scale)
        inverse = 1.0 / (here * stats_ref[1, at] + away * other_ref[1, at])
        delta = (here * stats_ref[2, at] + away * other_ref[2, at]) * inverse
        if first == 0:
            factor_ref[0, at] = here * inverse
            factor_ref[1, at] = away * other_ref[1, at] * inverse
        own_factor = jnp.exp2((m_own_ref[first + at] - top) * exponent_scale) * inverse
        prev_factor = jnp.exp2((m_prev_ref[at] - top) * exponent_scale) * inverse
        prev_factor = jnp.where(has_prev, prev_factor, 0.0)
        grad = dot_ref[first + at].astype(jnp.float32)
        dos_ref[at] = (grad * own_factor).astype(jnp.bfloat16)
        shift_ref[at] = delta * own_factor
        scaled_ref[at] = (grad * prev_factor).astype(jnp.bfloat16)
        lower_ref[at] = delta * prev_factor
    for tile in range(tiles):
        values = key_tile(kv_ref, tile, 1)
        key_grad = jnp.zeros((tile_keys, head_dim), jnp.float32)
        value_grad = jnp.zeros((tile_keys, head_dim), jnp.float32)
        for at in range(sets):
            weights = p_ref[at, tile]
            value_grad += dot_nt(weights, scaled_ref[at])
            change = dot_nn(values, scaled_ref[at]) - lower_ref[at]
            change = (weights.astype(jnp.float32) * change).astype(jnp.bfloat16)
            key_grad += dot_nn(change, qs_ref[first + at])
            ds_ref[at, tile] = change
        key_grad = key_grad * scale
        if first == 0:
            rows = slice(tile * tile_keys, (tile + 1) * tile_keys)
            terms_ref[rows, :head_dim] = key_grad
            terms_ref[rows, head_dim:] = value_grad
        else:
            rows = slice(tile * tile_keys, (tile + 1) * tile_keys)
            key_grad = (key_grad + before_ref[rows, :head_dim]).astype(jnp.bfloat16)
            value_grad = (value_grad + before_ref[rows, head_dim:]).astype(jnp.bfloat16)
            for j in range(per_tile):
                rows = slice(j * span, (j + 1) * span)
                terms_ref[tile * per_tile + j, :, :head_dim] = key_grad[rows]
                terms_ref[tile * per_tile + j, :, head_dim:] = value_grad[rows]


def own_backward(
    allowed_ref, slots_ref, qs_ref, ks_ref, vs_ref, p_ref,
    dos_mine_ref, shift_mine_ref, ds_mine_ref, dos_theirs_ref, shift_theirs_ref, ds_theirs_ref, kv_ref,
    dq_ref, dq_partner_ref, terms_ref, acc_ref, dqa_ref,
):
    steps, _, width = p_ref.shape
    group, span, _ = terms_ref.shape
    head_dim = ks_ref.shape[1]
    blocks = 2 * group
    tiles = blocks * block_rows // tile_keys
    scale = float(head_dim) ** (-0.5)

    acc_ref[...] = jnp.zeros(acc_ref.shape, jnp.float32)
    for at in range(4):
        changes = (ds_mine_ref, ds_theirs_ref)[at // 2]
        dqa_ref[at] = sum(
            dot_tn(key_tile(kv_ref, tile, 0), changes[at % 2, tile]) for tile in range(tiles)
        )
    for step in range(steps):
        at, tile = own_tile(step, allowed_ref)
        start = pl.multiple_of(jnp.minimum(tile, tiles - 1) * tile_keys, tile_keys)
        window = pl.ds(start, tile_keys)
        weights = p_ref[step]
        dos_ref, shift_ref, first = (
            (dos_mine_ref, shift_mine_ref, 0) if step < 5 else (dos_theirs_ref, shift_theirs_ref, 2)
        )
        grad = dos_ref[at - first]
        acc_ref[window, head_dim:] += dot_nt(weights, grad)
        change = dot_nn(vs_ref[window, :], grad) - shift_ref[at - first]
        change = (weights.astype(jnp.float32) * change).astype(jnp.bfloat16)
        acc_ref[window, :head_dim] += dot_nn(change, qs_ref[at]) * scale
        dqa_ref[at] += dot_tn(ks_ref[window, :], change)
    for g in range(group):
        slot = slots_ref[g]
        for half, place in ((0, slot), (1, blocks - 1 - slot)):
            source = pl.ds(pl.multiple_of(place * block_rows, block_rows), block_rows)
            terms_ref[g, half * block_rows : (half + 1) * block_rows, :] = acc_ref[
                source, :
            ].astype(jnp.bfloat16)
    for half in range(2):
        store_heads(dq_ref, half, dqa_ref[half].T * scale)
        store_heads(dq_partner_ref, half, dqa_ref[2 + half].T * scale)


def call(kernel, name, outs, in_smem, scratch, out_smem=(), flops=0, stream=()):
    vmem = pl.BlockSpec(memory_space=pltpu.VMEM)
    smem = pl.BlockSpec(memory_space=pltpu.SMEM)

    def spec(at, operand):
        if at in in_smem:
            return smem
        if at in stream:
            return pl.BlockSpec(operand.shape, lambda step: (0,) * operand.ndim)
        return vmem

    def run(*operands):
        return pl.pallas_call(
            kernel,
            name=name,
            grid=(1,) if stream else (),
            out_shape=[jax.ShapeDtypeStruct(shape, dtype) for shape, dtype in outs],
            in_specs=[spec(i, operand) for i, operand in enumerate(operands)],
            out_specs=[smem if i in out_smem else vmem for i in range(len(outs))],
            scratch_shapes=[pltpu.VMEM(shape, dtype) for shape, dtype in scratch],
            compiler_params=pltpu.CompilerParams(vmem_limit_bytes=16 * 1024 * 1024),
            cost_estimate=pl.CostEstimate(flops=flops, bytes_accessed=4 << 20, transcendentals=0),
        )(*operands)

    return run


def body(queries, key_vectors, value_vectors, grad_output, positions):
    tok_rows, full_width = queries.shape
    head_dim = key_vectors.shape[1]
    heads = full_width // head_dim
    group = lax.axis_size("inner") // 2
    segment = 2 * group * tok_rows
    span_rows = group * tok_rows
    width = heads * block_rows
    steps = 10
    bf16, f32 = jnp.bfloat16, jnp.float32
    query_partner = to_partner(queries, "inner")
    grad_partner = to_partner(grad_output, "inner")
    position_partner = to_partner(positions, "inner")
    anywhere = pl.BlockSpec(memory_space=pl.ANY)
    packed = pl.pallas_call(
        pack,
        name="pack",
        out_shape=jax.ShapeDtypeStruct((group, 2 * tok_rows + tag_rows, head_dim), bf16),
        in_specs=[anywhere] * 3,
        out_specs=anywhere,
        scratch_shapes=[
            pltpu.SMEM(positions.shape, jnp.int32),
            pltpu.VMEM((2 * tok_rows + tag_rows, head_dim), bf16),
            pltpu.SemaphoreType.DMA((3,)),
            pltpu.SemaphoreType.DMA((group,)),
        ],
        compiler_params=pltpu.CompilerParams(vmem_limit_bytes=60 * 1024 * 1024),
    )(positions, key_vectors, value_vectors)
    group_kv = exchange(packed, "inner")
    has_prev = (lax.axis_index("outer") > 0).astype(jnp.int32).reshape(1)

    unit = 2 * tile_keys * width * head_dim
    row_stat = ((4, 1, width), f32)
    by_query = ((4, head_dim, width), f32)
    by_query_16 = ((4, head_dim, width), bf16)
    tokens = ((tok_rows, full_width), bf16)
    terms_shape = ((group, tok_rows, 2 * head_dim), bf16)
    tiles = span_rows // tile_keys
    both_blocks, qs, dot = call(
        functools.partial(stack_pair, segment),
        "stack_pair",
        [((2,), jnp.int32), ((4, width, head_dim), bf16), by_query_16],
        (0, 1),
        [],
        out_smem=(0,),
        flops=4 * 10**9,
        stream=(2, 4),
    )(positions, position_partner, queries, query_partner, grad_output, grad_partner)
    group_kv, qs, dot, both_blocks = lax.optimization_barrier((group_kv, qs, dot, both_blocks))
    prev_kv = to_segment(group_kv, 1)
    ks, vs, slots, allowed, p_own, m_own, l_own, o_own = call(
        own_forward,
        "own_forward",
        [
            ((span_rows, head_dim), bf16),
            ((span_rows, head_dim), bf16),
            ((group,), jnp.int32),
            ((4,), jnp.int32),
            ((steps, tile_keys, width), bf16),
            row_stat,
            row_stat,
            by_query,
        ],
        (0,),
        [((steps, tile_keys, width), f32)],
        out_smem=(2, 3),
        flops=2 * steps * unit,
    )(both_blocks, qs, group_kv)
    half_stat = ((2, 1, width), f32)
    half_query = ((2, head_dim, width), f32)
    changes = ((2, tiles, tile_keys, width), bf16)
    half_query_16 = ((2, head_dim, width), bf16)

    def forward(first, name):
        return call(
            functools.partial(prev_forward, first),
            name,
            [
                ((2, tiles, tile_keys, width), bf16),
                half_stat,
                ((3, 2, 1, width), f32),
                half_query if first == 0 else half_query_16,
            ],
            (0,),
            [((2, tiles, tile_keys, width), f32)],
            flops=2 * 2 * tiles * unit,
        )(has_prev, qs, dot, prev_kv, m_own, l_own, o_own)

    p_theirs, m_theirs, stats_theirs, sent = forward(2, "prev_forward_theirs")
    other_mine = to_partner(stats_theirs, "inner")
    got = to_partner(sent, "inner")
    p_mine, m_mine, stats_mine, out = forward(0, "prev_forward_mine")
    other_theirs = to_partner(stats_mine, "inner")
    first_terms, dos_mine, shift_mine, ds_mine, factor = call(
        functools.partial(prev_backward, 0),
        "prev_backward_mine",
        [((span_rows, 2 * head_dim), f32), half_query_16, half_stat, changes, ((2, 2, 1, width), f32)],
        (0,),
        [half_query_16, half_stat],
        flops=4 * 2 * tiles * unit,
    )(has_prev, qs, dot, prev_kv, p_mine, m_own, m_mine, stats_mine, other_mine)
    prev_terms, dos_theirs, shift_theirs, ds_theirs = call(
        functools.partial(prev_backward, 2),
        "prev_backward_theirs",
        [terms_shape, half_query_16, half_stat, changes],
        (0,),
        [half_query_16, half_stat],
        flops=4 * 2 * tiles * unit,
    )(has_prev, qs, dot, prev_kv, p_theirs, m_own, m_theirs, stats_theirs, other_theirs, first_terms)
    returned = to_segment(prev_terms, -1)
    dq, dq_partner, own_terms = call(
        own_backward,
        "own_backward",
        [((tok_rows, full_width), f32), tokens, terms_shape],
        (0, 1),
        [((span_rows, 2 * head_dim), f32), by_query],
        flops=4 * steps * unit,
    )(allowed, slots, qs, ks, vs, p_own, dos_mine, shift_mine, ds_mine, dos_theirs, shift_theirs, ds_theirs, prev_kv)
    (attended,) = call(merge_attended, "merge_attended", [tokens], (), [])(out, got, factor)
    dq_other = to_partner(dq_partner, "inner")
    terms = (own_terms.astype(f32) + returned.astype(f32)).astype(bf16)
    parts = exchange(terms, "inner")
    grad_keys, grad_values = call(
        sum_parts, "sum_parts", [((tok_rows, head_dim), bf16)] * 2, (), []
    )(parts)
    grad_queries = (dq + dq_other.astype(f32)).astype(bf16)
    return (attended, grad_queries, grad_keys, grad_values)


def solution(mesh):
    rows = P(("outer", "inner"), None)
    return jax.shard_map(
        body,
        mesh=mesh,
        in_specs=(rows, rows, rows, rows, P(("outer", "inner"))),
        out_specs=(rows, rows, rows, rows),
        check_vma=False,
    )
```

```python
import functools

import jax
import jax.numpy as jnp
from jax import lax
from jax.experimental import pallas as pl
from jax.experimental.pallas import tpu as pltpu
from jax.sharding import PartitionSpec as P

masked_score = -1e30
tile_keys = 256
log2_e = 1.4426950408889634
block_rows = 64
tag_rows = 16


def to_segment(block, distance):
    outer, inner = lax.axis_size("outer"), lax.axis_size("inner")
    route = []
    for o in range(outer):
        if o + distance in range(outer):
            crossed = 1 if max(o, o + distance) == outer // 2 else 0
            route += [(o * inner + i, (o + distance) * inner + (i ^ crossed)) for i in range(inner)]
    return lax.ppermute(block, ("outer", "inner"), route)


def to_partner(block, axis):
    return lax.ppermute(block, axis, [(i, i ^ 1) for i in range(lax.axis_size(axis))])


def exchange(parts, axis):
    count = lax.axis_size(axis)
    groups = [list(range(first, count, 2)) for first in range(2)]
    return lax.all_to_all(parts, axis, 0, 0, axis_index_groups=groups, tiled=True)


def dot_nn(a, b):
    return lax.dot_general(a, b, (((1,), (0,)), ((), ())), preferred_element_type=jnp.float32)


def dot_nt(a, b):
    return lax.dot_general(a, b, (((1,), (1,)), ((), ())), preferred_element_type=jnp.float32)


def dot_tn(a, b):
    return lax.dot_general(a, b, (((0,), (0,)), ((), ())), preferred_element_type=jnp.float32)


def stack_heads(source, half, heads, head_dim):
    rows = slice(half * block_rows, (half + 1) * block_rows)
    return jnp.concatenate(
        [source[rows, h * head_dim : (h + 1) * head_dim] for h in range(heads)], axis=0
    )


def store_heads(target_ref, half, block):
    rows = slice(half * block_rows, (half + 1) * block_rows)
    head_dim = block.shape[1]
    for h in range(block.shape[0] // block_rows):
        target_ref[rows, h * head_dim : (h + 1) * head_dim] = block[
            h * block_rows : (h + 1) * block_rows
        ].astype(target_ref.dtype)


def pack(position_ref, key_ref, value_ref, packed_ref, place_ref, block_ref, in_sems, out_sems):
    count, rows, head_dim = packed_ref.shape
    span = key_ref.shape[0]
    loads = [
        pltpu.make_async_copy(position_ref, place_ref, in_sems.at[0]),
        pltpu.make_async_copy(key_ref, block_ref.at[pl.ds(0, span)], in_sems.at[1]),
        pltpu.make_async_copy(value_ref, block_ref.at[pl.ds(span, span)], in_sems.at[2]),
    ]
    for load in loads:
        load.start()
    loads[0].wait()
    tag = (lax.rem(place_ref[0], 2 * count * span) // block_rows).astype(jnp.float32)
    tag = jnp.full((rows - 2 * span, head_dim), tag, jnp.float32)
    block_ref[2 * span :, :] = tag.astype(packed_ref.dtype)
    loads[1].wait()
    loads[2].wait()
    stores = [
        pltpu.make_async_copy(block_ref, packed_ref.at[g], out_sems.at[g]) for g in range(count)
    ]
    for store in stores:
        store.start()
    for store in stores:
        store.wait()


def stack_pair(
    segment, position_ref, position_partner_ref, q_ref, q_partner_ref, do_ref, do_partner_ref,
    block_ref, qs_ref, dot_ref,
):
    _, width, head_dim = qs_ref.shape
    heads = width // block_rows
    block_ref[0] = lax.rem(position_ref[0], segment) // block_rows
    block_ref[1] = lax.rem(position_partner_ref[0], segment) // block_rows
    for j, (query, grad) in enumerate(((q_ref, do_ref), (q_partner_ref, do_partner_ref))):
        for half in range(2):
            qs_ref[2 * j + half] = stack_heads(query, half, heads, head_dim)
            stacked = stack_heads(grad, half, heads, head_dim).astype(jnp.float32)
            dot_ref[2 * j + half] = stacked.T.astype(jnp.bfloat16)


def sum_parts(parts_ref, key_ref, value_ref):
    head_dim = key_ref.shape[1]
    total = sum(parts_ref[g].astype(jnp.float32) for g in range(parts_ref.shape[0]))
    key_ref[...] = total[:, :head_dim].astype(key_ref.dtype)
    value_ref[...] = total[:, head_dim:].astype(value_ref.dtype)


def merge_attended(out_ref, got_ref, factor_ref, att_ref):
    for half in range(2):
        out = factor_ref[0, half] * out_ref[half]
        out = out + factor_ref[1, half] * got_ref[half].astype(jnp.float32)
        store_heads(att_ref, half, out.T)


def own_tile(step, allowed_ref):
    low = 0 if step < 5 else 2
    local = step % 5
    per_tile = tile_keys // block_rows
    low_tiles = (allowed_ref[low] + per_tile - 1) // per_tile
    high = jnp.where(local >= low_tiles, 1, 0)
    tile = local - high * low_tiles
    return low + high, tile


def own_forward(
    block_ref, qs_ref, kv_ref,
    ks_ref, vs_ref, slots_ref, allowed_ref, p_ref, m_ref, l_ref, o_ref, s_ref,
):
    group, _, head_dim = kv_ref.shape
    span = 2 * block_rows
    steps, _, width = p_ref.shape
    blocks = 2 * group
    tiles = blocks * block_rows // tile_keys
    exponent_scale = log2_e * float(head_dim) ** (-0.5)
    tags = [jnp.max(kv_ref[g, 2 * span :, :].astype(jnp.float32)).astype(jnp.int32) for g in range(group)]

    def count(test):
        return sum(jnp.where(test(tag), 1, 0) for tag in tags)

    for j in range(2):
        mine = block_ref[j]
        allowed_ref[2 * j] = count(lambda tag: tag <= mine)
        allowed_ref[2 * j + 1] = blocks - count(lambda tag: tag < mine)
    for g in range(group):
        slot = count(lambda tag: tag < tags[g])
        slots_ref[g] = slot
        for half, place in ((0, slot), (1, blocks - 1 - slot)):
            target = pl.ds(pl.multiple_of(place * block_rows, block_rows), block_rows)
            rows = slice(half * block_rows, (half + 1) * block_rows)
            ks_ref[target, :] = kv_ref[g, rows, :]
            rows = slice(span + half * block_rows, span + (half + 1) * block_rows)
            vs_ref[target, :] = kv_ref[g, rows, :]
    m_ref[...] = jnp.full(m_ref.shape, masked_score, jnp.float32)
    l_ref[...] = jnp.zeros(l_ref.shape, jnp.float32)
    o_ref[...] = jnp.zeros(o_ref.shape, jnp.float32)
    key_row = lax.broadcasted_iota(jnp.int32, (tile_keys, width), 0)
    query_row = lax.rem(lax.broadcasted_iota(jnp.int32, (1, width), 1), block_rows)
    for step in range(steps):
        at, tile = own_tile(step, allowed_ref)
        start = pl.multiple_of(jnp.minimum(tile, tiles - 1) * tile_keys, tile_keys)
        scores = dot_nt(ks_ref[pl.ds(start, tile_keys), :], qs_ref[at])
        last = query_row if step < 5 else block_rows - 1
        limit = (allowed_ref[at] - 1) * block_rows + last - tile * tile_keys
        scores = jnp.where(key_row <= limit, scores, masked_score)
        s_ref[step] = scores
        m_ref[at] = jnp.maximum(m_ref[at], jnp.max(scores, axis=0, keepdims=True))
    for step in range(steps):
        at, tile = own_tile(step, allowed_ref)
        start = pl.multiple_of(jnp.minimum(tile, tiles - 1) * tile_keys, tile_keys)
        raised = jnp.exp2((s_ref[step] - m_ref[at]) * exponent_scale)
        l_ref[at] += jnp.sum(raised, axis=0, keepdims=True)
        raised = raised.astype(jnp.bfloat16)
        p_ref[step] = raised
        o_ref[at] += dot_tn(vs_ref[pl.ds(start, tile_keys), :], raised)


def key_tile(ref, tile, part):
    span = 2 * block_rows
    per_tile = tile_keys // span
    return jnp.concatenate(
        [ref[tile * per_tile + j, part * span : (part + 1) * span, :] for j in range(per_tile)],
        axis=0,
    )


def prev_forward(
    first, has_ref, qs_ref, dot_ref, kv_ref, m_own_ref, l_own_ref, o_own_ref,
    p_ref, m_prev_ref, stats_ref, out_ref, s_ref,
):
    _, width, head_dim = qs_ref.shape
    sets, tiles = p_ref.shape[:2]
    exponent_scale = log2_e * float(head_dim) ** (-0.5)
    has_prev = has_ref[0] > 0
    def score(at, tile):
        scores = dot_nt(key_tile(kv_ref, tile, 0), qs_ref[first + at])
        s_ref[at, tile] = scores
        return jnp.max(scores, axis=0, keepdims=True)

    peaks = [functools.reduce(jnp.maximum, [score(0, tile) for tile in range(tiles)])]
    for at in range(sets):
        peak = peaks[at]
        total = jnp.zeros((1, width), jnp.float32)
        out = jnp.zeros((head_dim, width), jnp.float32)
        later = []
        for tile in range(tiles):
            if at + 1 < sets:
                later.append(score(at + 1, tile))
            raised = jnp.exp2((s_ref[at, tile] - peak) * exponent_scale)
            total += jnp.sum(raised, axis=0, keepdims=True)
            raised = raised.astype(jnp.bfloat16)
            p_ref[at, tile] = raised
            out += dot_tn(key_tile(kv_ref, tile, 1), raised)
        if later:
            peaks.append(functools.reduce(jnp.maximum, later))
        peak = jnp.where(has_prev, peak, masked_score)
        m_prev_ref[at] = peak
        top = jnp.maximum(peak, m_own_ref[first + at])
        own_factor = jnp.exp2((m_own_ref[first + at] - top) * exponent_scale)
        prev_factor = jnp.where(has_prev, jnp.exp2((peak - top) * exponent_scale), 0.0)
        total = own_factor * l_own_ref[first + at] + prev_factor * total
        out = own_factor * o_own_ref[first + at] + prev_factor * out
        grad = dot_ref[first + at].astype(jnp.float32)
        stats_ref[0, at] = top
        stats_ref[1, at] = total
        stats_ref[2, at] = jnp.sum(grad * out, axis=0, keepdims=True)
        if first == 0:
            out_ref[at] = out
        else:
            share = jnp.where(total > 0, 1.0 / total, 0.0)
            out_ref[at] = (out * share).astype(jnp.bfloat16)


def prev_backward(first, has_ref, qs_ref, dot_ref, kv_ref, p_ref, m_own_ref, m_prev_ref, stats_ref, other_ref, *rest):
    if first == 0:
        terms_ref, dos_ref, shift_ref, ds_ref, factor_ref, scaled_ref, lower_ref = rest
    else:
        before_ref, terms_ref, dos_ref, shift_ref, ds_ref, scaled_ref, lower_ref = rest
    _, width, head_dim = qs_ref.shape
    sets, tiles = p_ref.shape[:2]
    span = 2 * block_rows
    per_tile = tile_keys // span
    scale = float(head_dim) ** (-0.5)
    exponent_scale = log2_e * scale
    has_prev = has_ref[0] > 0
    for at in range(sets):
        top = jnp.maximum(stats_ref[0, at], other_ref[0, at])
        here = jnp.exp2((stats_ref[0, at] - top) * exponent_scale)
        away = jnp.exp2((other_ref[0, at] - top) * exponent_scale)
        inverse = 1.0 / (here * stats_ref[1, at] + away * other_ref[1, at])
        delta = (here * stats_ref[2, at] + away * other_ref[2, at]) * inverse
        if first == 0:
            factor_ref[0, at] = here * inverse
            factor_ref[1, at] = away * other_ref[1, at] * inverse
        own_factor = jnp.exp2((m_own_ref[first + at] - top) * exponent_scale) * inverse
        prev_factor = jnp.exp2((m_prev_ref[at] - top) * exponent_scale) * inverse
        prev_factor = jnp.where(has_prev, prev_factor, 0.0)
        grad = dot_ref[first + at].astype(jnp.float32)
        dos_ref[at] = (grad * own_factor).astype(jnp.bfloat16)
        shift_ref[at] = delta * own_factor
        scaled_ref[at] = (grad * prev_factor).astype(jnp.bfloat16)
        lower_ref[at] = delta * prev_factor
    for tile in range(tiles):
        values = key_tile(kv_ref, tile, 1)
        key_grad = jnp.zeros((tile_keys, head_dim), jnp.float32)
        value_grad = jnp.zeros((tile_keys, head_dim), jnp.float32)
        for at in range(sets):
            weights = p_ref[at, tile]
            value_grad += dot_nt(weights, scaled_ref[at])
            change = dot_nn(values, scaled_ref[at]) - lower_ref[at]
            change = (weights.astype(jnp.float32) * change).astype(jnp.bfloat16)
            key_grad += dot_nn(change, qs_ref[first + at])
            ds_ref[at, tile] = change
        key_grad = key_grad * scale
        if first == 0:
            rows = slice(tile * tile_keys, (tile + 1) * tile_keys)
            terms_ref[rows, :head_dim] = key_grad
            terms_ref[rows, head_dim:] = value_grad
        else:
            rows = slice(tile * tile_keys, (tile + 1) * tile_keys)
            key_grad = (key_grad + before_ref[rows, :head_dim]).astype(jnp.bfloat16)
            value_grad = (value_grad + before_ref[rows, head_dim:]).astype(jnp.bfloat16)
            for j in range(per_tile):
                rows = slice(j * span, (j + 1) * span)
                terms_ref[tile * per_tile + j, :, :head_dim] = key_grad[rows]
                terms_ref[tile * per_tile + j, :, head_dim:] = value_grad[rows]


def own_backward(
    allowed_ref, slots_ref, qs_ref, ks_ref, vs_ref, p_ref,
    dos_mine_ref, shift_mine_ref, ds_mine_ref, dos_theirs_ref, shift_theirs_ref, ds_theirs_ref, kv_ref,
    dq_ref, dq_partner_ref, terms_ref, acc_ref, dqa_ref,
):
    steps, _, width = p_ref.shape
    group, span, _ = terms_ref.shape
    head_dim = ks_ref.shape[1]
    blocks = 2 * group
    tiles = blocks * block_rows // tile_keys
    scale = float(head_dim) ** (-0.5)

    acc_ref[...] = jnp.zeros(acc_ref.shape, jnp.float32)
    for at in range(4):
        changes = (ds_mine_ref, ds_theirs_ref)[at // 2]
        dqa_ref[at] = sum(
            dot_tn(key_tile(kv_ref, tile, 0), changes[at % 2, tile]) for tile in range(tiles)
        )
    for step in range(steps):
        at, tile = own_tile(step, allowed_ref)
        start = pl.multiple_of(jnp.minimum(tile, tiles - 1) * tile_keys, tile_keys)
        window = pl.ds(start, tile_keys)
        weights = p_ref[step]
        dos_ref, shift_ref, first = (
            (dos_mine_ref, shift_mine_ref, 0) if step < 5 else (dos_theirs_ref, shift_theirs_ref, 2)
        )
        grad = dos_ref[at - first]
        acc_ref[window, head_dim:] += dot_nt(weights, grad)
        change = dot_nn(vs_ref[window, :], grad) - shift_ref[at - first]
        change = (weights.astype(jnp.float32) * change).astype(jnp.bfloat16)
        acc_ref[window, :head_dim] += dot_nn(change, qs_ref[at]) * scale
        dqa_ref[at] += dot_tn(ks_ref[window, :], change)
    for g in range(group):
        slot = slots_ref[g]
        for half, place in ((0, slot), (1, blocks - 1 - slot)):
            source = pl.ds(pl.multiple_of(place * block_rows, block_rows), block_rows)
            terms_ref[g, half * block_rows : (half + 1) * block_rows, :] = acc_ref[
                source, :
            ].astype(jnp.bfloat16)
    for half in range(2):
        store_heads(dq_ref, half, dqa_ref[half].T * scale)
        store_heads(dq_partner_ref, half, dqa_ref[2 + half].T * scale)


def call(kernel, name, outs, in_smem, scratch, out_smem=(), flops=0, stream=()):
    vmem = pl.BlockSpec(memory_space=pltpu.VMEM)
    smem = pl.BlockSpec(memory_space=pltpu.SMEM)

    def spec(at, operand):
        if at in in_smem:
            return smem
        if at in stream:
            return pl.BlockSpec(operand.shape, lambda step: (0,) * operand.ndim)
        return vmem

    def run(*operands):
        return pl.pallas_call(
            kernel,
            name=name,
            grid=(1,) if stream else (),
            out_shape=[jax.ShapeDtypeStruct(shape, dtype) for shape, dtype in outs],
            in_specs=[spec(i, operand) for i, operand in enumerate(operands)],
            out_specs=[smem if i in out_smem else vmem for i in range(len(outs))],
            scratch_shapes=[pltpu.VMEM(shape, dtype) for shape, dtype in scratch],
            compiler_params=pltpu.CompilerParams(vmem_limit_bytes=16 * 1024 * 1024),
            cost_estimate=pl.CostEstimate(flops=flops, bytes_accessed=4 << 20, transcendentals=0),
        )(*operands)

    return run


def body(queries, key_vectors, value_vectors, grad_output, positions):
    tok_rows, full_width = queries.shape
    head_dim = key_vectors.shape[1]
    heads = full_width // head_dim
    group = lax.axis_size("inner") // 2
    segment = 2 * group * tok_rows
    span_rows = group * tok_rows
    width = heads * block_rows
    steps = 10
    bf16, f32 = jnp.bfloat16, jnp.float32
    query_partner = to_partner(queries, "inner")
    grad_partner = to_partner(grad_output, "inner")
    position_partner = to_partner(positions, "inner")
    anywhere = pl.BlockSpec(memory_space=pl.ANY)
    packed = pl.pallas_call(
        pack,
        name="pack",
        out_shape=jax.ShapeDtypeStruct((group, 2 * tok_rows + tag_rows, head_dim), bf16),
        in_specs=[anywhere] * 3,
        out_specs=anywhere,
        scratch_shapes=[
            pltpu.SMEM(positions.shape, jnp.int32),
            pltpu.VMEM((2 * tok_rows + tag_rows, head_dim), bf16),
            pltpu.SemaphoreType.DMA((3,)),
            pltpu.SemaphoreType.DMA((group,)),
        ],
        compiler_params=pltpu.CompilerParams(vmem_limit_bytes=60 * 1024 * 1024),
    )(positions, key_vectors, value_vectors)
    group_kv = exchange(packed, "inner")
    has_prev = (lax.axis_index("outer") > 0).astype(jnp.int32).reshape(1)

    unit = 2 * tile_keys * width * head_dim
    row_stat = ((4, 1, width), f32)
    by_query = ((4, head_dim, width), f32)
    by_query_16 = ((4, head_dim, width), bf16)
    tokens = ((tok_rows, full_width), bf16)
    terms_shape = ((group, tok_rows, 2 * head_dim), bf16)
    tiles = span_rows // tile_keys
    both_blocks, qs, dot = call(
        functools.partial(stack_pair, segment),
        "stack_pair",
        [((2,), jnp.int32), ((4, width, head_dim), bf16), by_query_16],
        (0, 1),
        [],
        out_smem=(0,),
        flops=4 * 10**9,
        stream=(2, 4),
    )(positions, position_partner, queries, query_partner, grad_output, grad_partner)
    group_kv, qs, dot, both_blocks = lax.optimization_barrier((group_kv, qs, dot, both_blocks))
    prev_kv = to_segment(group_kv, 1)
    ks, vs, slots, allowed, p_own, m_own, l_own, o_own = call(
        own_forward,
        "own_forward",
        [
            ((span_rows, head_dim), bf16),
            ((span_rows, head_dim), bf16),
            ((group,), jnp.int32),
            ((4,), jnp.int32),
            ((steps, tile_keys, width), bf16),
            row_stat,
            row_stat,
            by_query,
        ],
        (0,),
        [((steps, tile_keys, width), f32)],
        out_smem=(2, 3),
        flops=2 * steps * unit,
    )(both_blocks, qs, group_kv)
    half_stat = ((2, 1, width), f32)
    half_query = ((2, head_dim, width), f32)
    changes = ((2, tiles, tile_keys, width), bf16)
    half_query_16 = ((2, head_dim, width), bf16)

    def forward(first, name):
        return call(
            functools.partial(prev_forward, first),
            name,
            [
                ((2, tiles, tile_keys, width), bf16),
                half_stat,
                ((3, 2, 1, width), f32),
                half_query if first == 0 else half_query_16,
            ],
            (0,),
            [((2, tiles, tile_keys, width), f32)],
            flops=2 * 2 * tiles * unit,
        )(has_prev, qs, dot, prev_kv, m_own, l_own, o_own)

    p_theirs, m_theirs, stats_theirs, sent = forward(2, "prev_forward_theirs")
    other_mine = to_partner(stats_theirs, "inner")
    got = to_partner(sent, "inner")
    p_mine, m_mine, stats_mine, out = forward(0, "prev_forward_mine")
    other_theirs = to_partner(stats_mine, "inner")
    first_terms, dos_mine, shift_mine, ds_mine, factor = call(
        functools.partial(prev_backward, 0),
        "prev_backward_mine",
        [((span_rows, 2 * head_dim), f32), half_query_16, half_stat, changes, ((2, 2, 1, width), f32)],
        (0,),
        [half_query_16, half_stat],
        flops=4 * 2 * tiles * unit,
    )(has_prev, qs, dot, prev_kv, p_mine, m_own, m_mine, stats_mine, other_mine)
    prev_terms, dos_theirs, shift_theirs, ds_theirs = call(
        functools.partial(prev_backward, 2),
        "prev_backward_theirs",
        [terms_shape, half_query_16, half_stat, changes],
        (0,),
        [half_query_16, half_stat],
        flops=4 * 2 * tiles * unit,
    )(has_prev, qs, dot, prev_kv, p_theirs, m_own, m_theirs, stats_theirs, other_theirs, first_terms)
    returned = to_segment(prev_terms, -1)
    dq, dq_partner, own_terms = call(
        own_backward,
        "own_backward",
        [((tok_rows, full_width), f32), tokens, terms_shape],
        (0, 1),
        [((span_rows, 2 * head_dim), f32), by_query],
        flops=4 * steps * unit,
    )(allowed, slots, qs, ks, vs, p_own, dos_mine, shift_mine, ds_mine, dos_theirs, shift_theirs, ds_theirs, prev_kv)
    (attended,) = call(merge_attended, "merge_attended", [tokens], (), [])(out, got, factor)
    dq_other = to_partner(dq_partner, "inner")
    terms = (own_terms.astype(f32) + returned.astype(f32)).astype(bf16)
    parts = exchange(terms, "inner")
    grad_keys, grad_values = call(
        sum_parts, "sum_parts", [((tok_rows, head_dim), bf16)] * 2, (), []
    )(parts)
    grad_queries = (dq + dq_other.astype(f32)).astype(bf16)
    return (attended, grad_queries, grad_keys, grad_values)


def solution(mesh):
    rows = P(("outer", "inner"), None)
    return jax.shard_map(
        body,
        mesh=mesh,
        in_specs=(rows, rows, rows, rows, P(("outer", "inner"))),
        out_specs=(rows, rows, rows, rows),
        check_vma=False,
    )
```

```python
import functools

import jax
import jax.numpy as jnp
from jax import lax
from jax.experimental import pallas as pl
from jax.experimental.pallas import tpu as pltpu
from jax.sharding import PartitionSpec as P

masked_score = -1e30
tile_keys = 256
log2_e = 1.4426950408889634
block_rows = 64
tag_rows = 16


def to_segment(block, distance):
    outer, inner = lax.axis_size("outer"), lax.axis_size("inner")
    route = []
    for o in range(outer):
        if o + distance in range(outer):
            crossed = 1 if max(o, o + distance) == outer // 2 else 0
            route += [(o * inner + i, (o + distance) * inner + (i ^ crossed)) for i in range(inner)]
    return lax.ppermute(block, ("outer", "inner"), route)


def to_partner(block, axis):
    return lax.ppermute(block, axis, [(i, i ^ 1) for i in range(lax.axis_size(axis))])


def exchange(parts, axis):
    count = lax.axis_size(axis)
    groups = [list(range(first, count, 2)) for first in range(2)]
    return lax.all_to_all(parts, axis, 0, 0, axis_index_groups=groups, tiled=True)


def dot_nn(a, b):
    return lax.dot_general(a, b, (((1,), (0,)), ((), ())), preferred_element_type=jnp.float32)


def dot_nt(a, b):
    return lax.dot_general(a, b, (((1,), (1,)), ((), ())), preferred_element_type=jnp.float32)


def dot_tn(a, b):
    return lax.dot_general(a, b, (((0,), (0,)), ((), ())), preferred_element_type=jnp.float32)


def stack_heads(source, half, heads, head_dim):
    rows = slice(half * block_rows, (half + 1) * block_rows)
    return jnp.concatenate(
        [source[rows, h * head_dim : (h + 1) * head_dim] for h in range(heads)], axis=0
    )


def store_heads(target_ref, half, block):
    rows = slice(half * block_rows, (half + 1) * block_rows)
    head_dim = block.shape[1]
    for h in range(block.shape[0] // block_rows):
        target_ref[rows, h * head_dim : (h + 1) * head_dim] = block[
            h * block_rows : (h + 1) * block_rows
        ].astype(target_ref.dtype)


def pack(position_ref, key_ref, value_ref, packed_ref, place_ref, block_ref, in_sems, out_sems):
    count, rows, head_dim = packed_ref.shape
    span = key_ref.shape[0]
    loads = [
        pltpu.make_async_copy(position_ref, place_ref, in_sems.at[0]),
        pltpu.make_async_copy(key_ref, block_ref.at[pl.ds(0, span)], in_sems.at[1]),
        pltpu.make_async_copy(value_ref, block_ref.at[pl.ds(span, span)], in_sems.at[2]),
    ]
    for load in loads:
        load.start()
    loads[0].wait()
    tag = (lax.rem(place_ref[0], 2 * count * span) // block_rows).astype(jnp.float32)
    tag = jnp.full((rows - 2 * span, head_dim), tag, jnp.float32)
    block_ref[2 * span :, :] = tag.astype(packed_ref.dtype)
    loads[1].wait()
    loads[2].wait()
    stores = [
        pltpu.make_async_copy(block_ref, packed_ref.at[g], out_sems.at[g]) for g in range(count)
    ]
    for store in stores:
        store.start()
    for store in stores:
        store.wait()


def stack_pair(
    segment, position_ref, position_partner_ref, q_ref, q_partner_ref, do_ref, do_partner_ref,
    block_ref, qs_ref, dot_ref,
):
    _, width, head_dim = qs_ref.shape
    heads = width // block_rows
    block_ref[0] = lax.rem(position_ref[0], segment) // block_rows
    block_ref[1] = lax.rem(position_partner_ref[0], segment) // block_rows
    for j, (query, grad) in enumerate(((q_ref, do_ref), (q_partner_ref, do_partner_ref))):
        for half in range(2):
            qs_ref[2 * j + half] = stack_heads(query, half, heads, head_dim)
            stacked = stack_heads(grad, half, heads, head_dim).astype(jnp.float32)
            dot_ref[2 * j + half] = stacked.T.astype(jnp.bfloat16)


def merge_attended(out_ref, got_ref, factor_ref, att_ref):
    for half in range(2):
        out = factor_ref[0, half] * out_ref[half]
        out = out + factor_ref[1, half] * got_ref[half].astype(jnp.float32)
        store_heads(att_ref, half, out.T)


def own_tile(step, allowed_ref):
    low = 0 if step < 5 else 2
    local = step % 5
    per_tile = tile_keys // block_rows
    low_tiles = (allowed_ref[low] + per_tile - 1) // per_tile
    high = jnp.where(local >= low_tiles, 1, 0)
    tile = local - high * low_tiles
    return low + high, tile


def own_forward(
    block_ref, qs_ref, kv_ref,
    ks_ref, vs_ref, slots_ref, allowed_ref, p_ref, m_ref, l_ref, o_ref, s_ref,
):
    group, _, head_dim = kv_ref.shape
    span = 2 * block_rows
    steps, _, width = p_ref.shape
    blocks = 2 * group
    tiles = blocks * block_rows // tile_keys
    exponent_scale = log2_e * float(head_dim) ** (-0.5)
    tags = [jnp.max(kv_ref[g, 2 * span :, :].astype(jnp.float32)).astype(jnp.int32) for g in range(group)]

    def count(test):
        return sum(jnp.where(test(tag), 1, 0) for tag in tags)

    for j in range(2):
        mine = block_ref[j]
        allowed_ref[2 * j] = count(lambda tag: tag <= mine)
        allowed_ref[2 * j + 1] = blocks - count(lambda tag: tag < mine)
    for g in range(group):
        slot = count(lambda tag: tag < tags[g])
        slots_ref[g] = slot
        for half, place in ((0, slot), (1, blocks - 1 - slot)):
            target = pl.ds(pl.multiple_of(place * block_rows, block_rows), block_rows)
            rows = slice(half * block_rows, (half + 1) * block_rows)
            ks_ref[target, :] = kv_ref[g, rows, :]
            rows = slice(span + half * block_rows, span + (half + 1) * block_rows)
            vs_ref[target, :] = kv_ref[g, rows, :]
    m_ref[...] = jnp.full(m_ref.shape, masked_score, jnp.float32)
    l_ref[...] = jnp.zeros(l_ref.shape, jnp.float32)
    o_ref[...] = jnp.zeros(o_ref.shape, jnp.float32)
    key_row = lax.broadcasted_iota(jnp.int32, (tile_keys, width), 0)
    query_row = lax.rem(lax.broadcasted_iota(jnp.int32, (1, width), 1), block_rows)
    for step in range(steps):
        at, tile = own_tile(step, allowed_ref)
        start = pl.multiple_of(jnp.minimum(tile, tiles - 1) * tile_keys, tile_keys)
        scores = dot_nt(ks_ref[pl.ds(start, tile_keys), :], qs_ref[at])
        last = query_row if step < 5 else block_rows - 1
        limit = (allowed_ref[at] - 1) * block_rows + last - tile * tile_keys
        scores = jnp.where(key_row <= limit, scores, masked_score)
        s_ref[step] = scores
        m_ref[at] = jnp.maximum(m_ref[at], jnp.max(scores, axis=0, keepdims=True))
    for step in range(steps):
        at, tile = own_tile(step, allowed_ref)
        start = pl.multiple_of(jnp.minimum(tile, tiles - 1) * tile_keys, tile_keys)
        raised = jnp.exp2((s_ref[step] - m_ref[at]) * exponent_scale)
        l_ref[at] += jnp.sum(raised, axis=0, keepdims=True)
        raised = raised.astype(jnp.bfloat16)
        p_ref[step] = raised
        o_ref[at] += dot_tn(vs_ref[pl.ds(start, tile_keys), :], raised)


def key_tile(ref, tile, part):
    span = 2 * block_rows
    per_tile = tile_keys // span
    return jnp.concatenate(
        [ref[tile * per_tile + j, part * span : (part + 1) * span, :] for j in range(per_tile)],
        axis=0,
    )


def prev_forward(
    first, has_ref, qs_ref, dot_ref, kv_ref, m_own_ref, l_own_ref, o_own_ref,
    p_ref, m_prev_ref, stats_ref, out_ref, s_ref,
):
    _, width, head_dim = qs_ref.shape
    sets, tiles = p_ref.shape[:2]
    exponent_scale = log2_e * float(head_dim) ** (-0.5)
    has_prev = has_ref[0] > 0
    for at in range(sets):
        peak = jnp.full((1, width), masked_score, jnp.float32)
        for tile in range(tiles):
            scores = dot_nt(key_tile(kv_ref, tile, 0), qs_ref[first + at])
            s_ref[at, tile] = scores
            peak = jnp.maximum(peak, jnp.max(scores, axis=0, keepdims=True))
        m_prev_ref[at] = peak
    for at in range(sets):
        peak = m_prev_ref[at]
        total = jnp.zeros((1, width), jnp.float32)
        out = jnp.zeros((head_dim, width), jnp.float32)
        for tile in range(tiles):
            raised = jnp.exp2((s_ref[at, tile] - peak) * exponent_scale)
            total += jnp.sum(raised, axis=0, keepdims=True)
            raised = raised.astype(jnp.bfloat16)
            p_ref[at, tile] = raised
            out += dot_tn(key_tile(kv_ref, tile, 1), raised)
        peak = jnp.where(has_prev, peak, masked_score)
        m_prev_ref[at] = peak
        top = jnp.maximum(peak, m_own_ref[first + at])
        own_factor = jnp.exp2((m_own_ref[first + at] - top) * exponent_scale)
        prev_factor = jnp.where(has_prev, jnp.exp2((peak - top) * exponent_scale), 0.0)
        total = own_factor * l_own_ref[first + at] + prev_factor * total
        out = own_factor * o_own_ref[first + at] + prev_factor * out
        grad = dot_ref[first + at].astype(jnp.float32)
        stats_ref[0, at] = top
        stats_ref[1, at] = total
        stats_ref[2, at] = jnp.sum(grad * out, axis=0, keepdims=True)
        if first == 0:
            out_ref[at] = out
        else:
            share = jnp.where(total > 0, 1.0 / total, 0.0)
            out_ref[at] = (out * share).astype(jnp.bfloat16)


def prev_backward(first, has_ref, qs_ref, dot_ref, kv_ref, p_ref, m_own_ref, m_prev_ref, stats_ref, other_ref, *rest):
    if first == 0:
        terms_ref, dos_ref, shift_ref, ds_ref, factor_ref, scaled_ref, lower_ref = rest
    else:
        before_ref, terms_ref, dos_ref, shift_ref, ds_ref, scaled_ref, lower_ref = rest
    _, width, head_dim = qs_ref.shape
    sets, tiles = p_ref.shape[:2]
    span = 2 * block_rows
    per_tile = tile_keys // span
    scale = float(head_dim) ** (-0.5)
    exponent_scale = log2_e * scale
    has_prev = has_ref[0] > 0
    for at in range(sets):
        top = jnp.maximum(stats_ref[0, at], other_ref[0, at])
        here = jnp.exp2((stats_ref[0, at] - top) * exponent_scale)
        away = jnp.exp2((other_ref[0, at] - top) * exponent_scale)
        inverse = 1.0 / (here * stats_ref[1, at] + away * other_ref[1, at])
        delta = (here * stats_ref[2, at] + away * other_ref[2, at]) * inverse
        if first == 0:
            factor_ref[0, at] = here * inverse
            factor_ref[1, at] = away * other_ref[1, at] * inverse
        own_factor = jnp.exp2((m_own_ref[first + at] - top) * exponent_scale) * inverse
        prev_factor = jnp.exp2((m_prev_ref[at] - top) * exponent_scale) * inverse
        prev_factor = jnp.where(has_prev, prev_factor, 0.0)
        grad = dot_ref[first + at].astype(jnp.float32)
        dos_ref[at] = (grad * own_factor).astype(jnp.bfloat16)
        shift_ref[at] = delta * own_factor
        scaled_ref[at] = (grad * prev_factor).astype(jnp.bfloat16)
        lower_ref[at] = delta * prev_factor
    for tile in range(tiles):
        values = key_tile(kv_ref, tile, 1)
        key_grad = jnp.zeros((tile_keys, head_dim), jnp.float32)
        value_grad = jnp.zeros((tile_keys, head_dim), jnp.float32)
        for at in range(sets):
            weights = p_ref[at, tile]
            value_grad += dot_nt(weights, scaled_ref[at])
            change = dot_nn(values, scaled_ref[at]) - lower_ref[at]
            change = (weights.astype(jnp.float32) * change).astype(jnp.bfloat16)
            key_grad += dot_nn(change, qs_ref[first + at])
            ds_ref[at, tile] = change
        key_grad = key_grad * scale
        if first == 0:
            rows = slice(tile * tile_keys, (tile + 1) * tile_keys)
            terms_ref[rows, :head_dim] = key_grad
            terms_ref[rows, head_dim:] = value_grad
        else:
            rows = slice(tile * tile_keys, (tile + 1) * tile_keys)
            key_grad = (key_grad + before_ref[rows, :head_dim]).astype(jnp.bfloat16)
            value_grad = (value_grad + before_ref[rows, head_dim:]).astype(jnp.bfloat16)
            for j in range(per_tile):
                rows = slice(j * span, (j + 1) * span)
                terms_ref[tile * per_tile + j, :, :head_dim] = key_grad[rows]
                terms_ref[tile * per_tile + j, :, head_dim:] = value_grad[rows]


def own_backward(
    allowed_ref, slots_ref, qs_ref, ks_ref, vs_ref, p_ref,
    dos_mine_ref, shift_mine_ref, ds_mine_ref, dos_theirs_ref, shift_theirs_ref, ds_theirs_ref, kv_ref,
    dq_ref, dq_partner_ref, terms_ref, acc_ref, dqa_ref,
):
    steps, _, width = p_ref.shape
    group, span, _ = terms_ref.shape
    head_dim = ks_ref.shape[1]
    blocks = 2 * group
    tiles = blocks * block_rows // tile_keys
    scale = float(head_dim) ** (-0.5)

    acc_ref[...] = jnp.zeros(acc_ref.shape, jnp.float32)
    for at in range(4):
        changes = (ds_mine_ref, ds_theirs_ref)[at // 2]
        dqa_ref[at] = sum(
            dot_tn(key_tile(kv_ref, tile, 0), changes[at % 2, tile]) for tile in range(tiles)
        )
    for step in range(steps):
        at, tile = own_tile(step, allowed_ref)
        start = pl.multiple_of(jnp.minimum(tile, tiles - 1) * tile_keys, tile_keys)
        window = pl.ds(start, tile_keys)
        weights = p_ref[step]
        dos_ref, shift_ref, first = (
            (dos_mine_ref, shift_mine_ref, 0) if step < 5 else (dos_theirs_ref, shift_theirs_ref, 2)
        )
        grad = dos_ref[at - first]
        acc_ref[window, head_dim:] += dot_nt(weights, grad)
        change = dot_nn(vs_ref[window, :], grad) - shift_ref[at - first]
        change = (weights.astype(jnp.float32) * change).astype(jnp.bfloat16)
        acc_ref[window, :head_dim] += dot_nn(change, qs_ref[at]) * scale
        dqa_ref[at] += dot_tn(ks_ref[window, :], change)
    for g in range(group):
        slot = slots_ref[g]
        for half, place in ((0, slot), (1, blocks - 1 - slot)):
            source = pl.ds(pl.multiple_of(place * block_rows, block_rows), block_rows)
            terms_ref[g, half * block_rows : (half + 1) * block_rows, :] = acc_ref[
                source, :
            ].astype(jnp.bfloat16)
    for half in range(2):
        store_heads(dq_ref, half, dqa_ref[half].T * scale)
        store_heads(dq_partner_ref, half, dqa_ref[2 + half].T * scale)


def call(kernel, name, outs, in_smem, scratch, out_smem=(), flops=0, stream=()):
    vmem = pl.BlockSpec(memory_space=pltpu.VMEM)
    smem = pl.BlockSpec(memory_space=pltpu.SMEM)

    def spec(at, operand):
        if at in in_smem:
            return smem
        if at in stream:
            return pl.BlockSpec(operand.shape, lambda step: (0,) * operand.ndim)
        return vmem

    def run(*operands):
        return pl.pallas_call(
            kernel,
            name=name,
            grid=(1,) if stream else (),
            out_shape=[jax.ShapeDtypeStruct(shape, dtype) for shape, dtype in outs],
            in_specs=[spec(i, operand) for i, operand in enumerate(operands)],
            out_specs=[smem if i in out_smem else vmem for i in range(len(outs))],
            scratch_shapes=[pltpu.VMEM(shape, dtype) for shape, dtype in scratch],
            compiler_params=pltpu.CompilerParams(vmem_limit_bytes=16 * 1024 * 1024),
            cost_estimate=pl.CostEstimate(flops=flops, bytes_accessed=4 << 20, transcendentals=0),
        )(*operands)

    return run


def body(queries, key_vectors, value_vectors, grad_output, positions):
    tok_rows, full_width = queries.shape
    head_dim = key_vectors.shape[1]
    heads = full_width // head_dim
    group = lax.axis_size("inner") // 2
    segment = 2 * group * tok_rows
    span_rows = group * tok_rows
    width = heads * block_rows
    steps = 10
    bf16, f32 = jnp.bfloat16, jnp.float32
    query_partner = to_partner(queries, "inner")
    grad_partner = to_partner(grad_output, "inner")
    position_partner = to_partner(positions, "inner")
    anywhere = pl.BlockSpec(memory_space=pl.ANY)
    packed = pl.pallas_call(
        pack,
        name="pack",
        out_shape=jax.ShapeDtypeStruct((group, 2 * tok_rows + tag_rows, head_dim), bf16),
        in_specs=[anywhere] * 3,
        out_specs=anywhere,
        scratch_shapes=[
            pltpu.SMEM(positions.shape, jnp.int32),
            pltpu.VMEM((2 * tok_rows + tag_rows, head_dim), bf16),
            pltpu.SemaphoreType.DMA((3,)),
            pltpu.SemaphoreType.DMA((group,)),
        ],
        compiler_params=pltpu.CompilerParams(vmem_limit_bytes=60 * 1024 * 1024),
    )(positions, key_vectors, value_vectors)
    group_kv = exchange(packed, "inner")
    has_prev = (lax.axis_index("outer") > 0).astype(jnp.int32).reshape(1)

    unit = 2 * tile_keys * width * head_dim
    row_stat = ((4, 1, width), f32)
    by_query = ((4, head_dim, width), f32)
    by_query_16 = ((4, head_dim, width), bf16)
    tokens = ((tok_rows, full_width), bf16)
    terms_shape = ((group, tok_rows, 2 * head_dim), bf16)
    tiles = span_rows // tile_keys
    both_blocks, qs, dot = call(
        functools.partial(stack_pair, segment),
        "stack_pair",
        [((2,), jnp.int32), ((4, width, head_dim), bf16), by_query_16],
        (0, 1),
        [],
        out_smem=(0,),
        flops=4 * 10**9,
        stream=(2, 4),
    )(positions, position_partner, queries, query_partner, grad_output, grad_partner)
    group_kv, qs, dot, both_blocks = lax.optimization_barrier((group_kv, qs, dot, both_blocks))
    prev_kv = to_segment(group_kv, 1)
    ks, vs, slots, allowed, p_own, m_own, l_own, o_own = call(
        own_forward,
        "own_forward",
        [
            ((span_rows, head_dim), bf16),
            ((span_rows, head_dim), bf16),
            ((group,), jnp.int32),
            ((4,), jnp.int32),
            ((steps, tile_keys, width), bf16),
            row_stat,
            row_stat,
            by_query,
        ],
        (0,),
        [((steps, tile_keys, width), f32)],
        out_smem=(2, 3),
        flops=2 * steps * unit,
    )(both_blocks, qs, group_kv)
    half_stat = ((2, 1, width), f32)
    half_query = ((2, head_dim, width), f32)
    changes = ((2, tiles, tile_keys, width), bf16)
    half_query_16 = ((2, head_dim, width), bf16)

    def forward(first, name):
        return call(
            functools.partial(prev_forward, first),
            name,
            [
                ((2, tiles, tile_keys, width), bf16),
                half_stat,
                ((3, 2, 1, width), f32),
                half_query if first == 0 else half_query_16,
            ],
            (0,),
            [((2, tiles, tile_keys, width), f32)],
            flops=2 * 2 * tiles * unit,
        )(has_prev, qs, dot, prev_kv, m_own, l_own, o_own)

    p_theirs, m_theirs, stats_theirs, sent = forward(2, "prev_forward_theirs")
    other_mine = to_partner(stats_theirs, "inner")
    got = to_partner(sent, "inner")
    p_mine, m_mine, stats_mine, out = forward(0, "prev_forward_mine")
    other_theirs = to_partner(stats_mine, "inner")
    first_terms, dos_mine, shift_mine, ds_mine, factor = call(
        functools.partial(prev_backward, 0),
        "prev_backward_mine",
        [((span_rows, 2 * head_dim), f32), half_query_16, half_stat, changes, ((2, 2, 1, width), f32)],
        (0,),
        [half_query_16, half_stat],
        flops=4 * 2 * tiles * unit,
    )(has_prev, qs, dot, prev_kv, p_mine, m_own, m_mine, stats_mine, other_mine)
    prev_terms, dos_theirs, shift_theirs, ds_theirs = call(
        functools.partial(prev_backward, 2),
        "prev_backward_theirs",
        [terms_shape, half_query_16, half_stat, changes],
        (0,),
        [half_query_16, half_stat],
        flops=4 * 2 * tiles * unit,
    )(has_prev, qs, dot, prev_kv, p_theirs, m_own, m_theirs, stats_theirs, other_theirs, first_terms)
    returned = to_segment(prev_terms, -1)
    dq, dq_partner, own_terms = call(
        own_backward,
        "own_backward",
        [((tok_rows, full_width), f32), tokens, terms_shape],
        (0, 1),
        [((span_rows, 2 * head_dim), f32), by_query],
        flops=4 * steps * unit,
    )(allowed, slots, qs, ks, vs, p_own, dos_mine, shift_mine, ds_mine, dos_theirs, shift_theirs, ds_theirs, prev_kv)
    own_terms, got, dq_partner = lax.optimization_barrier((own_terms, got, dq_partner))
    terms = (own_terms.astype(f32) + returned.astype(f32)).astype(bf16)
    (attended,) = call(merge_attended, "merge_attended", [tokens], (), [])(out, got, factor)
    dq_other = to_partner(dq_partner, "inner")
    key_grads = jnp.sum(exchange(terms, "inner").astype(f32), axis=0)
    grad_queries = (dq + dq_other.astype(f32)).astype(bf16)
    grad_keys = key_grads[:, :head_dim].astype(bf16)
    grad_values = key_grads[:, head_dim:].astype(bf16)
    return (attended, grad_queries, grad_keys, grad_values)


def solution(mesh):
    rows = P(("outer", "inner"), None)
    return jax.shard_map(
        body,
        mesh=mesh,
        in_specs=(rows, rows, rows, rows, P(("outer", "inner"))),
        out_specs=(rows, rows, rows, rows),
        check_vma=False,
    )
```
